32 devices in a mesh: dp: 4 (over z), expert: 8 (over y, x, core).
Axes of the slice: x: 2, y: 2, z: 4, core: 2. Of those that a mesh axis runs over, the one named last changes fastest.
Arguments:
- hidden_in: bfloat16 [32768, 512], P(('dp', 'expert')), may hold values from -6 to 6
- lengths: int32 [32, 32], P(('dp', 'expert')), may hold values from 1 to 64, 1024 in all within a row
- task_ids: int32 [32, 32], P(('dp', 'expert')), may hold values from 0 to 29
- task_experts: int32 [30, 2], replicated, may hold values from 0 to 7, all different within a row
- capacity: int32 [8], replicated, may hold values from 256 to 512, as said below
- task_logits: float32 [30, 8], replicated, may hold values from -4 to 4
- norm_params: bfloat16 [512, 8], P('dp'), may hold values from -0.6 to 1.6
- w_qkv: bfloat16 [512, 2, 1536], P('dp'), may hold values from -0.25 to 0.25
- w_attn: bfloat16 [512, 2, 512], P('dp'), may hold values from -1 to 1
- w_up: bfloat16 [512, 2048], P('dp'), may hold values from -0.25 to 0.25
- w_down: bfloat16 [2048, 512], P('dp'), may hold values from -0.125 to 0.125
- expert_up: bfloat16 [8, 512, 2048], P('expert', 'dp'), may hold values from -0.25 to 0.25
- expert_down: bfloat16 [8, 2048, 512], P('expert', 'dp'), may hold values from -0.5 to 0.5
- cotangent: bfloat16 [32768, 512], P(('dp', 'expert')), may hold values from -6 to 6
Outputs:
- hidden_out: bfloat16 [32768, 512], P(('dp', 'expert'))
- grad_in: float32 [32768, 512], P(('dp', 'expert'))
- grad_task_logits: float32 [30, 8], replicated
- grad_norm_params: float32 [512, 8], P('dp')
- grad_qkv: float32 [512, 2, 1536], P('dp')
- grad_attn: float32 [512, 2, 512], P('dp')
- grad_up: float32 [512, 2048], P('dp')
- grad_down: float32 [2048, 512], P('dp')
- grad_expert_up: float32 [8, 512, 2048], P('expert', 'dp')
- grad_expert_down: float32 [8, 2048, 512], P('expert', 'dp')
The draws below stay inside these ranges and needn't reach their ends.
Inputs may be any that keep to these rules, and one draw needn't show every extreme that they name: The lengths of each pack sum to 1024, and the longest of each pack has exactly 64 tokens. `task_experts`: each task names two different experts; every expert is named by some task. Some expert has a capacity of exactly 512.
All inputs are finite; a program needn't handle non-finite values.
Results may differ from the reference program's by a relative error of at most 0.02.
Values may be sent and summed in bfloat16 or wider, within the bound.
No kernel may reach another device: no remote copies, remote signals or barrier semaphores. Data moves between devices by JAX's collectives and lax.ppermute only.
A program may use at most 256 MiB of HBM per device.

```python
import math
from functools import partial
import jax
import jax.numpy as jnp
import numpy as np
from jax import lax

D = 512
FF = 2048
HEADS = 8
TASKS = 30
EXPERTS = 8
PACK = 1024
SENT = 32
MOST_LEN = 64
PACKS_DEV = 1
TOK_DEV = 1024
PACKS = 32
TOKENS = 32768
CAP = 512
DEVICES = 32


def draw_capacity(key, part):
    key = jax.random.fold_in(key, 11)
    value_key, pick_key = jax.random.split(key)
    values = jax.random.randint(value_key, (EXPERTS,), CAP // 2, CAP + 1)
    chosen = jax.random.randint(pick_key, (), 0, EXPERTS)
    return jnp.where(jnp.arange(EXPERTS) == chosen, CAP, values).astype(jnp.int32)


def draw_norm_params(key, part):
    key = jax.random.fold_in(key, 23)
    noise_vals = jnp.clip(jax.random.normal(key, (D, 8), jnp.float32), -2.95, 2.95)
    is_gain = (jnp.arange(8) % 2 == 0)[None, :]
    return jnp.where(is_gain, 1.0 + 0.2 * noise_vals, 0.2 * noise_vals).astype(jnp.bfloat16)


def plant(values, own_key, smallest, largest):
    index_at = [jax.random.randint(jax.random.fold_in(own_key, axis), (), 0, length) for axis, length in enumerate(values.shape)]
    main_axis = values.shape.index(max(values.shape))
    next_to = index_at[:main_axis] + [(index_at[main_axis] + 1) % values.shape[main_axis]] + index_at[main_axis + 1:]
    return values.at[tuple(index_at)].set(smallest).at[tuple(next_to)].set(largest)


def levels(own_key, shape, pieces, least, high):
    factor_of, own = 1.0, jax.random.fold_in(own_key, 6)
    for dim, blocks in pieces:
        draws = jnp.exp(jax.random.uniform(jax.random.fold_in(own, dim), (blocks,), jnp.float32, least / len(pieces), high / len(pieces)))
        factor_of = factor_of * jnp.repeat(draws, shape[dim] // blocks).reshape([-1 if axis == dim else 1 for axis in range(len(shape))])
    return factor_of


def rank_bounds(count, skew):
    portions = [(1 << 20) // math.isqrt(rank ** skew) + 1 for rank in range(1, count + 1)]
    scale = 1 + sum(portions) // (1 << 30)
    return np.cumsum(np.array([max(1, weight // scale) for weight in portions]))


def ranked_ids(key, extent, amount, slope):
    table = rank_bounds(amount, slope)
    pick = jax.random.randint(jax.random.fold_in(key, 1), extent, 0, int(table[amount - 1]))
    grade = jnp.searchsorted(jnp.asarray(table, jnp.int32), pick, side="right")
    return jax.random.permutation(jax.random.fold_in(key, 2), amount)[grade].astype(jnp.int32)


def picks_of(rng, rows, count, top, lift):
    order = jax.random.permutation(jax.random.fold_in(rng, 1), count)
    pull = order
    for power in range(3):
        pull = pull * pull // count
    pull = pull * lift // count
    chance = jax.random.randint(jax.random.fold_in(rng, 2), (rows, count), 0, 4096) + pull
    sure = jax.random.permutation(jax.random.fold_in(rng, 3), rows)[jnp.arange(count) % rows]
    chance = jnp.where(jnp.arange(rows)[:, None] == sure[None, :], 1 << 14, chance)
    score = chance * count + jnp.arange(count)
    return lax.top_k(score.astype(jnp.int32), top)[1].astype(jnp.int32)


def profile(number_of, total, bound, slope):
    weights = [(1 << 20) // math.isqrt(standing ** slope) + 1 for standing in range(2, number_of + 1)]
    spare, given = total - bound - (number_of - 1), [1] * (number_of - 1)
    while spare > 0:
        free = [i for i in range(number_of - 1) if given[i] < bound]
        whole, remaining = sum([weights[i] for i in free]), spare
        for i in free:
            extra = min(bound - given[i], max(1, remaining * weights[i] // whole), spare)
            given[i] = given[i] + extra
            spare = spare - extra
    return np.array([bound] + given)


def uneven(rng, number_of, total, most, lean):
    if number_of == 2:
        one = jax.random.randint(rng, (), max(1, total - most), min(most, total - 1) + 1)
        return jnp.stack([one, total - one])
    tallies = jnp.asarray(profile(number_of, total, most, lean), jnp.int32)
    twos = (number_of - 1) // 2
    giver, sink = tallies[1:1 + 2 * twos:2], tallies[2:2 + 2 * twos:2]
    margin = jnp.minimum(giver - 1, most - sink)
    moved = jax.random.randint(jax.random.fold_in(rng, 1), (twos,), 0, 1 << 20) % (margin + 1)
    tallies = tallies.at[1:1 + 2 * twos:2].set(giver - moved).at[2:2 + 2 * twos:2].set(sink + moved)
    return tallies[jax.random.permutation(jax.random.fold_in(rng, 2), number_of)]


def noise(own_key, extent, scale, bound, pieces=(), held_as=jnp.bfloat16):
    factor_of = levels(own_key, extent, pieces, -0.22, 0.18) if pieces else 1.0
    values = jax.random.normal(own_key, extent, jnp.float32) * scale * factor_of
    return jnp.minimum(jnp.maximum(values, -bound), bound).astype(held_as)


def setup_inputs(seed: int = 0) -> dict:
    arg_keys = jax.random.split(jax.random.key(seed), 15)
    return {
        "hidden_in": noise(arg_keys[0], (TOKENS, D), 1.0, 6.0, ((0, 32),)),
        "lengths": jax.vmap(lambda own: uneven(own, SENT, PACK, MOST_LEN, 2))(jax.random.split(arg_keys[1], PACKS)).reshape((PACKS, SENT)).astype(jnp.int32),
        "task_ids": plant(ranked_ids(arg_keys[2], (PACKS, SENT), TASKS, 2), jax.random.fold_in(arg_keys[2], 3), 0, TASKS - 1).astype(jnp.int32),
        "task_experts": picks_of(arg_keys[3], TASKS, EXPERTS, 2, 0),
        "capacity": draw_capacity(jax.random.fold_in(arg_keys[14], 71), 0),
        "task_logits": noise(arg_keys[5], (TASKS, EXPERTS), 0.7, 4.0, (), jnp.float32),
        "norm_params": draw_norm_params(jax.random.fold_in(arg_keys[14], 71), 0),
        "w_qkv": noise(arg_keys[7], (D, 2, 3 * D), D ** -0.5, 0.25, ((0, 4),)),
        "w_attn": noise(arg_keys[8], (D, 2, D), (D // 16) ** -0.5, 1.0, ((0, 4),)),
        "w_up": noise(arg_keys[9], (D, FF), D ** -0.5, 0.25, ((0, 4),)),
        "w_down": noise(arg_keys[10], (FF, D), FF ** -0.5, 0.125, ((0, 4),)),
        "expert_up": noise(arg_keys[11], (EXPERTS, D, FF), D ** -0.5, 0.25, ((0, 8), (1, 4))),
        "expert_down": noise(arg_keys[12], (EXPERTS, FF, D), (FF // 16) ** -0.5, 0.5, ((0, 8), (1, 4))),
        "cotangent": noise(arg_keys[13], (TOKENS, D), 1.0, 6.0, ((0, 32),)),
    }


@jax.custom_vjp
def low(v):
    return lax.optimization_barrier(v.astype(jnp.bfloat16)).astype(jnp.float32)

@jax.custom_vjp
def low_back(v):
    return v

def low_keep(v):
    return (low(v), None)

def low_pass(kept, grad):
    return (grad,)

def back_keep(v):
    return (v, None)

def back_low(kept, grad):
    return (low(grad),)
low.defvjp(low_keep, low_pass)
low_back.defvjp(back_keep, back_low)
highest = lax.Precision.HIGHEST
epsilon = 1e-05
blocked = -1e+30

def norm_rows(hidden, gain, shift):
    centre = lax.optimization_barrier(jnp.mean(hidden, axis=-1, keepdims=True))
    centered = hidden - centre
    spread = lax.optimization_barrier(jnp.mean(centered * centered, axis=-1, keepdims=True))
    return centered * lax.rsqrt(spread + epsilon) * gain + shift

def route_block(lengths, task_ids, task_experts, capacity, cap_slots, length):
    pack_count, sentences = lengths.shape
    experts = capacity.shape[0]
    task_count = task_experts.shape[0]
    sent_ends = jnp.cumsum(lengths, axis=1)
    starts = sent_ends - lengths
    position = lax.broadcasted_iota(jnp.int32, (pack_count, length), 1)
    segment = lax.optimization_barrier(jnp.sum((position[:, :, None] >= sent_ends[:, None, :]).astype(jnp.int32), axis=2))
    member = (segment[:, :, None] == lax.broadcasted_iota(jnp.int32, (1, 1, sentences), 2)).astype(jnp.int32)
    offset = position - lax.optimization_barrier(jnp.sum(member * starts[:, None, :], axis=2))
    task_flat = task_ids.reshape(-1)
    task_hot = (task_flat[:, None] == lax.broadcasted_iota(jnp.int32, (1, task_count), 1)).astype(jnp.int32)
    pair_expert = lax.optimization_barrier(jnp.sum(task_hot[:, :, None] * task_experts[None, :, :], axis=1))
    pair_len = jnp.broadcast_to(lengths.reshape(-1, 1), pair_expert.shape).reshape(-1)
    pair_flat = pair_expert.reshape(-1)
    expert_hot = (pair_flat[:, None] == lax.broadcasted_iota(jnp.int32, (1, experts), 1)).astype(jnp.int32)
    running = jnp.cumsum(expert_hot * pair_len[:, None], axis=0)
    filled = lax.optimization_barrier(jnp.sum(running * expert_hot, axis=1))
    limits = lax.optimization_barrier(jnp.sum(expert_hot * capacity[None, :], axis=1))
    pair_base = jnp.where(filled <= limits, pair_flat * cap_slots + filled - pair_len, -1)
    token_base = lax.optimization_barrier(jnp.sum(member[:, :, :, None] * pair_base.reshape(pack_count, 1, sentences, 2), axis=2))
    tokens = pack_count * length
    slot_ids = jnp.where(token_base >= 0, token_base + offset[:, :, None], experts * cap_slots).reshape(tokens, 2)
    pair_index = lax.broadcasted_iota(jnp.int32, (tokens, 2), 0) * 2 + lax.broadcasted_iota(jnp.int32, (tokens, 2), 1)
    pair_source = jnp.full((experts * cap_slots,), 2 * tokens, jnp.int32).at[slot_ids.reshape(-1)].set(pair_index.reshape(-1), mode='drop')
    task_tok = lax.optimization_barrier(jnp.sum(member * task_ids[:, None, :], axis=2)).reshape(tokens)
    expert_tok = lax.optimization_barrier(jnp.sum(member[:, :, :, None] * pair_expert.reshape(pack_count, 1, sentences, 2), axis=2)).reshape(tokens, 2)
    return (slot_ids, pair_source, task_tok, expert_tok, segment)

def attend_pack(inputs):
    pack_qkv, segment = inputs
    score_scale = pack_qkv.shape[-1] ** (-0.5)
    scores = jnp.einsum('qhd,khd->hqk', pack_qkv[:, 0], pack_qkv[:, 1], precision=highest) * score_scale
    scores = low_back(jnp.where((segment[:, None] == segment[None, :])[None], scores, blocked))
    row_max = lax.optimization_barrier(jnp.max(scores, axis=-1, keepdims=True))
    raised = jnp.exp(scores - row_max)
    soft_weights = low(raised / lax.optimization_barrier(jnp.sum(raised, axis=-1, keepdims=True)))
    context = jnp.einsum('hqk,khd->qhd', soft_weights, pack_qkv[:, 2], precision=highest)
    return context.reshape(context.shape[0], -1)

def attend(hidden, gain, shift, w_qkv_layer, w_attn_layer, segment):
    normed = low(norm_rows(hidden, gain, shift))
    qkv = low(low_back(jnp.dot(normed, w_qkv_layer, precision=highest)))
    pack_qkv = qkv.reshape(segment.shape[0], segment.shape[1], 3, HEADS, -1)
    context = lax.map(jax.checkpoint(attend_pack), (pack_qkv, segment))
    context = low(low_back(context.reshape(hidden.shape[0], -1)))
    return low_back(jnp.dot(context, w_attn_layer, precision=highest))

def feed(hidden, gain, shift, up_weight, down_weight):
    normed = low(norm_rows(hidden, gain, shift))
    inner_act = low_back(jnp.dot(normed, up_weight, precision=highest))
    active = low(jax.nn.gelu(inner_act))
    return low_back(jnp.dot(active, down_weight, precision=highest))

def expert_apply(inputs):
    rows_in, up_weight, down_weight = inputs
    inner_act = low_back(jnp.dot(rows_in, up_weight, precision=highest))
    active = low(jax.nn.gelu(inner_act))
    return low(low_back(jnp.dot(active, down_weight, precision=highest)))

def pick_rows(table, indices):
    return table[indices]

def mixture(hidden, gain, shift, up_experts, down_experts, logit_table, routes):
    slot_ids, pair_source, task_tok, expert_tok = routes
    normed = low(norm_rows(hidden, gain, shift))
    blocks = normed.reshape(DEVICES, TOK_DEV, D)
    padded = jnp.concatenate([blocks, jnp.zeros((DEVICES, 1, D), jnp.float32)], axis=1)
    buffer = low_back(jax.vmap(pick_rows)(padded, pair_source // 2))
    buffer = buffer.reshape(DEVICES, EXPERTS, CAP, D).transpose(1, 0, 2, 3).reshape(EXPERTS, DEVICES * CAP, D)
    result = lax.map(jax.checkpoint(expert_apply), (buffer, up_experts, down_experts))
    result = result.reshape(EXPERTS, DEVICES, CAP, D).transpose(1, 0, 2, 3).reshape(DEVICES, EXPERTS * CAP, D)
    padded_out = jnp.concatenate([result, jnp.zeros((DEVICES, 1, D), jnp.float32)], axis=1)
    pair_out = jax.vmap(pick_rows)(padded_out, slot_ids)
    logits = logit_table[task_tok[:, :, None], expert_tok]
    gate_vals = jax.nn.softmax(logits, axis=-1)
    return lax.optimization_barrier(jnp.sum(gate_vals[..., None] * pair_out, axis=2)).reshape(TOKENS, D)

def reference(hidden_in, lengths, task_ids, task_experts, capacity, task_logits, norm_params, w_qkv, w_attn, w_up, w_down, expert_up, expert_down, cotangent):
    router = partial(route_block, task_experts=task_experts, capacity=capacity, cap_slots=CAP, length=PACK)
    slot_ids, pair_source, task_tok, expert_tok, segment = jax.vmap(router)(lengths.reshape(DEVICES, PACKS_DEV, SENT), task_ids.reshape(DEVICES, PACKS_DEV, SENT))
    segment = segment.reshape(PACKS, PACK)
    routes = (slot_ids, pair_source, task_tok, expert_tok)

    def forward(hidden, logit_table, params, qkv_weight, attn_weight, up_weight, down_weight, up_experts, down_experts):
        hidden = hidden + attend(hidden, params[:, 0], params[:, 1], qkv_weight[:, 0], attn_weight[:, 0], segment)
        hidden = hidden + feed(hidden, params[:, 2], params[:, 3], up_weight, down_weight)
        hidden = hidden + attend(hidden, params[:, 4], params[:, 5], qkv_weight[:, 1], attn_weight[:, 1], segment)
        return hidden + mixture(hidden, params[:, 6], params[:, 7], up_experts, down_experts, logit_table, routes)
    floats = [item.astype(jnp.float32) for item in (hidden_in, task_logits, norm_params, w_qkv, w_attn, w_up, w_down, expert_up, expert_down)]
    output, pullback = jax.vjp(forward, *floats)
    gradients = pullback(cotangent.astype(jnp.float32))
    return (output.astype(jnp.bfloat16), gradients[0], gradients[1], gradients[2], gradients[3], gradients[4], gradients[5], gradients[6], gradients[7], gradients[8])
```

```python
import functools

import jax
import jax.numpy as jnp
from jax import lax
from jax.experimental import pallas as pl
from jax.experimental.pallas import tpu as pltpu
from jax.sharding import PartitionSpec as P

D = 512
FF = 2048
HEADS = 8
HEAD = D // HEADS
PACK = 1024
MOST_LEN = 64
ROWS = 256
QB = 128
KB = QB + 2 * MOST_LEN
EPS = 1e-05
BLOCKED = -1e30
BF = jnp.bfloat16
F32 = jnp.float32
GELU_C = 0.7978845608028654
GELU_A = 0.044715


def mm(left, right):
    return lax.dot_general(left, right, (((1,), (0,)), ((), ())), preferred_element_type=F32)


def mm_t(left, right):
    return lax.dot_general(left, right, (((1,), (1,)), ((), ())), preferred_element_type=F32)


def t_mm(left, right):
    return lax.dot_general(left, right, (((0,), (0,)), ((), ())), preferred_element_type=F32)


def unit_rows(hidden):
    centered = hidden - jnp.mean(hidden, axis=-1, keepdims=True)
    spread = jnp.mean(centered * centered, axis=-1, keepdims=True)
    scale = lax.rsqrt(spread + EPS)
    return centered * scale, scale


def unit_back(unit, scale, gain, grad):
    inner = grad * gain
    first = jnp.mean(inner, axis=-1, keepdims=True)
    second = jnp.mean(inner * unit, axis=-1, keepdims=True)
    return scale * (inner - first - unit * second)


def gelu_both(z):
    square = z * z
    t = jnp.tanh(GELU_C * z * (1.0 + GELU_A * square))
    half = 0.5 * (1.0 + t)
    slope = half + 0.5 * z * (1.0 - t * t) * (GELU_C * (1.0 + 3.0 * GELU_A * square))
    return z * half, slope


def call(kernel, out_shape, *args, grid=None, in_specs=None, out_specs=None, scratch=(), mib=48, flops=0, moved=0,
         alias=None, pos=False):
    extra = {}
    if grid is not None:
        extra = dict(grid=grid, in_specs=in_specs, out_specs=out_specs)
    elif pos:
        held = pl.BlockSpec(memory_space=pltpu.VMEM)
        extra = dict(in_specs=[pl.BlockSpec(memory_space=pltpu.SMEM)] + [held] * (len(args) - 1))
    if alias:
        extra["input_output_aliases"] = alias
    return pl.pallas_call(
        kernel,
        out_shape=out_shape,
        scratch_shapes=scratch,
        compiler_params=pltpu.CompilerParams(vmem_limit_bytes=mib << 20),
        cost_estimate=pl.CostEstimate(flops=flops, bytes_accessed=moved, transcendentals=0),
        **extra,
    )(*args)


def sds(shape, dtype):
    return jax.ShapeDtypeStruct(shape, dtype)


WIRE = 512


def piece_rows(split):
    dp, ex = split
    return D // (dp * ex)


def wired(split):
    dp, ex = split
    return piece_rows(split) % 16 == 0 and ex >= 2


def near(split, pos_ref, j, k):
    dp, ex = split
    return lax.rem(pos_ref[1] + k, dp) * ex + jnp.bitwise_xor(pos_ref[0], j)


def send_rows(split, pos_ref, scr_ref, own_ref, core_ref, at, rows):
    dp, ex = split
    for j in range(ex):
        out = core_ref if j % 2 else own_ref
        for k in range(dp):
            start = pl.multiple_of(near(split, pos_ref, j, k) * rows, rows)
            out[j // 2, k, at : at + rows, :] = scr_ref[pl.ds(start, rows), :]


def wire_shapes(split, blocks):
    dp, ex = split
    shape = (ex // 2, dp, blocks * piece_rows(split), WIRE)
    return [sds(shape, BF), sds(shape, BF)]


def route_kernel(slots, sent_ref, pair_ref, tok_ref, slot_ref):
    t = lax.broadcasted_iota(jnp.int32, (PACK, 128), 0).astype(F32)
    start, end = sent_ref[0:1, :], sent_ref[1:2, :]
    member = (t >= start) & (t < end)

    def pick(value):
        return jnp.sum(jnp.where(member, value, 0.0), axis=1, keepdims=True)

    lane = lax.broadcasted_iota(jnp.int32, (PACK, 8), 1)
    out = jnp.where(lane == 0, pick(start), 0.0)
    out = jnp.where(lane == 1, pick(end), out)
    for k in range(2):
        base = sent_ref[2 + k : 3 + k, :]
        slot = pick(jnp.where(base >= 0, base - start + t + 1.0, 0.0)) - 1.0
        out = jnp.where(lane == 2 + k, slot, out)
    tok_ref[...] = out
    chunk = 512
    base, length, first = pair_ref[0:1, :], pair_ref[1:2, :], pair_ref[2:3, :]
    gate, task = pair_ref[3:4, :], pair_ref[4:5, :]
    for i in range(slots // chunk):
        s = lax.broadcasted_iota(jnp.int32, (chunk, 128), 0).astype(F32) + float(i * chunk)
        held = (base >= 0) & (s >= base) & (s < base + length)

        def take(value, held=held):
            return jnp.sum(jnp.where(held, value, 0.0), axis=1, keepdims=True)

        lane = lax.broadcasted_iota(jnp.int32, (chunk, 8), 1)
        out = jnp.where(lane == 0, take(first - base + s + 1.0) - 1.0, 0.0)
        out = jnp.where(lane == 1, take(gate), out)
        out = jnp.where(lane == 2, take(task + 1.0) - 1.0, out)
        slot_ref[i * chunk : (i + 1) * chunk, :] = out


def head_halves(block):
    low = lax.broadcasted_iota(jnp.int32, (1, 128), 1) < HEAD
    zero = jnp.zeros_like(block)
    return jnp.concatenate([jnp.where(low, block, zero), jnp.where(low, zero, block)], axis=0)


def merge_halves(stacked):
    low = lax.broadcasted_iota(jnp.int32, (1, 128), 1) < HEAD
    return jnp.where(low, stacked[:QB], stacked[QB:])


def key_start(i):
    return jnp.clip(i * QB - MOST_LEN, 0, PACK - KB)


def attention_kernel(norm_at, last, x_ref, np_ref, tok_ref, w_ref, *refs):
    if last:
        h_ref, a_ref, qkv_ref, ctx_ref, c_ref = refs
    else:
        h_ref, a_ref, qkv_ref, ctx_ref = refs
    gain, shift = np_ref[norm_at : norm_at + 1, :], np_ref[norm_at + 1 : norm_at + 2, :]
    for r in range(PACK // ROWS):
        rows = slice(r * ROWS, (r + 1) * ROWS)
        unit, _ = unit_rows(x_ref[rows, :].astype(F32))
        a = (unit * gain + shift).astype(BF)
        a_ref[rows, :] = a
        qkv_ref[rows, :] = mm(a, w_ref[:, 0 : 3 * D]).astype(BF)

    def block(i, carry):
        q0 = pl.multiple_of(i * QB, QB)
        k0 = pl.multiple_of(key_start(i), MOST_LEN)
        start, end = tok_ref[pl.ds(q0, QB), 0:1], tok_ref[pl.ds(q0, QB), 1:2]
        key = (lax.broadcasted_iota(jnp.int32, (QB, KB), 1) + k0).astype(F32)
        mask = (key >= start) & (key < end)
        mask = jnp.concatenate([mask, mask], axis=0)
        for pair in range(HEADS // 2):
            at = pair * 128
            q = head_halves(qkv_ref[pl.ds(q0, QB), at : at + 128] * BF(HEAD**-0.5))
            k = qkv_ref[pl.ds(k0, KB), D + at : D + at + 128]
            v = qkv_ref[pl.ds(k0, KB), 2 * D + at : 2 * D + at + 128]
            scores = jnp.where(mask, mm_t(q, k), BLOCKED)
            raised = jnp.exp(scores - jnp.max(scores, axis=1, keepdims=True))
            probs = (raised * (1.0 / jnp.sum(raised, axis=1, keepdims=True))).astype(BF)
            ctx_ref[pl.ds(q0, QB), at : at + 128] = merge_halves(mm(probs, v)).astype(BF)
        return carry

    lax.fori_loop(0, PACK // QB, block, 0)
    for r in range(PACK // ROWS):
        rows = slice(r * ROWS, (r + 1) * ROWS)
        h = x_ref[rows, :].astype(F32) + mm(ctx_ref[rows, :], w_ref[:, 3 * D : 4 * D])
        h_ref[rows, :] = h
        if last:
            unit, _ = unit_rows(h)
            c_ref[rows, :] = (unit * np_ref[6:7, :] + np_ref[7:8, :]).astype(BF)


def attention_forward(hidden, params, tok, weights, norm_at, last):
    outs = [sds((PACK, D), F32), sds((PACK, D), BF), sds((PACK, 3 * D), BF), sds((PACK, D), BF)]
    if last:
        outs.append(sds((PACK, D), BF))
    return call(
        functools.partial(attention_kernel, norm_at, last),
        outs, hidden, params, tok, weights,
        flops=6_000_000_000, moved=12 << 20, mib=40,
    )


def attention_back_kernel(norm_at, split, pos_ref, dx_ref, x_ref, a_ref, qkv_ref, ctx_ref, np_ref, tok_ref, w_ref,
                          out_ref, gn_ref, *refs):
    wire = wired(split)
    if wire:
        own_ref, core_ref, dctx_ref, dqkv_ref, acc_ref, scr_ref = refs
    else:
        gw_ref, dctx_ref, dqkv_ref, acc_ref = refs
    for r in range(PACK // ROWS):
        rows = slice(r * ROWS, (r + 1) * ROWS)
        dctx_ref[rows, :] = mm_t(dx_ref[rows, :].astype(BF), w_ref[:, 3 * D : 4 * D]).astype(BF)
    acc_ref[...] = jnp.zeros_like(acc_ref)

    def block(i, carry):
        q0 = pl.multiple_of(i * QB, QB)
        k0 = pl.multiple_of(key_start(i), MOST_LEN)
        start, end = tok_ref[pl.ds(k0, KB), 0:1], tok_ref[pl.ds(k0, KB), 1:2]
        query = (lax.broadcasted_iota(jnp.int32, (KB, QB), 1) + q0).astype(F32)
        mask = (query >= start) & (query < end)
        mask = jnp.concatenate([mask, mask], axis=1)
        for pair in range(HEADS // 2):
            at = pair * 128
            q = head_halves(qkv_ref[pl.ds(q0, QB), at : at + 128] * BF(HEAD**-0.5))
            k = qkv_ref[pl.ds(k0, KB), D + at : D + at + 128]
            v = qkv_ref[pl.ds(k0, KB), 2 * D + at : 2 * D + at + 128]
            g = head_halves(dctx_ref[pl.ds(q0, QB), at : at + 128])
            scores = jnp.where(mask, mm_t(k, q), BLOCKED)
            raised = jnp.exp(scores - jnp.max(scores, axis=0, keepdims=True))
            probs = raised * (1.0 / jnp.sum(raised, axis=0, keepdims=True))
            dprobs = mm_t(v, g)
            delta = jnp.sum(probs * dprobs, axis=0, keepdims=True)
            dscores = (probs * (dprobs - delta)).astype(BF)
            acc_ref[pl.ds(k0, KB), at : at + 128] += mm(dscores, q)
            acc_ref[pl.ds(k0, KB), D + at : D + at + 128] += mm(probs.astype(BF), g)
            dq = merge_halves(t_mm(dscores, k)) * (HEAD**-0.5)
            dqkv_ref[pl.ds(q0, QB), at : at + 128] = dq.astype(BF)
        return carry

    lax.fori_loop(0, PACK // QB, block, 0)
    dqkv_ref[:, D:] = acc_ref[...].astype(BF)
    for c in range(4):
        cols = slice(c * D, (c + 1) * D)
        if c < 3:
            grad = t_mm(a_ref[...], dqkv_ref[:, cols]).astype(BF)
        else:
            grad = t_mm(ctx_ref[...], dx_ref[...].astype(BF)).astype(BF)
        if wire:
            scr_ref[...] = grad
            rows = piece_rows(split)
            send_rows(split, pos_ref, scr_ref, own_ref, core_ref, c * rows, rows)
        else:
            gw_ref[:, cols] = grad
    gain = np_ref[norm_at : norm_at + 1, :]
    dgain, dshift = jnp.zeros((1, D), F32), jnp.zeros((1, D), F32)
    for r in range(PACK // ROWS):
        rows = slice(r * ROWS, (r + 1) * ROWS)
        dnorm = mm_t(dqkv_ref[rows, :], w_ref[:, 0 : 3 * D])
        unit, scale = unit_rows(x_ref[rows, :].astype(F32))
        dgain += jnp.sum(dnorm * unit, axis=0, keepdims=True)
        dshift += jnp.sum(dnorm, axis=0, keepdims=True)
        out_ref[rows, :] = dx_ref[rows, :] + unit_back(unit, scale, gain, dnorm)
    gn_ref[0:1, :] = dgain
    gn_ref[1:2, :] = dshift


def attention_backward(pos, dx, hidden, saved, params, tok, weights, norm_at, split):
    a, qkv, ctx = saved
    scratch = [pltpu.VMEM((PACK, D), BF), pltpu.VMEM((PACK, 3 * D), BF), pltpu.VMEM((PACK, 2 * D), F32)]
    if wired(split):
        grads = wire_shapes(split, 4)
        scratch.append(pltpu.VMEM((D, D), BF))
    else:
        grads = [sds((D, 4 * D), BF)]
    out, norm, *grads = call(
        functools.partial(attention_back_kernel, norm_at, split),
        [sds((PACK, D), F32), sds((2, D), F32)] + grads,
        pos, dx, hidden, a, qkv, ctx, params, tok, weights,
        scratch=scratch, pos=True,
        flops=12_000_000_000, moved=16 << 20, mib=48,
    )
    return out, norm, grads


def feed_kernel(x_ref, np_ref, up_ref, down_ref, h_ref, n_ref, act_ref, slope_ref):
    gain, shift = np_ref[2:3, :], np_ref[3:4, :]
    for r in range(PACK // ROWS):
        rows = slice(r * ROWS, (r + 1) * ROWS)
        x = x_ref[rows, :]
        unit, _ = unit_rows(x)
        n = (unit * gain + shift).astype(BF)
        n_ref[rows, :] = n
        act, slope = gelu_both(mm(n, up_ref[...]))
        act = act.astype(BF)
        act_ref[rows, :] = act
        slope_ref[rows, :] = slope.astype(BF)
        h_ref[rows, :] = x + mm(act, down_ref[...])


def feed_forward(hidden, params, up, down):
    return call(
        feed_kernel,
        [sds((PACK, D), F32), sds((PACK, D), BF), sds((PACK, FF), BF), sds((PACK, FF), BF)],
        hidden, params, up, down,
        flops=4_300_000_000, moved=17 << 20, mib=48,
    )


def feed_back_kernel(split, pos_ref, dx_ref, x_ref, n_ref, act_ref, slope_ref, np_ref, up_ref, down_ref,
                     out_ref, gn_ref, *refs):
    wire = wired(split)
    if wire:
        own_ref, core_ref, dz_ref, dy_ref, scr_ref, tall_ref = refs
    else:
        gup_ref, gdown_ref, dz_ref, dy_ref = refs
    gain = np_ref[2:3, :]
    dgain, dshift = jnp.zeros((1, D), F32), jnp.zeros((1, D), F32)
    for r in range(PACK // ROWS):
        rows = slice(r * ROWS, (r + 1) * ROWS)
        dx = dx_ref[rows, :]
        dy = dx.astype(BF)
        dy_ref[rows, :] = dy
        dz = (mm_t(dy, down_ref[...]) * slope_ref[rows, :].astype(F32)).astype(BF)
        dz_ref[rows, :] = dz
        dnorm = mm_t(dz, up_ref[...])
        unit, scale = unit_rows(x_ref[rows, :])
        dgain += jnp.sum(dnorm * unit, axis=0, keepdims=True)
        dshift += jnp.sum(dnorm, axis=0, keepdims=True)
        out_ref[rows, :] = dx + unit_back(unit, scale, gain, dnorm)
    gn_ref[0:1, :] = dgain
    gn_ref[1:2, :] = dshift
    if wire:
        rows = piece_rows(split)
        for c in range(FF // D):
            scr_ref[...] = t_mm(n_ref[...], dz_ref[:, c * D : (c + 1) * D]).astype(BF)
            send_rows(split, pos_ref, scr_ref, own_ref, core_ref, c * rows, rows)
        for c in range(FF // D):
            tall_ref[c * D : (c + 1) * D, :] = t_mm(act_ref[:, c * D : (c + 1) * D], dy_ref[...]).astype(BF)
        send_rows(split, pos_ref, tall_ref, own_ref, core_ref, FF // D * rows, FF // D * rows)
    else:
        gdown_ref[...] = t_mm(act_ref[...], dy_ref[...]).astype(BF)
        gup_ref[...] = t_mm(n_ref[...], dz_ref[...]).astype(BF)


def feed_backward(pos, dx, hidden, saved, params, up, down, split):
    n, act, slope = saved
    scratch = [pltpu.VMEM((PACK, FF), BF), pltpu.VMEM((PACK, D), BF)]
    if wired(split):
        grads = wire_shapes(split, 8)
        scratch += [pltpu.VMEM((D, D), BF), pltpu.VMEM((FF, D), BF)]
    else:
        grads = [sds((D, FF), BF), sds((FF, D), BF)]
    out, norm, *grads = call(
        functools.partial(feed_back_kernel, split),
        [sds((PACK, D), F32), sds((2, D), F32)] + grads,
        pos, dx, hidden, n, act, slope, params, up, down,
        scratch=scratch, pos=True,
        flops=8_600_000_000, moved=26 << 20, mib=58,
    )
    return out, norm, grads


def assemble_kernel(split, blocks, tall, *refs):
    dp, ex = split
    rows = piece_rows(split)
    pos_ref, pieces, outs = refs[0], refs[1 : 1 + ex], refs[1 + ex :]
    for j in range(ex):
        for k in range(dp):
            at = lax.rem(pos_ref[1] + dp - k, dp) * ex + jnp.bitwise_xor(pos_ref[0], j)
            start = pl.multiple_of(at * rows, rows)
            for c in range(blocks):
                outs[0][pl.ds(start, rows), c * WIRE : (c + 1) * WIRE] = pieces[j][k, c * rows : (c + 1) * rows, :]
            if tall:
                high = blocks * rows
                start = pl.multiple_of(at * high, high)
                outs[1][pl.ds(start, high), :] = pieces[j][k, high : 2 * high, :]


def assemble(split, pos, pieces, tall):
    outs = [sds((D, 4 * D), BF)] + ([sds((FF, D), BF)] if tall else [])
    return call(
        functools.partial(assemble_kernel, split, 4, tall), outs, pos, *pieces,
        pos=True, flops=1_000_000, moved=4 << 20, mib=24,
    )


def assemble_norm_kernel(split, *refs):
    dp, ex = split
    rows = piece_rows(split)
    pos_ref, pieces, (w_ref, np_ref, scr_ref) = refs[0], refs[1 : 1 + ex], refs[1 + ex :]
    for j in range(ex):
        for k in range(dp):
            at = lax.rem(pos_ref[1] + dp - k, dp) * ex + jnp.bitwise_xor(pos_ref[0], j)
            start = pl.multiple_of(at * rows, rows)
            for c in range(4):
                w_ref[pl.ds(start, rows), c * WIRE : (c + 1) * WIRE] = pieces[j][k, c * rows : (c + 1) * rows, :]
            scr_ref[pl.ds(start, rows), :] = pieces[j][k, 4 * rows : 5 * rows, 0:128].astype(F32)
    np_ref[...] = jnp.transpose(scr_ref[...])[:8]


def add_core_kernel(own_ref, got_ref, *outs):
    for j, out in enumerate(outs):
        out[...] = (own_ref[j].astype(F32) + got_ref[j].astype(F32)).astype(BF)


def add_all_kernel(count, *refs):
    total = refs[0][...].astype(F32)
    for ref in refs[1:count]:
        total = total + ref[...].astype(F32)
    total = total.astype(BF)
    outs = refs[count:]
    for k, out in enumerate(outs):
        out[...] = total[k] if len(outs) > 1 else total


def spread_kernel(split, layers, feed, *refs):
    dp, ex = split
    rows = piece_rows(split)
    pos_ref, refs = refs[0], refs[1:]
    count = len(layers)
    outs = refs[ex * (count + feed) :]
    for j in range(ex):
        at = jnp.bitwise_xor(pos_ref[0], j)
        start = pl.multiple_of(at * rows, rows)
        for n in range(count):
            piece = refs[n * ex + j][...].astype(F32)
            for c in range(3):
                outs[0][n, pl.ds(start, rows), c * D : (c + 1) * D] = piece[c * rows : (c + 1) * rows]
            outs[1][n, pl.ds(start, rows), :] = piece[3 * rows :]
        if feed:
            piece = refs[count * ex + j][...].astype(F32)
            for c in range(4):
                outs[2][pl.ds(start, rows), c * D : (c + 1) * D] = piece[c * rows : (c + 1) * rows]
            high = pl.multiple_of(at * 4 * rows, 4 * rows)
            outs[3][pl.ds(high, 4 * rows), :] = piece[4 * rows :]


def gather_kernel(gated, slot_ref, src_ref, *outs):
    size = outs[0].shape[0]
    tokens = lax.broadcasted_iota(jnp.int32, (size, PACK), 1).astype(F32)
    for n, out in enumerate(outs):
        slot = slot_ref[n * size : (n + 1) * size, :]
        hot = jnp.where(slot[:, 0:1] == tokens, 1.0, 0.0).astype(BF)
        rows = mm(hot, src_ref[...])
        if gated:
            rows = rows * slot[:, 1:2]
        out[...] = rows.astype(BF)


def gather_rows(slot, source, experts, gated):
    size = slot.shape[0] // experts
    return call(
        functools.partial(gather_kernel, gated), [sds((size, D), BF)] * experts, slot, source,
        flops=2 * slot.shape[0] * PACK * D, moved=6 << 20, mib=32,
    )


def slots_hot(tok_ref, size, n):
    at = lax.broadcasted_iota(jnp.int32, (PACK, size), 1).astype(F32) + float(n * size)
    return jnp.where((tok_ref[:, 2:3] == at) | (tok_ref[:, 3:4] == at), 1.0, 0.0).astype(BF)


def combine_back_kernel(experts, tok_ref, h_ref, cot_ref, np_ref, *refs):
    rows_refs, (out_ref, gn_ref, acc_ref) = refs[:experts], refs[experts:]
    for e, ref in enumerate(rows_refs):
        part = mm(slots_hot(tok_ref, ref.shape[0], e), ref[...])
        acc_ref[...] = part if e == 0 else acc_ref[...] + part
    gain = np_ref[6:7, :]
    dgain, dshift = jnp.zeros((1, D), F32), jnp.zeros((1, D), F32)
    for r in range(PACK // ROWS):
        rows = slice(r * ROWS, (r + 1) * ROWS)
        dnorm = acc_ref[rows, :]
        unit, scale = unit_rows(h_ref[rows, :])
        dgain += jnp.sum(dnorm * unit, axis=0, keepdims=True)
        dshift += jnp.sum(dnorm, axis=0, keepdims=True)
        out_ref[rows, :] = cot_ref[rows, :].astype(F32) + unit_back(unit, scale, gain, dnorm)
    gn_ref[0:1, :] = dgain
    gn_ref[1:2, :] = dshift


def whole(shape):
    return pl.BlockSpec(shape, lambda e: (0,) * len(shape))


def combine_back(tok, rows, hidden, cotangent, params):
    experts = len(rows)
    return call(
        functools.partial(combine_back_kernel, experts),
        [sds((PACK, D), F32), sds((2, D), F32)], tok, hidden, cotangent, params, *rows,
        scratch=[pltpu.VMEM((PACK, D), F32)],
        flops=2 * 4096 * PACK * D, moved=12 << 20, mib=40,
    )


def combine_out_kernel(experts, tok_ref, slot_ref, h_ref, *refs):
    rows_refs, dout_refs = refs[:experts], refs[experts : 2 * experts]
    out_ref, table_ref, acc_ref = refs[2 * experts :]
    size = rows_refs[0].shape[0]
    for e in range(experts):
        rows = rows_refs[e][...].astype(F32)
        slot = slot_ref[e * size : (e + 1) * size, :]
        gate, task = slot[:, 1:2], slot[:, 2:3]
        part = mm(slots_hot(tok_ref, size, e), (rows * gate).astype(BF))
        acc_ref[...] = part if e == 0 else acc_ref[...] + part
        held = task >= 0
        dgate = jnp.sum(rows * dout_refs[e][...].astype(F32), axis=1, keepdims=True)
        dgate = jnp.where(held, dgate / jnp.where(held, gate, 1.0), 0.0)
        tasks = lax.broadcasted_iota(jnp.int32, (size, 128), 1).astype(F32)
        table_ref[e : e + 1, :] = jnp.sum(jnp.where(tasks == task, dgate, 0.0), axis=0, keepdims=True)
    out_ref[...] = (h_ref[...] + acc_ref[...]).astype(BF)


def combine_out(tok, slot, rows, dout, hidden):
    experts = len(rows)
    return call(
        functools.partial(combine_out_kernel, experts),
        [sds((PACK, D), BF), sds((experts, 128), F32)], tok, slot, hidden, *rows, *dout,
        scratch=[pltpu.VMEM((PACK, D), F32)],
        flops=2 * 4096 * PACK * D, moved=14 << 20, mib=40,
    )


def expert_kernel(count, steps, *refs):
    bufs, douts = refs[:count], refs[count : 2 * count]
    up_ref, down_ref = refs[2 * count : 2 * count + 2]
    outs, dbufs = refs[-2 * count - 4 : -count - 4], refs[-count - 4 : -4]
    act_ref, du_ref, buf_ref, dout_ref = refs[-4:]
    i = pl.program_id(0)

    def work(n):
        buf, dout = bufs[n][...], douts[n][...]
        buf_ref[...] = buf
        dout_ref[...] = dout
        act, slope = gelu_both(mm(buf, up_ref[...]))
        act = act.astype(BF)
        act_ref[...] = act
        du = (mm_t(dout, down_ref[...]) * slope).astype(BF)
        du_ref[...] = du
        dbufs[n][...] = mm_t(du, up_ref[...]).astype(BF)
        outs[n][...] = mm(act, down_ref[...]).astype(BF)

    if count == 1:
        work(0)
    else:
        for n in range(count):
            pl.when(i // steps == n)(functools.partial(work, n))


def expert_rows(bufs, douts, up, down, total, at, held):
    rows = bufs[0].shape[0]
    count = len(bufs)
    size = min(256, rows)
    steps = rows // size
    blocks = [
        pl.BlockSpec((size, D), lambda i, n=n: (jnp.clip(i - n * steps, 0, steps - 1), 0)) for n in range(count)
    ]
    first = at // size
    keep = [pl.BlockSpec((size, cols), lambda i: (i + first, 0)) for cols in (FF, FF, D, D)]
    alias = {2 * count + 2 + n: 2 * count + n for n in range(4)} if held else None
    outs = call(
        functools.partial(expert_kernel, count, steps),
        [sds((rows, D), BF)] * (2 * count) + [sds((total, cols), BF) for cols in (FF, FF, D, D)],
        *bufs, *douts, up, down, *held,
        grid=(count * steps,),
        in_specs=blocks + blocks + [whole((D, FF)), whole((FF, D))] + [pl.BlockSpec(memory_space=pl.ANY)] * len(held),
        out_specs=blocks + blocks + keep,
        alias=alias,
        flops=8 * rows * count * D * FF, moved=count * rows * 13 << 10, mib=44,
    )
    return outs[:count], outs[count : 2 * count], outs[2 * count :]


def expert_grad_kernel(steps, act_ref, du_ref, buf_ref, dout_ref, gup_ref, gdown_ref, up_acc, down_acc):
    i = pl.program_id(0)

    @pl.when(i == 0)
    def _():
        up_acc[...] = jnp.zeros_like(up_acc)
        down_acc[...] = jnp.zeros_like(down_acc)

    up_acc[...] += t_mm(buf_ref[...], du_ref[...])
    down_acc[...] += t_mm(act_ref[...], dout_ref[...])

    @pl.when(i == steps - 1)
    def _():
        gup_ref[...] = up_acc[...].astype(BF)
        gdown_ref[...] = down_acc[...].astype(BF)


def expert_grads(act, du, buf, dout):
    rows = buf.shape[0]
    size = 1024
    tile = lambda cols: pl.BlockSpec((size, cols), lambda i: (i, 0))
    return call(
        functools.partial(expert_grad_kernel, rows // size),
        [sds((D, FF), BF), sds((FF, D), BF)], act, du, buf, dout,
        grid=(rows // size,),
        in_specs=[tile(FF), tile(FF), tile(D), tile(D)],
        out_specs=[whole((D, FF)), whole((FF, D))],
        scratch=[pltpu.VMEM((D, FF), F32), pltpu.VMEM((FF, D), F32)],
        flops=4 * rows * D * FF, moved=44 << 20, mib=56,
    )


def route(lengths, task_ids, task_experts, capacity, task_logits, cap_slots, rel):
    sentences = lengths.shape[1]
    experts = capacity.shape[0]
    tasks = task_experts.shape[0]
    lens, ids = lengths.reshape(-1), task_ids.reshape(-1)
    ends = jnp.cumsum(lens)
    starts = ends - lens
    table = jnp.take_along_axis(task_logits, task_experts, axis=1)
    gates = jax.nn.softmax(table, axis=-1)
    hot = ids[:, None] == lax.broadcasted_iota(jnp.int32, (1, tasks), 1)
    expert = jnp.sum(jnp.where(hot[:, :, None], task_experts[None], 0), axis=1)
    gate = jnp.sum(jnp.where(hot[:, :, None], gates[None], 0.0), axis=1)
    pair_expert = expert.reshape(-1)
    pair_len = jnp.repeat(lens, 2)
    expert_hot = (pair_expert[:, None] == lax.broadcasted_iota(jnp.int32, (1, experts), 1)).astype(jnp.int32)
    running = jnp.cumsum(expert_hot * pair_len[:, None], axis=0)
    filled = jnp.sum(running * expert_hot, axis=1)
    limits = jnp.sum(expert_hot * capacity[None, :], axis=1)
    base = jnp.where(filled <= limits, jnp.bitwise_xor(pair_expert, rel) * cap_slots + filled - pair_len, -1)
    base_two = base.reshape(sentences, 2)

    def lanes(rows):
        rows = jnp.stack([row.astype(F32) for row in rows])
        return jnp.pad(rows, ((0, 8 - rows.shape[0]), (0, 128 - rows.shape[1])))

    sent = lanes([starts, ends, base_two[:, 0], base_two[:, 1]])
    pair = lanes([base, pair_len, jnp.repeat(starts, 2), gate.reshape(-1), jnp.repeat(ids, 2)])
    slots = experts * cap_slots
    tok, slot = call(
        functools.partial(route_kernel, slots),
        [sds((PACK, 8), F32), sds((slots, 8), F32)], sent, pair,
        flops=1_000_000, moved=3 << 20, mib=24,
    )
    return tok, slot, gates


def flip(rows, j, ex):
    return lax.ppermute(rows, "expert", [(i, i ^ j) for i in range(ex)])


def turn(rows, k, dp):
    return lax.ppermute(rows, "dp", [(i, (i + k) % dp) for i in range(dp)])


def tie(value, *after):
    return lax.optimization_barrier((value,) + after)[0]


def gather_pieces(piece, split):
    dp, ex = split
    here = jnp.stack([piece] + [turn(piece, k, dp) for k in range(1, dp)])
    even = [here] + [flip(here, j, ex) for j in range(2, ex, 2)]
    got = []
    for one in even:
        got += [one, flip(one, 1, ex)]
    return got


def reduce_pieces(own, core, split):
    dp, ex = split
    rows = own.shape[2]
    got = flip(core, 1, ex)
    sums = call(
        add_core_kernel, [sds((dp, rows, WIRE), BF)] * (ex // 2), own, got,
        flops=1_000_000, moved=own.size * 6, mib=32,
    )
    got = [flip(sums[j], 2 * j, ex) for j in range(1, ex // 2)]
    sums = call(
        functools.partial(add_all_kernel, ex // 2), [sds((rows, WIRE), BF)] * dp, sums[0], *got,
        flops=1_000_000, moved=own.size * 2, mib=32,
    )
    got = [turn(sums[k], k, dp) for k in range(1, dp)]
    mine = call(
        functools.partial(add_all_kernel, dp), [sds((rows, WIRE), BF)], sums[0], *got,
        flops=1_000_000, moved=rows * WIRE * 10, mib=16,
    )[0]
    even = [mine] + [flip(mine, j, ex) for j in range(2, ex, 2)]
    out = []
    for one in even:
        out += [one, flip(one, 1, ex)]
    return out


def local(n_dp, n_ex, hidden_in, lengths, task_ids, task_experts, capacity, task_logits, norm_params,
          w_qkv, w_attn, w_up, w_down, expert_up, expert_down, cotangent):
    experts = capacity.shape[0]
    cap_slots = max(4 * hidden_in.shape[0] // experts, 2 * MOST_LEN)
    both = ("dp", "expert")
    me, here = lax.axis_index("expert"), lax.axis_index("dp")
    pos = jnp.stack([me, here]).astype(jnp.int32)
    split = (n_dp, n_ex)
    wire = wired(split)

    def mine(shard):
        rows = shard.shape[0] // n_ex
        return lax.dynamic_slice_in_dim(shard, me * rows, rows, 0)

    if wire:
        rows = piece_rows(split)

        def blocks(wide):
            return [wide[:, c * WIRE : (c + 1) * WIRE] for c in range(wide.shape[1] // WIRE)]

        norms = jnp.pad(mine(norm_params), ((0, 0), (0, WIRE - 8)))
        qkv, attn = mine(w_qkv), mine(w_attn)
        piece = jnp.concatenate(blocks(qkv[:, 0]) + [attn[:, 0], norms])
        zero = gather_pieces(piece, split)
        feed = gather_pieces(jnp.concatenate(blocks(mine(w_up)) + [mine(w_down)]), split)
        one = gather_pieces(jnp.concatenate(blocks(qkv[:, 1]) + [attn[:, 1]]), split)
        attn_zero, params = call(
            functools.partial(assemble_norm_kernel, split), [sds((D, 4 * D), BF), sds((8, D), F32)], pos, *zero,
            scratch=[pltpu.VMEM((D, 128), F32)], pos=True, flops=1_000_000, moved=4 << 20, mib=24,
        )
        up, down = assemble(split, pos, feed, True)
        attn_one = assemble(split, pos, one, False)[0]
    else:

        def gather_all(shard):
            return lax.all_gather(mine(shard), both, axis=0, tiled=True)

        params = lax.all_gather(norm_params, "dp", axis=0, tiled=True).astype(F32).T
        attn_zero = gather_all(jnp.concatenate([w_qkv[:, 0], w_attn[:, 0]], axis=1))
        up, down = gather_all(w_up), gather_all(w_down)
        attn_one = gather_all(jnp.concatenate([w_qkv[:, 1], w_attn[:, 1]], axis=1))
    up_expert = lax.all_gather(expert_up[0], "dp", axis=0, tiled=True)
    down_expert = lax.all_gather(expert_down[0], "dp", axis=0, tiled=True)

    rel = me if wire else 0
    tok, slot, gates = route(lengths, task_ids, task_experts, capacity, task_logits, cap_slots, rel)

    def exchange(blocks):
        if wire:
            return [blocks[0]] + [flip(blocks[j], j, n_ex) for j in range(1, n_ex)]
        rows = lax.all_to_all(jnp.stack(blocks), "expert", split_axis=0, concat_axis=0, tiled=True)
        return [rows[j] for j in range(n_ex)]

    dout_home = gather_rows(slot, cotangent, experts, True)
    dout = exchange(dout_home)
    h1, *saved_zero = attention_forward(hidden_in, params, tok, attn_zero, 0, False)
    h2, *saved_feed = feed_forward(h1, params, up, down)
    h3, *saved_one, c = attention_forward(h2, params, tok, attn_one, 4, True)
    buf = exchange(gather_rows(slot, c, experts, False))
    out, dbuf, held = [], [], ()
    step = 2
    for j in range(0, experts, step):
        some, back, held = expert_rows(
            buf[j : j + step], dout[j : j + step], up_expert, down_expert, experts * cap_slots, j * cap_slots, held
        )
        out += some
        dbuf += back
    dbuf_home = exchange(dbuf)
    gup_expert, gdown_expert = expert_grads(*held)
    expert_up_sum = lax.psum_scatter(gup_expert, "dp", scatter_dimension=0, tiled=True)
    expert_down_sum = lax.psum_scatter(gdown_expert, "dp", scatter_dimension=0, tiled=True)
    dx, gn_moe = combine_back(tok, dbuf_home, h3, cotangent, params)
    out_home = exchange([tie(one, gn_moe) for one in out])

    dx, gn_one, g_one = attention_backward(pos, dx, h2, saved_one, params, tok, attn_one, 4, split)
    dx, gn_feed, g_feed = feed_backward(pos, dx, h1, saved_feed, params, up, down, split)
    grad_in, gn_zero, g_zero = attention_backward(pos, dx, hidden_in, saved_zero, params, tok, attn_zero, 0, split)
    out_home = [tie(one, gn_zero) for one in out_home]
    hidden_out, table = combine_out(tok, slot, out_home, dout_home, h3)

    small = jnp.concatenate([gn_zero, gn_feed, gn_one, gn_moe], axis=0)
    table = jnp.take(table, jnp.bitwise_xor(jnp.arange(experts), rel), axis=0)
    table = jnp.pad(table, ((0, 0), (0, D - 128)))
    small = jnp.concatenate([small, table], axis=0)
    j = 1
    while j < n_ex:
        small = small + flip(small, j, n_ex)
        j *= 2
    j = 1
    while j < n_dp:
        small = small + lax.ppermute(small, "dp", [(i, i ^ j) for i in range(n_dp)])
        j *= 2
    gn = lax.dynamic_slice_in_dim(small[:8], here * (D // n_dp), D // n_dp, 1).T
    sums = small[8:, : task_logits.shape[0]].T

    if wire:
        parts = [reduce_pieces(*g, split) for g in (g_one, g_feed, g_zero)]
        rows = D // n_dp
        grad_qkv, grad_attn, grad_up, grad_down = call(
            functools.partial(spread_kernel, split, (0, 1), True),
            [sds((2, rows, 3 * D), F32), sds((2, rows, D), F32), sds((rows, FF), F32), sds((FF // n_dp, D), F32)],
            pos, *parts[2], *parts[0], *parts[1],
            pos=True, flops=1_000_000, moved=7 << 20, mib=32,
        )
        grad_qkv, grad_attn = grad_qkv.transpose(1, 0, 2), grad_attn.transpose(1, 0, 2)
    else:

        def reduce_all(grad):
            rows = grad.shape[0] // (n_dp * n_ex)
            grad = grad.reshape(n_dp, n_ex, rows, -1).transpose(1, 0, 2, 3).reshape(grad.shape)
            part = lax.psum_scatter(grad, "expert", scatter_dimension=0, tiled=True)
            part = lax.psum_scatter(part, "dp", scatter_dimension=0, tiled=True)
            return lax.all_gather(part, "expert", axis=0, tiled=True).astype(F32)

        g_one, grad_up, grad_down, g_zero = [reduce_all(g) for g in (*g_one, *g_feed, *g_zero)]
        grad_qkv = jnp.stack([g_zero[:, : 3 * D], g_one[:, : 3 * D]], axis=1)
        grad_attn = jnp.stack([g_zero[:, 3 * D :], g_one[:, 3 * D :]], axis=1)
    hot = task_experts[:, :, None] == lax.broadcasted_iota(jnp.int32, (1, 1, experts), 2)
    pair_sum = jnp.sum(jnp.where(hot, sums[:, None, :], 0.0), axis=2)
    lean = gates[:, 0] * gates[:, 1] * (pair_sum[:, 0] - pair_sum[:, 1])
    grad_logits = jnp.where(hot[:, 0], lean[:, None], 0.0) - jnp.where(hot[:, 1], lean[:, None], 0.0)
    return (
        hidden_out, grad_in, grad_logits, gn, grad_qkv, grad_attn, grad_up, grad_down,
        expert_up_sum.astype(F32)[None], expert_down_sum.astype(F32)[None],
    )


def solution(mesh):
    token = P(("dp", "expert"), None)
    expert = P("expert", "dp", None)
    in_specs = (
        token, token, token, P(), P(), P(), P("dp", None), P("dp", None, None), P("dp", None, None),
        P("dp", None), P("dp", None), expert, expert, token,
    )
    out_specs = (
        token, token, P(), P("dp", None), P("dp", None, None), P("dp", None, None), P("dp", None), P("dp", None),
        expert, expert,
    )
    step = functools.partial(local, mesh.shape["dp"], mesh.shape["expert"])
    return jax.shard_map(step, mesh=mesh, in_specs=in_specs, out_specs=out_specs, check_vma=False)
```

```python
import functools

import jax
import jax.numpy as jnp
from jax import lax
from jax.experimental import pallas as pl
from jax.experimental.pallas import tpu as pltpu
from jax.sharding import PartitionSpec as P

D = 512
FF = 2048
HEADS = 8
HEAD = D // HEADS
PACK = 1024
MOST_LEN = 64
ROWS = 256
QB = 128
KB = QB + 2 * MOST_LEN
EPS = 1e-05
BLOCKED = -1e30
BF = jnp.bfloat16
F32 = jnp.float32
GELU_C = 0.7978845608028654
GELU_A = 0.044715


COST = 4


def mm(left, right):
    return lax.dot_general(left, right, (((1,), (0,)), ((), ())), preferred_element_type=F32)


def mm_t(left, right):
    return lax.dot_general(left, right, (((1,), (1,)), ((), ())), preferred_element_type=F32)


def t_mm(left, right):
    return lax.dot_general(left, right, (((0,), (0,)), ((), ())), preferred_element_type=F32)


def unit_rows(hidden):
    centered = hidden - jnp.mean(hidden, axis=-1, keepdims=True)
    spread = jnp.mean(centered * centered, axis=-1, keepdims=True)
    scale = lax.rsqrt(spread + EPS)
    return centered * scale, scale


def unit_back(unit, scale, gain, grad):
    inner = grad * gain
    first = jnp.mean(inner, axis=-1, keepdims=True)
    second = jnp.mean(inner * unit, axis=-1, keepdims=True)
    return scale * (inner - first - unit * second)


def gelu_both(z):
    square = z * z
    half = 0.5 + 0.5 * jnp.tanh(z * (GELU_C + GELU_C * GELU_A * square))
    act = z * half
    return act, half + (act - act * half) * (2.0 * GELU_C + 6.0 * GELU_C * GELU_A * square)


def call(kernel, out_shape, *args, grid=None, in_specs=None, out_specs=None, scratch=(), mib=62, flops=0, moved=0,
         alias=None, pos=False):
    extra = {}
    if grid is not None and pos:
        extra["grid_spec"] = pltpu.PrefetchScalarGridSpec(
            num_scalar_prefetch=1, grid=grid, in_specs=in_specs, out_specs=out_specs, scratch_shapes=scratch
        )
    else:
        extra["scratch_shapes"] = scratch
        if grid is not None:
            extra.update(grid=grid, in_specs=in_specs, out_specs=out_specs)
        elif pos:
            held = pl.BlockSpec(memory_space=pltpu.VMEM)
            extra["in_specs"] = [pl.BlockSpec(memory_space=pltpu.SMEM)] + [held] * (len(args) - 1)
    if alias:
        extra["input_output_aliases"] = alias
    return pl.pallas_call(
        kernel,
        out_shape=out_shape,
        compiler_params=pltpu.CompilerParams(vmem_limit_bytes=mib << 20),
        cost_estimate=pl.CostEstimate(flops=flops // COST, bytes_accessed=moved // COST, transcendentals=0),
        **extra,
    )(*args)


def sds(shape, dtype):
    return jax.ShapeDtypeStruct(shape, dtype)


WIRE = 512


def piece_rows(split):
    dp, ex = split
    return D // (dp * ex)


def wired(split):
    dp, ex = split
    return piece_rows(split) % 16 == 0 and ex == 8


def near(split, pos_ref, j, k):
    return k * split[1] + jnp.bitwise_xor(pos_ref[0], j)


def send_rows(split, pos_ref, scr_ref, own_ref, core_ref, at, rows):
    dp, ex = split
    for j in range(ex):
        out = core_ref if j % 2 else own_ref
        for k in range(dp):
            start = pl.multiple_of(near(split, pos_ref, j, k) * rows, rows)
            out[j // 2, k, at : at + rows, :] = scr_ref[pl.ds(start, rows), :]


def wire_shapes(split, blocks):
    dp, ex = split
    shape = (ex // 2, dp, blocks * piece_rows(split), WIRE)
    return [sds(shape, BF), sds(shape, BF)]


WINDOW = 3 << 20


class Stage:
    def __init__(self, ins, outs, split_in, split_out, hold_in, hold_out, sem_in, sem_out, order):
        self.ins, self.outs = hold_in, hold_out
        self.split_in, self.split_out = split_in, split_out
        self.out_hbm, self.out_sem, self.sent = outs, sem_out, []
        self.got, self.begun, self.copies, self.bytes = set(), 0, {}, {}
        order = order or [(i, r) for i, parts in enumerate(split_in) for r in range(parts)]
        for n, (i, r) in enumerate(order):
            rows = self.rows(hold_in[i], split_in[i], r)
            self.copies[i, r] = pltpu.make_async_copy(ins[i].at[rows], hold_in[i].at[rows], sem_in.at[n])
            self.bytes[i, r] = hold_in[i].size * hold_in[i].dtype.itemsize // split_in[i]
        self.order = order
        self.ahead(0)

    def rows(self, ref, parts, r):
        size = ref.shape[0] // parts
        return pl.ds(r * size, size)

    def ahead(self, least):
        while self.begun < len(self.order):
            flying = sum(self.bytes[key] for key in self.order[: self.begun] if key not in self.got)
            if self.begun >= least and flying >= WINDOW:
                break
            self.copies[self.order[self.begun]].start()
            self.begun += 1

    def need(self, *which):
        for i in which:
            i, r = i if isinstance(i, tuple) else (i, None)
            for k in range(self.split_in[i]) if r is None else [r]:
                if (i, k) not in self.got:
                    self.ahead(self.order.index((i, k)) + 1)
                    self.copies[i, k].wait()
                    self.got.add((i, k))
                    self.ahead(0)

    def done(self, i, r=None):
        parts = self.split_out[i]
        for k in range(parts) if r is None else [r]:
            rows = self.rows(self.outs[i], parts, k)
            sem = self.out_sem.at[sum(self.split_out[:i]) + k]
            copy = pltpu.make_async_copy(self.outs[i].at[rows], self.out_hbm[i].at[rows], sem)
            copy.start()
            self.sent.append(copy)

    def finish(self):
        self.need(*self.order)
        for copy in self.sent:
            copy.wait()


def staged(body, outs, ins, small=(), small_outs=(), scratch=(), flops=0, moved=0, order=None):
    arrays, split_in = [x for x, _ in ins], [n for _, n in ins]
    shapes, split_out = [x for x, _ in outs], [n for _, n in outs]

    def kernel(*refs):
        at = 0
        groups = []
        for n in (len(small), len(arrays), len(small_outs), len(shapes), len(arrays), len(shapes), len(scratch), 2):
            groups.append(refs[at : at + n])
            at += n
        few, hbm_in, few_out, hbm_out, hold_in, hold_out, own, (sem_in, sem_out) = groups
        stage = Stage(hbm_in, hbm_out, split_in, split_out, hold_in, hold_out, sem_in, sem_out, order)
        body(stage, few, few_out, own)
        stage.finish()

    space = [pl.BlockSpec(memory_space=pltpu.SMEM if x.dtype == jnp.int32 else pltpu.VMEM) for x in small]
    got = pl.pallas_call(
        kernel,
        out_shape=list(small_outs) + shapes,
        in_specs=space + [pl.BlockSpec(memory_space=pl.ANY)] * len(arrays),
        out_specs=[pl.BlockSpec(memory_space=pltpu.VMEM)] * len(small_outs)
        + [pl.BlockSpec(memory_space=pl.ANY)] * len(shapes),
        scratch_shapes=[pltpu.VMEM(x.shape, x.dtype) for x in arrays + shapes]
        + list(scratch)
        + [pltpu.SemaphoreType.DMA((sum(split_in),)), pltpu.SemaphoreType.DMA((max(sum(split_out), 1),))],
        compiler_params=pltpu.CompilerParams(vmem_limit_bytes=62 << 20),
        cost_estimate=pl.CostEstimate(flops=flops // COST, bytes_accessed=moved // COST, transcendentals=0),
    )(*small, *arrays)
    return list(got)


def route_kernel(slots, sent_ref, pair_ref, tok_ref, slot_ref):
    t = lax.broadcasted_iota(jnp.int32, (PACK, 128), 0).astype(F32)
    start, end = sent_ref[0:1, :], sent_ref[1:2, :]
    member = (t >= start) & (t < end)

    def pick(value):
        return jnp.sum(jnp.where(member, value, 0.0), axis=1, keepdims=True)

    lane = lax.broadcasted_iota(jnp.int32, (PACK, 8), 1)
    out = jnp.where(lane == 0, pick(start), 0.0)
    out = jnp.where(lane == 1, pick(end), out)
    for k in range(2):
        base = sent_ref[2 + k : 3 + k, :]
        slot = pick(jnp.where(base >= 0, base - start + t + 1.0, 0.0)) - 1.0
        out = jnp.where(lane == 2 + k, slot, out)
    tok_ref[...] = out
    chunk = 512
    base, length, first = pair_ref[0:1, :], pair_ref[1:2, :], pair_ref[2:3, :]
    gate, task = pair_ref[3:4, :], pair_ref[4:5, :]
    for i in range(slots // chunk):
        s = lax.broadcasted_iota(jnp.int32, (chunk, 128), 0).astype(F32) + float(i * chunk)
        held = (base >= 0) & (s >= base) & (s < base + length)

        def take(value, held=held):
            return jnp.sum(jnp.where(held, value, 0.0), axis=1, keepdims=True)

        lane = lax.broadcasted_iota(jnp.int32, (chunk, 8), 1)
        out = jnp.where(lane == 0, take(first - base + s + 1.0) - 1.0, 0.0)
        out = jnp.where(lane == 1, take(gate), out)
        out = jnp.where(lane == 2, take(task + 1.0) - 1.0, out)
        slot_ref[i * chunk : (i + 1) * chunk, :] = out


def head_halves(block):
    low = lax.broadcasted_iota(jnp.int32, (1, 128), 1) < HEAD
    zero = jnp.zeros_like(block)
    return jnp.concatenate([jnp.where(low, block, zero), jnp.where(low, zero, block)], axis=0)


def merge_halves(stacked):
    low = lax.broadcasted_iota(jnp.int32, (1, 128), 1) < HEAD
    return jnp.where(low, stacked[:QB], stacked[QB:])


def key_start(i):
    return jnp.clip(i * QB - MOST_LEN, 0, PACK - KB)


def attention_kernel(norm_at, last, x_ref, np_ref, tok_ref, w_ref, *refs):
    if last:
        h_ref, a_ref, qkv_ref, ctx_ref, c_ref = refs
    else:
        h_ref, a_ref, qkv_ref, ctx_ref = refs
    gain, shift = np_ref[norm_at : norm_at + 1, :], np_ref[norm_at + 1 : norm_at + 2, :]
    for r in range(PACK // ROWS):
        rows = slice(r * ROWS, (r + 1) * ROWS)
        unit, _ = unit_rows(x_ref[rows, :].astype(F32))
        a = (unit * gain + shift).astype(BF)
        a_ref[rows, :] = a
        qkv_ref[rows, :] = mm(a, w_ref[:, 0 : 3 * D]).astype(BF)

    def block(i, carry):
        q0 = pl.multiple_of(i * QB, QB)
        k0 = pl.multiple_of(key_start(i), MOST_LEN)
        start, end = tok_ref[pl.ds(q0, QB), 0:1], tok_ref[pl.ds(q0, QB), 1:2]
        key = (lax.broadcasted_iota(jnp.int32, (QB, KB), 1) + k0).astype(F32)
        mask = (key >= start) & (key < end)
        mask = jnp.concatenate([mask, mask], axis=0)
        for pair in range(HEADS // 2):
            at = pair * 128
            q = head_halves(qkv_ref[pl.ds(q0, QB), at : at + 128] * BF(HEAD**-0.5))
            k = qkv_ref[pl.ds(k0, KB), D + at : D + at + 128]
            v = qkv_ref[pl.ds(k0, KB), 2 * D + at : 2 * D + at + 128]
            scores = jnp.where(mask, mm_t(q, k), BLOCKED)
            raised = jnp.exp(scores - jnp.max(scores, axis=1, keepdims=True))
            probs = (raised * (1.0 / jnp.sum(raised, axis=1, keepdims=True))).astype(BF)
            ctx_ref[pl.ds(q0, QB), at : at + 128] = merge_halves(mm(probs, v)).astype(BF)
        return carry

    lax.fori_loop(0, PACK // QB, block, 0)
    for r in range(PACK // ROWS):
        rows = slice(r * ROWS, (r + 1) * ROWS)
        h = x_ref[rows, :].astype(F32) + mm(ctx_ref[rows, :], w_ref[:, 3 * D : 4 * D])
        h_ref[rows, :] = h
        if last:
            unit, _ = unit_rows(h)
            c_ref[rows, :] = (unit * np_ref[6:7, :] + np_ref[7:8, :]).astype(BF)


def attention_forward(hidden, params, tok, weights, norm_at, last):
    outs = [sds((PACK, D), F32), sds((PACK, D), BF), sds((PACK, 3 * D), BF), sds((PACK, D), BF)]
    if last:
        outs.append(sds((PACK, D), BF))
    return call(
        functools.partial(attention_kernel, norm_at, last),
        outs, hidden, params, tok, weights,
        flops=6_000_000_000, moved=12 << 20, mib=40,
    )


def combine_grads(io, tok_ref, h_ref, cot_ref, blocks, np_ref, dx_ref, gn_ref, needs):
    for e, ref in enumerate(blocks):
        size = ref.shape[0] // 2
        io.need((needs[2 + e], e % 2))
        part = mm(slots_hot(tok_ref, size, e), ref[e % 2 * size : (e % 2 + 1) * size, :])
        dx_ref[...] = part if e == 0 else dx_ref[...] + part
    io.need(*needs[:2])
    dgain, dshift = jnp.zeros((1, D), F32), jnp.zeros((1, D), F32)
    for r in range(PACK // ROWS):
        rows = slice(r * ROWS, (r + 1) * ROWS)
        dnorm = dx_ref[rows, :]
        unit, scale = unit_rows(h_ref[rows, :])
        dgain += jnp.sum(dnorm * unit, axis=0, keepdims=True)
        dshift += jnp.sum(dnorm, axis=0, keepdims=True)
        dx_ref[rows, :] = cot_ref[rows, :].astype(F32) + unit_back(unit, scale, np_ref[6:7, :], dnorm)
    gn_ref[0:1, :] = dgain
    gn_ref[1:2, :] = dshift


def attention_core_back(io, dx_ref, dx_at, w_ref, w_at, tok_ref, qkv_ref, at_need, dctx_ref, dqkv_ref, acc_ref):
    io.need(w_at)
    for r in range(PACK // ROWS):
        rows = slice(r * ROWS, (r + 1) * ROWS)
        if dx_at is not None:
            io.need((dx_at, r))
        dctx_ref[rows, :] = mm_t(dx_ref[rows, :].astype(BF), w_ref[:, 3 * D : 4 * D]).astype(BF)
    acc_ref[...] = jnp.zeros_like(acc_ref)
    io.need(*at_need)

    def block(i, carry):
        q0 = pl.multiple_of(i * QB, QB)
        k0 = pl.multiple_of(key_start(i), MOST_LEN)
        start, end = tok_ref[pl.ds(k0, KB), 0:1], tok_ref[pl.ds(k0, KB), 1:2]
        query = (lax.broadcasted_iota(jnp.int32, (KB, QB), 1) + q0).astype(F32)
        mask = (query >= start) & (query < end)
        mask = jnp.concatenate([mask, mask], axis=1)
        for pair in range(HEADS // 2):
            at = pair * 128
            q = head_halves(qkv_ref[pl.ds(q0, QB), at : at + 128] * BF(HEAD**-0.5))
            k = qkv_ref[pl.ds(k0, KB), D + at : D + at + 128]
            v = qkv_ref[pl.ds(k0, KB), 2 * D + at : 2 * D + at + 128]
            g = head_halves(dctx_ref[pl.ds(q0, QB), at : at + 128])
            scores = jnp.where(mask, mm_t(k, q), BLOCKED)
            raised = jnp.exp(scores - jnp.max(scores, axis=0, keepdims=True))
            probs = raised * (1.0 / jnp.sum(raised, axis=0, keepdims=True))
            dprobs = mm_t(v, g)
            delta = jnp.sum(probs * dprobs, axis=0, keepdims=True)
            dscores = (probs * (dprobs - delta)).astype(BF)
            acc_ref[pl.ds(k0, KB), at : at + 128] += mm(dscores, q)
            acc_ref[pl.ds(k0, KB), D + at : D + at + 128] += mm(probs.astype(BF), g)
            dq = merge_halves(t_mm(dscores, k)) * (HEAD**-0.5)
            dqkv_ref[pl.ds(q0, QB), at : at + 128] = dq.astype(BF)
        return carry

    lax.fori_loop(0, PACK // QB, block, 0)
    dqkv_ref[:, D:] = acc_ref[...].astype(BF)


def attention_weight_back(split, pos_ref, a_ref, ctx_ref, dx_ref, dqkv_ref, grads, scr_ref):
    rows = piece_rows(split)
    for c in range(4):
        cols = slice(c * D, (c + 1) * D)
        if c < 3:
            grad = t_mm(a_ref[...], dqkv_ref[:, cols]).astype(BF)
        else:
            grad = t_mm(ctx_ref[...], dx_ref[...].astype(BF)).astype(BF)
        if wired(split):
            scr_ref[...] = grad
            send_rows(split, pos_ref, scr_ref, grads[0], grads[1], c * rows, rows)
        else:
            grads[0][:, cols] = grad


def first_back_kernel(split, norm_at, io, few, few_out, own):
    pos_ref, np_ref = few
    tok_ref, h_ref, cot_ref, w_ref, qkv_ref, a_ref, ctx_ref, x_ref = io.ins[:8]
    dx_ref, dctx_ref, dqkv_ref, acc_ref, scr_ref = own
    blocks = io.ins[8:]
    io.need(0)
    combine_grads(io, tok_ref, h_ref, cot_ref, blocks, np_ref, dx_ref, few_out[1], [1, 2] + list(range(8, 8 + len(blocks))))
    attention_core_back(io, dx_ref, None, w_ref, 3, tok_ref, qkv_ref, [4], dctx_ref, dqkv_ref, acc_ref)
    io.need(5, 6, 7)
    attention_weight_back(split, pos_ref, a_ref, ctx_ref, dx_ref, dqkv_ref, io.outs[1:], scr_ref)
    for n in range(1, len(io.outs)):
        io.done(n)
    norm_back_rows(norm_at, dx_ref, x_ref, dqkv_ref, np_ref, w_ref, io.outs[0], few_out[0], io)


def first_backward(pos, blocks, h, cotangent, hidden, saved, params, tok, weights, norm_at, split):
    a, qkv, ctx = saved
    grads = wire_shapes(split, 4) if wired(split) else [sds((D, 4 * D), BF)]
    ins = [(x, 1) for x in (tok, h, cotangent, weights, qkv, a, ctx, hidden)] + [(x, 2) for x in blocks]
    order = [(0, 0)] + [(8 + n, n % 2) for n in range(len(blocks))] + [(n, 0) for n in range(1, 8)]
    norm, norm_moe, out, *grads = staged(
        functools.partial(first_back_kernel, split, norm_at),
        [(sds((PACK, D), F32), 4)] + [(x, 1) for x in grads], ins, [pos, params], [sds((2, D), F32)] * 2,
        [pltpu.VMEM((PACK, D), F32), pltpu.VMEM((PACK, D), BF), pltpu.VMEM((PACK, 3 * D), BF),
         pltpu.VMEM((PACK, 2 * D), F32), pltpu.VMEM((D, D), BF)],
        flops=16_000_000_000, moved=20 << 20, order=order,
    )
    return norm, norm_moe, out, grads


def last_back_kernel(split, norm_at, io, few, few_out, own):
    pos_ref, np_ref, more = few[0], few[1], few[2:]
    dx_ref, w_ref, tok_ref, qkv_ref, a_ref, ctx_ref, x_ref = io.ins
    gn_ref, grads = few_out[0], io.outs[1:]
    dctx_ref, dqkv_ref, acc_ref, scr_ref, row_ref = own
    attention_core_back(io, dx_ref, 0, w_ref, 1, tok_ref, qkv_ref, [2, 3], dctx_ref, dqkv_ref, acc_ref)
    io.need(4, 5, 6)
    attention_weight_back(split, pos_ref, a_ref, ctx_ref, dx_ref, dqkv_ref, grads, scr_ref)
    norm_back_rows(norm_at, dx_ref, x_ref, dqkv_ref, np_ref, w_ref, io.outs[0], gn_ref, io)
    if wired(split):
        dp, ex = split
        rows, wide = piece_rows(split), D // dp
        for n, ref in enumerate((gn_ref,) + tuple(more[:-1])):
            for i in range(2):
                for d in range(dp):
                    row_ref[(2 * n + i) * dp + d : (2 * n + i) * dp + d + 1, :] = ref[i : i + 1, d * wide : (d + 1) * wide]
        first = lax.broadcasted_iota(jnp.int32, (16, WIRE), 0) == 0
        for j in range(ex):
            for k in range(dp):
                at = jnp.bitwise_xor(pos_ref[0], j) * dp + k
                table = jnp.zeros((1, 128), F32) if j else more[-1][0:1, :]
                row = jnp.concatenate(
                    [row_ref[pl.ds(at, 1), :], table, jnp.zeros((1, WIRE - wide - 128), F32)], axis=1
                )
                grads[j % 2][j // 2, k, 4 * rows : 4 * rows + 16, :] = jnp.where(first, row, 0.0).astype(BF)
    for n in range(1, len(io.outs)):
        io.done(n)


def last_backward(pos, dx, hidden, saved, params, tok, weights, norm_at, split, more):
    a, qkv, ctx = saved
    grads = wire_shapes(split, 5) if wired(split) else [sds((D, 4 * D), BF)]
    norm, out, *grads = staged(
        functools.partial(last_back_kernel, split, norm_at),
        [(sds((PACK, D), F32), 4)] + [(x, 1) for x in grads],
        [(dx, 4), (weights, 1), (tok, 1), (qkv, 1), (a, 1), (ctx, 1), (hidden, 1)], [pos, params, *more],
        [sds((2, D), F32)],
        [pltpu.VMEM((PACK, D), BF), pltpu.VMEM((PACK, 3 * D), BF), pltpu.VMEM((PACK, 2 * D), F32),
         pltpu.VMEM((D, D), BF), pltpu.VMEM((8 * split[0], D // split[0]), F32)],
        flops=14_000_000_000, moved=16 << 20,
        order=[(0, 0), (1, 0), (0, 1), (0, 2), (0, 3), (2, 0), (3, 0), (4, 0), (5, 0), (6, 0)],
    )
    return norm, out, grads


def feed_kernel(io, few, few_out, own):
    (np_ref,) = few
    x_ref, up_ref, down_ref = io.ins
    h_ref, n_ref, act_ref, slope_ref = io.outs
    gain, shift = np_ref[2:3, :], np_ref[3:4, :]
    for r in range(PACK // ROWS):
        rows = slice(r * ROWS, (r + 1) * ROWS)
        io.need((0, r))
        x = x_ref[rows, :]
        unit, _ = unit_rows(x)
        n = (unit * gain + shift).astype(BF)
        n_ref[rows, :] = n
        io.need(1)
        act, slope = gelu_both(mm(n, up_ref[...]))
        act = act.astype(BF)
        act_ref[rows, :] = act
        slope_ref[rows, :] = slope.astype(BF)
        io.need(2)
        h_ref[rows, :] = x + mm(act, down_ref[...])
        for i in range(4):
            io.done(i, r)


def feed_forward(hidden, params, up, down):
    return staged(
        feed_kernel,
        [(sds((PACK, D), F32), 4), (sds((PACK, D), BF), 4), (sds((PACK, FF), BF), 4), (sds((PACK, FF), BF), 4)],
        [(hidden, 4), (up, 1), (down, 1)], [params], flops=4_300_000_000, moved=17 << 20,
        order=[(0, 0), (1, 0), (2, 0), (0, 1), (0, 2), (0, 3)],
    )


def feed_back_kernel(split, io, few, few_out, own):
    wire = wired(split)
    pos_ref, np_ref = few
    dx_ref, down_ref, slope_ref, n_ref, act_ref, up_ref, x_ref = io.ins
    out_ref, grads = io.outs[0], io.outs[1:]
    dz_ref, dy_ref, scr_ref, tall_ref = own
    for r in range(PACK // ROWS):
        rows = slice(r * ROWS, (r + 1) * ROWS)
        io.need((0, r), 1, (2, r))
        dy = dx_ref[rows, :].astype(BF)
        dy_ref[rows, :] = dy
        dz_ref[rows, :] = (mm_t(dy, down_ref[...]) * slope_ref[rows, :].astype(F32)).astype(BF)
    io.need(3, 4)
    if wire:
        rows = piece_rows(split)
        for c in range(FF // D):
            scr_ref[...] = t_mm(n_ref[...], dz_ref[:, c * D : (c + 1) * D]).astype(BF)
            send_rows(split, pos_ref, scr_ref, *grads, c * rows, rows)
        for c in range(FF // D):
            tall_ref[c * D : (c + 1) * D, :] = t_mm(act_ref[:, c * D : (c + 1) * D], dy_ref[...]).astype(BF)
        send_rows(split, pos_ref, tall_ref, *grads, FF // D * rows, FF // D * rows)
    else:
        grads[0][...] = t_mm(n_ref[...], dz_ref[...]).astype(BF)
        grads[1][...] = t_mm(act_ref[...], dy_ref[...]).astype(BF)
    io.done(1)
    io.done(2)
    io.need(5, 6)
    norm_back_rows(2, dx_ref, x_ref, dz_ref, np_ref, up_ref, out_ref, few_out[0], io)


def feed_backward(pos, dx, hidden, saved, params, up, down, split):
    n, act, slope = saved
    grads = wire_shapes(split, 8) if wired(split) else [sds((D, FF), BF), sds((FF, D), BF)]
    norm, out, *grads = staged(
        functools.partial(feed_back_kernel, split),
        [(sds((PACK, D), F32), 4)] + [(x, 1) for x in grads],
        [(dx, 4), (down, 1), (slope, 4), (n, 1), (act, 1), (up, 1), (hidden, 1)], [pos, params], [sds((2, D), F32)],
        scratch=[pltpu.VMEM((PACK, FF), BF), pltpu.VMEM((PACK, D), BF), pltpu.VMEM((D, D), BF), pltpu.VMEM((FF, D), BF)],
        order=[(0, 0), (1, 0), (2, 0)] + [(i, r) for r in range(1, 4) for i in (0, 2)] + [(n, 0) for n in range(3, 7)],
        flops=8_600_000_000, moved=24 << 20,
    )
    return norm, out, grads


def norm_back_rows(norm_at, dx_ref, x_ref, grad_ref, np_ref, w_ref, out_ref, gn_ref, io, needs=()):
    gain = np_ref[norm_at : norm_at + 1, :]
    dgain, dshift = jnp.zeros((1, D), F32), jnp.zeros((1, D), F32)
    for r in range(PACK // ROWS):
        rows = slice(r * ROWS, (r + 1) * ROWS)
        for i in needs:
            io.need((i, r))
        dnorm = mm_t(grad_ref[rows, :], w_ref[:, : grad_ref.shape[1]])
        unit, scale = unit_rows(x_ref[rows, :].astype(F32))
        dgain += jnp.sum(dnorm * unit, axis=0, keepdims=True)
        dshift += jnp.sum(dnorm, axis=0, keepdims=True)
        out_ref[rows, :] = dx_ref[rows, :] + unit_back(unit, scale, gain, dnorm)
        io.done(0, r)
    gn_ref[0:1, :] = dgain
    gn_ref[1:2, :] = dshift


def assemble_kernel(split, blocks, tall, *refs):
    dp, ex = split
    rows = piece_rows(split)
    pos_ref, pieces, outs = refs[0], refs[1 : 1 + ex], refs[1 + ex :]
    for j in range(ex):
        for k in range(dp):
            at = lax.rem(pos_ref[1] + dp - k, dp) * ex + jnp.bitwise_xor(pos_ref[0], j)
            start = pl.multiple_of(at * rows, rows)
            for c in range(blocks):
                outs[0][pl.ds(start, rows), c * WIRE : (c + 1) * WIRE] = pieces[j][k, c * rows : (c + 1) * rows, :]
            if tall:
                high = blocks * rows
                start = pl.multiple_of(at * high, high)
                outs[1][pl.ds(start, high), :] = pieces[j][k, high : 2 * high, :]


def assemble(split, pos, pieces, tall):
    outs = [sds((D, 4 * D), BF)] + ([sds((FF, D), BF)] if tall else [])
    return call(
        functools.partial(assemble_kernel, split, 4, tall), outs, pos, *pieces,
        pos=True, flops=1_000_000, moved=4 << 20, mib=24,
    )


def assemble_norm_kernel(split, *refs):
    dp, ex = split
    rows = piece_rows(split)
    pos_ref, pieces, (w_ref, np_ref, scr_ref) = refs[0], refs[1 : 1 + ex], refs[1 + ex :]
    for j in range(ex):
        for k in range(dp):
            at = lax.rem(pos_ref[1] + dp - k, dp) * ex + jnp.bitwise_xor(pos_ref[0], j)
            start = pl.multiple_of(at * rows, rows)
            for c in range(4):
                w_ref[pl.ds(start, rows), c * WIRE : (c + 1) * WIRE] = pieces[j][k, c * rows : (c + 1) * rows, :]
            scr_ref[pl.ds(start, rows), :] = pieces[j][k, 4 * rows : 5 * rows, 0:128].astype(F32)
    np_ref[...] = jnp.transpose(scr_ref[...])[:8]


def add_core_kernel(near, io, few, few_out, own):
    mine_ref, got_ref = io.ins
    for j in range(mine_ref.shape[0]):
        io.need((0, j), (1, j))
        total = (mine_ref[j].astype(F32) + got_ref[j].astype(F32)).astype(BF)
        if near:
            io.outs[j][...] = total
            io.done(j)
        else:
            io.outs[0][jnp.bitwise_xor(few[0][0] // 2, j)] = total
    if not near:
        io.done(0)


def add_near_kernel(lists, pos_ref, *refs):
    ins, outs = refs[: sum(lists)], refs[sum(lists) :]
    dp = len(outs)
    for k, out in enumerate(outs):
        at = lax.rem(pos_ref[1] + k, dp)
        first, top = 0, 0
        for n in lists:
            parts = ins[first : first + n]
            first += n
            parts = [parts[0].at[i] for i in range(parts[0].shape[0])] if n == 1 else parts
            total = parts[0][at].astype(F32)
            for part in parts[1:]:
                total = total + part[at].astype(F32)
            out[top : top + total.shape[0], :] = total.astype(BF)
            top += total.shape[0]


def add_turn_kernel(*refs):
    total = refs[0][...].astype(F32)
    for ref in refs[1:-1]:
        total = total + ref[...].astype(F32)
    refs[-1][...] = total.astype(BF)


def spread_kernel(split, *refs):
    dp, ex = split
    rows = piece_rows(split)
    pos_ref, last_ref, early_ref, qkv_ref, attn_ref, up_ref, down_ref, gn_ref, table_ref = refs

    def put(n, start, piece):
        for c in range(3):
            qkv_ref[n, pl.ds(start, rows), c * D : (c + 1) * D] = piece[c * rows : (c + 1) * rows]
        attn_ref[n, pl.ds(start, rows), :] = piece[3 * rows : 4 * rows]

    for j in range(ex):
        start, high = j * rows, j * 4 * rows
        piece = early_ref[j].astype(F32)
        for c in range(4):
            up_ref[pl.ds(start, rows), c * D : (c + 1) * D] = piece[c * rows : (c + 1) * rows]
        down_ref[pl.ds(high, 4 * rows), :] = piece[4 * rows : 8 * rows]
        put(1, start, piece[8 * rows :])
        piece = last_ref[j].astype(F32)
        put(0, j * rows, piece)
        gn_ref[j : j + 1, :] = piece[4 * rows : 4 * rows + 1, 0 : D // dp]
        table_ref[j : j + 1, :] = piece[4 * rows : 4 * rows + 1, D // dp : D // dp + 128]


def gather_kernel(io, few, few_out, own):
    src_ref, slot_ref = io.ins
    pairs = len(io.outs)
    size = io.outs[0].shape[0] // 2
    tokens = lax.broadcasted_iota(jnp.int32, (size, PACK), 1).astype(F32)
    io.need(0)
    for n in range(2 * pairs):
        io.need((1, n))
        hot = jnp.where(slot_ref[n * size : (n + 1) * size, 0:1] == tokens, 1.0, 0.0).astype(BF)
        io.outs[n // 2][n % 2 * size : (n % 2 + 1) * size, :] = mm(hot, src_ref[...]).astype(BF)
        io.done(n // 2, n % 2)


def gather_rows(slot, source, experts):
    size = slot.shape[0] // experts
    return staged(
        gather_kernel, [(sds((2 * size, D), BF), 2)] * (experts // 2), [(source, 1), (slot, experts)],
        flops=2 * slot.shape[0] * PACK * D, moved=6 << 20,
    )


def gather_near_kernel(at, io, few, few_out, own):
    (pair_ref,) = few
    size = io.outs[0].shape[0] // len(io.ins)
    tokens = lax.broadcasted_iota(jnp.int32, (size, PACK), 1).astype(F32)
    lane = lax.broadcasted_iota(jnp.int32, (size, 8), 1)
    for n, source in enumerate(io.ins):
        one = 8 * (at + n)
        base, length, first, gate, task = [pair_ref[one + i : one + i + 1, :] for i in range(5)]
        s = lax.broadcasted_iota(jnp.int32, (size, 128), 0).astype(F32) + float((at + n) * size)
        held = (base >= 0) & (s >= base) & (s < base + length)

        def take(value, held=held):
            return jnp.sum(jnp.where(held, value, 0.0), axis=1, keepdims=True)

        gate, task = take(gate), take(task + 1.0) - 1.0
        hot = jnp.where(take(first - base + s + 1.0) - 1.0 == tokens, 1.0, 0.0).astype(BF)
        io.need(n)
        rows = slice(n * size, (n + 1) * size)
        io.outs[0][rows, :] = (mm(hot, source[...]) * gate).astype(BF)
        io.outs[1][rows, :] = jnp.where(lane == 0, gate, jnp.where(lane == 1, task, 0.0))
        io.done(0, n)
        io.done(1, n)


def gather_near(pairs, sources, size, at):
    count = len(sources)
    return staged(
        functools.partial(gather_near_kernel, at),
        [(sds((count * size, D), BF), count), (sds((count * size, 8), F32), count)], [(x, 1) for x in sources], [pairs],
        flops=2 * count * size * PACK * D, moved=4 << 20,
    )


def slots_hot(tok_ref, size, n):
    at = lax.broadcasted_iota(jnp.int32, (PACK, size), 1).astype(F32) + float(n * size)
    return jnp.where((tok_ref[:, 2:3] == at) | (tok_ref[:, 3:4] == at), 1.0, 0.0).astype(BF)


def whole(shape):
    return pl.BlockSpec(shape, lambda e: (0,) * len(shape))


def combine_out_kernel(experts, io, few, few_out, own):
    pos_ref = few[0]
    tok_ref, slot_ref, rows_ref, h_ref = io.ins
    acc_ref, size = own[0], rows_ref.shape[0] // experts
    io.need(0, 1, 2)
    for e in range(experts):
        start = pl.multiple_of(jnp.bitwise_xor(pos_ref[0], e) * size, size)
        rows = rows_ref[pl.ds(start, size), :].astype(F32)
        part = mm(slots_hot(tok_ref, size, e), (rows * slot_ref[e * size : (e + 1) * size, 1:2]).astype(BF))
        acc_ref[...] = part if e == 0 else acc_ref[...] + part
    for r in range(PACK // ROWS):
        rows = slice(r * ROWS, (r + 1) * ROWS)
        io.need((3, r))
        io.outs[0][rows, :] = (h_ref[rows, :] + acc_ref[rows, :]).astype(BF)
        io.done(0, r)


def combine_out(pos, tok, slot, rows, hidden, experts):
    return staged(
        functools.partial(combine_out_kernel, experts), [(sds((PACK, D), BF), 4)],
        [(tok, 1), (slot, 1), (rows, 1), (hidden, 4)], [pos], scratch=[pltpu.VMEM((PACK, D), F32)],
        flops=2 * 4096 * PACK * D, moved=14 << 20,
    )[0]


def expert_kernel(count, steps, *refs):
    bufs = refs[1 : 1 + count]
    dout_in, slot_ref, up_ref, down_ref = refs[1 + count : 5 + count]
    dbufs = refs[-count // 2 - 6 : -6]
    table_ref, out_ref, act_ref, du_ref, buf_ref, dout_ref = refs[-6:]
    i = pl.program_id(0)

    @pl.when(i == 0)
    def _():
        table_ref[...] = jnp.zeros_like(table_ref)

    def work(n):
        buf, dout = bufs[n][...], dout_in[...]
        buf_ref[...] = buf
        dout_ref[...] = dout
        z, dact = mm(buf, up_ref[...]), mm_t(dout, down_ref[...])
        act, slope = gelu_both(z)
        act = act.astype(BF)
        act_ref[...] = act
        out = mm(act, down_ref[...]).astype(BF)
        du = (dact * slope).astype(BF)
        du_ref[...] = du
        dbufs[n // 2][...] = mm_t(du, up_ref[...]).astype(BF)
        out_ref[...] = out
        gate, task = slot_ref[:, 0:1], slot_ref[:, 1:2]
        dgate = jnp.sum(out.astype(F32) * dout.astype(F32), axis=1, keepdims=True)
        dgate = jnp.where(task >= 0, dgate / jnp.where(task >= 0, gate, 1.0), 0.0)
        tasks = lax.broadcasted_iota(jnp.int32, (buf.shape[0], 128), 1).astype(F32)
        table_ref[0:1, :] += jnp.sum(jnp.where(tasks == task, dgate, 0.0), axis=0, keepdims=True)

    for n in range(count):
        pl.when(i // steps == n)(functools.partial(work, n))


def expert_rows(pos, bufs, dout, slot, up, down, total, at, held):
    rows = bufs[0].shape[0] // 2
    count = len(bufs)
    size = min(256, rows)
    steps = rows // size
    blocks = [
        pl.BlockSpec((size, D), lambda i, p, n=n: (jnp.clip(i - n * steps, 0, steps - 1) + n % 2 * steps, 0))
        for n in range(count)
    ]
    pairs = [
        pl.BlockSpec((size, D), lambda i, p, n=n: (jnp.clip(i - 2 * n * steps, 0, 2 * steps - 1), 0))
        for n in range(count // 2)
    ]

    def there(i, p):
        return (jnp.bitwise_xor(p[0], at + i // steps) * steps + lax.rem(i, steps), 0)

    def fixed(shape):
        return pl.BlockSpec(shape, lambda i, p: (0, 0), pipeline_mode=pl.Buffered(1))

    first = at * steps

    def tile(cols, first=first):
        return pl.BlockSpec((size, cols), lambda i, p: (i + first, 0))

    alias = {count + 5 + n: count // 2 + 1 + n for n in range(5)} if held else None
    outs = call(
        functools.partial(expert_kernel, count, steps),
        [sds((2 * rows, D), BF)] * (count // 2) + [sds((8, 128), F32)]
        + [sds((total, cols), BF) for cols in (D, FF, FF, D, D)],
        pos, *bufs, dout, slot, up, down, *held,
        grid=(count * steps,), pos=True,
        in_specs=blocks + [tile(D, 0), tile(8, 0), fixed((D, FF)), fixed((FF, D))]
        + [pl.BlockSpec(memory_space=pl.ANY)] * len(held),
        out_specs=pairs + [pl.BlockSpec((8, 128), lambda i, p: (0, 0)), pl.BlockSpec((size, D), there)]
        + [tile(FF), tile(FF), tile(D), tile(D)],
        alias=alias,
        flops=8 * rows * count * D * FF, moved=count * rows * 13 << 10,
    )
    return outs[: count // 2], outs[count // 2], outs[count // 2 + 1 :]


def expert_grad_kernel(steps, act_ref, du_ref, buf_ref, dout_ref, gup_ref, gdown_ref, up_acc, down_acc):
    i = pl.program_id(0)

    @pl.when(i == 0)
    def _():
        up_acc[...] = jnp.zeros_like(up_acc)
        down_acc[...] = jnp.zeros_like(down_acc)

    up_acc[...] += t_mm(buf_ref[...], du_ref[...])
    down_acc[...] += t_mm(act_ref[...], dout_ref[...])

    @pl.when(i == steps - 1)
    def _():
        gup_ref[...] = up_acc[...].astype(BF)
        gdown_ref[...] = down_acc[...].astype(BF)


def expert_grads(act, du, buf, dout):
    rows = buf.shape[0]
    size = 1024
    tile = lambda cols: pl.BlockSpec((size, cols), lambda i: (i, 0))
    return call(
        functools.partial(expert_grad_kernel, rows // size),
        [sds((D, FF), BF), sds((FF, D), BF)], act, du, buf, dout,
        grid=(rows // size,),
        in_specs=[tile(FF), tile(FF), tile(D), tile(D)],
        out_specs=[whole((D, FF)), whole((FF, D))],
        scratch=[pltpu.VMEM((D, FF), F32), pltpu.VMEM((FF, D), F32)],
        flops=4 * rows * D * FF, moved=44 << 20, mib=62,
    )


def route(lengths, task_ids, task_experts, capacity, task_logits, cap_slots, rel):
    sentences = lengths.shape[1]
    experts = capacity.shape[0]
    tasks = task_experts.shape[0]
    lens, ids = lengths.reshape(-1), task_ids.reshape(-1)
    ends = jnp.cumsum(lens)
    starts = ends - lens
    table = jnp.take_along_axis(task_logits, task_experts, axis=1)
    gates = jax.nn.softmax(table, axis=-1)
    hot = ids[:, None] == lax.broadcasted_iota(jnp.int32, (1, tasks), 1)
    expert = jnp.sum(jnp.where(hot[:, :, None], task_experts[None], 0), axis=1)
    gate = jnp.sum(jnp.where(hot[:, :, None], gates[None], 0.0), axis=1)
    pair_expert = expert.reshape(-1)
    pair_len = jnp.repeat(lens, 2)
    expert_hot = (pair_expert[:, None] == lax.broadcasted_iota(jnp.int32, (1, experts), 1)).astype(jnp.int32)
    running = jnp.cumsum(expert_hot * pair_len[:, None], axis=0)
    filled = jnp.sum(running * expert_hot, axis=1)
    limits = jnp.sum(expert_hot * capacity[None, :], axis=1)
    base = jnp.where(filled <= limits, jnp.bitwise_xor(pair_expert, rel) * cap_slots + filled - pair_len, -1)
    base_two = base.reshape(sentences, 2)

    def lanes(rows):
        rows = jnp.stack([row.astype(F32) for row in rows])
        return jnp.pad(rows, ((0, 8 - rows.shape[0]), (0, 128 - rows.shape[1])))

    sent = lanes([starts, ends, base_two[:, 0], base_two[:, 1]])
    pair = lanes([base, pair_len, jnp.repeat(starts, 2), gate.reshape(-1), jnp.repeat(ids, 2)])
    slots = experts * cap_slots
    tok, slot = call(
        functools.partial(route_kernel, slots),
        [sds((PACK, 8), F32), sds((slots, 8), F32)], sent, pair,
        flops=1_000_000, moved=3 << 20, mib=24,
    )
    return tok, slot, pair, gates


EXPERT = ("xy", "core")
BOTH = ("dp", "xy", "core")


def flip(rows, j, ex):
    return lax.ppermute(rows, EXPERT, [(i, i ^ j) for i in range(ex)])


def turn(rows, k, dp):
    return lax.ppermute(rows, "dp", [(i, (i + k) % dp) for i in range(dp)])


def tie(value, *after):
    return lax.optimization_barrier((value,) + after)[0]


def send_even(here, ex):
    return [here] + [flip(here, j, ex) for j in range(2, ex, 2)]


def send_core(even, ex):
    got = []
    for one in even:
        got += [one, flip(one, 1, ex)]
    return got


def add_core(pos, own, got, near=False):
    parts = own.shape[0]
    outs = [(sds(own.shape[1:], BF), 1)] * parts if near else [(sds(own.shape, BF), parts)]
    got = staged(
        functools.partial(add_core_kernel, near), outs, [(own, parts), (got, parts)], [pos],
        order=[(i, j) for j in range(parts) for i in range(2)], flops=1_000_000, moved=own.size * 6,
    )
    return got if near else got[0]


def add_near(pos, *lists):
    lists = [one if isinstance(one, list) else [one] for one in lists]
    rows = sum(one[0].shape[-2] for one in lists)
    dp = lists[0][0].shape[-3]
    return call(
        functools.partial(add_near_kernel, [len(one) for one in lists]), [sds((rows, WIRE), BF)] * dp,
        pos, *sum(lists, []), pos=True, flops=1_000_000, moved=rows << 14,
    )


def send_near(sums, ex):
    return [sums[0]] + [flip(sums[j], 2 * j, ex) for j in range(1, ex // 2)]


def send_turn(sums, dp):
    return [sums[0]] + [turn(sums[k], k, dp) for k in range(1, dp)]


def add_turn(got):
    return call(add_turn_kernel, sds(got[0].shape, BF), *got, flops=1_000_000, moved=got[0].size * 10, mib=62)


def swap(parts, axis):
    return lax.all_to_all(parts, axis, split_axis=0, concat_axis=0, tiled=True)


def local(n_dp, n_ex, hidden_in, lengths, task_ids, task_experts, capacity, task_logits, norm_params,
          w_qkv, w_attn, w_up, w_down, expert_up, expert_down, cotangent):
    experts = capacity.shape[0]
    cap_slots = max(4 * hidden_in.shape[0] // experts, 2 * MOST_LEN)
    slots = experts * cap_slots
    me, here = lax.axis_index(EXPERT), lax.axis_index("dp")
    pos = jnp.stack([me, here]).astype(jnp.int32)
    split = (n_dp, n_ex)
    wire = wired(split)

    def mine(shard):
        rows = shard.shape[0] // n_ex
        return lax.dynamic_slice_in_dim(shard, me * rows, rows, 0)

    def exchange(pair, j):
        return flip(pair, j, n_ex) if j else pair

    tok, slot, pair, gates = route(lengths, task_ids, task_experts, capacity, task_logits, cap_slots, me)
    if wire:
        rows = piece_rows(split)

        def blocks(wide):
            return [wide[:, c * WIRE : (c + 1) * WIRE] for c in range(wide.shape[1] // WIRE)]

        norms = jnp.pad(mine(norm_params), ((0, 0), (0, WIRE - 8)))
        qkv, attn = mine(w_qkv), mine(w_attn)
        piece = blocks(qkv[:, 0]) + [attn[:, 0], norms] + blocks(mine(w_up)) + [mine(w_down)]
        piece = jnp.concatenate(piece + blocks(qkv[:, 1]) + [attn[:, 1]])
        parts = [piece] + [turn(piece, k, n_dp) for k in range(1, n_dp)]
        expert_up, expert_down = tie(expert_up, *parts[1:]), tie(expert_down, *parts[1:])
        zero, feed, one = [
            jnp.stack([part[lo * rows : hi * rows] for part in parts]) for lo, hi in ((0, 5), (5, 13), (13, 17))
        ]
        cots = [cotangent, flip(cotangent, 2, n_ex), flip(cotangent, 4, n_ex)]
        zero = send_even(tie(zero, *cots[1:]), n_ex)
        pairs = pair
        j = 1
        while j < n_ex:
            pairs = jnp.concatenate([pairs, flip(pairs, j, n_ex)])
            j *= 2
        zero = send_core([tie(part, tok, pairs) for part in zero], n_ex)
        feed = send_even(tie(feed, *zero[1:]), n_ex)
        groups = [(0, 2), (2, 6), (6, 8)]

        def gather_group(lo, hi):
            sources = sum([[cots[j], flip(cots[j], 1, n_ex)] for j in range(lo // 2, hi // 2)], [])
            return gather_near(pairs, sources, cap_slots, lo)

        near = [gather_group(*group) for group in groups[:2]]
        attn_zero, params = call(
            functools.partial(assemble_norm_kernel, split), [sds((D, 4 * D), BF), sds((8, D), F32)], pos, *zero,
            scratch=[pltpu.VMEM((D, 128), F32)], pos=True, flops=1_000_000, moved=4 << 20, mib=24,
        )
        fwd = tie(hidden_in, *sum(near, []))
        h1, *saved_zero = attention_forward(fwd, params, tok, attn_zero, 0, False)
        one = send_even(tie(one, h1, *feed[1:]), n_ex)
        feed = send_core([tie(part, h1) for part in feed], n_ex)
        up, down = assemble(split, pos, feed, True)
        h2, *saved_feed = feed_forward(h1, params, up, down)
        one = [tie(part, h2) for part in one]
        cots.append(flip(tie(cotangent, *one[1:]), 6, n_ex))
        one = send_core(one, n_ex)
        attn_one = assemble(split, pos, one, False)[0]
    else:

        def gather_all(shard):
            return lax.all_gather(mine(shard), BOTH, axis=0, tiled=True)

        params = lax.all_gather(norm_params, "dp", axis=0, tiled=True).astype(F32).T
        attn_zero = gather_all(jnp.concatenate([w_qkv[:, 0], w_attn[:, 0]], axis=1))
        up, down = gather_all(w_up), gather_all(w_down)
        attn_one = gather_all(jnp.concatenate([w_qkv[:, 1], w_attn[:, 1]], axis=1))
        h1, *saved_zero = attention_forward(hidden_in, params, tok, attn_zero, 0, False)
        h2, *saved_feed = feed_forward(h1, params, up, down)
        pairs = pair
        j = 1
        while j < n_ex:
            pairs = jnp.concatenate([pairs, flip(pairs, j, n_ex)])
            j *= 2
        groups = [(j, j + 4) for j in range(0, n_ex, 4)]
        cots = [cotangent] + [flip(cotangent, j, n_ex) for j in range(1, n_ex)]
        near = [gather_near(pairs, cots[lo:hi], cap_slots, lo) for lo, hi in groups]
    up_expert = lax.all_gather(expert_up[0], "dp", axis=0, tiled=True)
    down_expert = lax.all_gather(expert_down[0], "dp", axis=0, tiled=True)
    h3, *saved_one, c = attention_forward(h2, params, tok, attn_one, 4, True)
    if wire:
        c = tie(c, cots[-1])
    sent = gather_rows(slot, c, experts)
    if wire:
        near.append(gather_group(*groups[2]))
    sums, held, table = [], (), 0.0
    bufs = {j: exchange(sent[j // 2], j) for j in range(0, groups[-1][0], 2)}
    for n, ((lo, hi), (dout, slot_near)) in enumerate(zip(groups, near)):
        if n == 1:
            for j in range(groups[-1][0], n_ex, 2):
                bufs[j] = exchange(tie(sent[j // 2], *[bufs[i] for i in range(lo, hi, 2)], *sums[:1]), j)
        for j in range(lo, hi, 2):
            bufs[j + 1] = flip(tie(bufs[j], *sums[-1:]), 1, n_ex)
        back, part, held = expert_rows(
            pos, [bufs[j] for j in range(lo, hi)], dout, slot_near, up_expert, down_expert, slots, lo, held
        )
        sums += back
        table = table + part
    out, *held = held
    back = [exchange(pair, 2 * j) for j, pair in enumerate(sums)]
    early_back = len(back) - (groups[-1][1] - groups[-1][0]) // 2
    far = [flip(tie(pair, sums[-1]), 1, n_ex) for pair in back[:early_back]]
    held = [tie(one, *far) for one in held]
    gup_expert, gdown_expert = expert_grads(*held)
    far += [flip(tie(pair, gup_expert), 1, n_ex) for pair in back[early_back:]]
    dbuf_home = sum([list(both) for both in zip(back, far)], [])
    out_home = swap(tie(out, *back, gup_expert).reshape(experts, cap_slots, D), EXPERT).reshape(-1, D)
    gn_one, gn_moe, dx, g_one = first_backward(
        pos, dbuf_home, h3, cotangent, h2, saved_one, params, tok, attn_one, 4, split
    )
    expert_up_sum = lax.psum_scatter(tie(gup_expert, gn_moe), "dp", scatter_dimension=0, tiled=True).astype(F32)
    expert_down_sum = lax.psum_scatter(tie(gdown_expert, gn_moe), "dp", scatter_dimension=0, tiled=True).astype(F32)
    if wire:
        got_one = flip(g_one[1], 1, n_ex)
    gn_feed, dx, g_feed = feed_backward(pos, dx, h1, saved_feed, params, up, down, split)
    if wire:
        got_one = add_core(pos, g_one[0], tie(got_one, gn_feed), True)
        got_feed = flip(tie(g_feed[1], out_home), 1, n_ex)
        sum_feed = add_core(pos, g_feed[0], tie(got_feed, *got_one))
        got_one = send_near(got_one, n_ex)
        dx = tie(dx, sum_feed)
        got_feed = swap(sum_feed, "xy")
    gn_zero, grad_in, g_zero = last_backward(
        pos, dx, hidden_in, saved_zero, params, tok, attn_zero, 0, split, (gn_feed, gn_one, gn_moe, table)
    )
    if wire:
        early = add_near(pos, tie(got_feed, gn_zero), got_one)
        got_zero = flip(tie(g_zero[1], early[0]), 1, n_ex)
        early = send_turn(early, n_dp)
        sum_zero = add_core(pos, g_zero[0], got_zero)
        h3 = tie(h3, sum_zero)
        sum_zero = swap(sum_zero, "xy")
    hidden_out = combine_out(pos, tok, slot, out_home, h3, experts)
    if wire:
        sum_zero = tie(sum_zero, hidden_out)
        early = lax.all_gather(add_turn([tie(one, sum_zero) for one in early]), EXPERT, axis=0)
        sum_zero = add_near(pos, tie(sum_zero, hidden_out, expert_up_sum, expert_down_sum))
        sum_zero = add_turn(send_turn(sum_zero, n_dp))
        last = lax.all_gather(sum_zero, EXPERT, axis=0)
        rows = D // n_dp
        grad_qkv, grad_attn, grad_up, grad_down, gn, sums = call(
            functools.partial(spread_kernel, split),
            [sds((2, rows, 3 * D), F32), sds((2, rows, D), F32), sds((rows, FF), F32), sds((FF // n_dp, D), F32),
             sds((8, rows), F32), sds((experts, 128), F32)],
            pos, last, early,
            pos=True, flops=1_000_000, moved=7 << 20, mib=32,
        )
        grad_qkv, grad_attn, gn = grad_qkv.transpose(1, 0, 2), grad_attn.transpose(1, 0, 2), gn.T
    else:
        small = jnp.concatenate([gn_zero, gn_feed, gn_one, gn_moe], axis=0)
        table = lax.dynamic_update_slice_in_dim(jnp.zeros((experts, 128), F32), table[:1], me, 0)
        small = jnp.concatenate([small, jnp.pad(table, ((0, 0), (0, D - 128)))], axis=0)
        small = lax.psum(small, BOTH)
        gn = lax.dynamic_slice_in_dim(small[:8], here * (D // n_dp), D // n_dp, 1).T
        sums = small[8:]

        def reduce_all(grad):
            rows = grad.shape[0] // (n_dp * n_ex)
            grad = grad.reshape(n_dp, n_ex, rows, -1).transpose(1, 0, 2, 3).reshape(grad.shape)
            part = lax.psum_scatter(grad, EXPERT, scatter_dimension=0, tiled=True)
            part = lax.psum_scatter(part, "dp", scatter_dimension=0, tiled=True)
            return lax.all_gather(part, EXPERT, axis=0, tiled=True).astype(F32)

        g_one, grad_up, grad_down, g_zero = [reduce_all(g) for g in (*g_one, *g_feed, *g_zero)]
        grad_qkv = jnp.stack([g_zero[:, : 3 * D], g_one[:, : 3 * D]], axis=1)
        grad_attn = jnp.stack([g_zero[:, 3 * D :], g_one[:, 3 * D :]], axis=1)
    sums = sums[:, : task_logits.shape[0]].T
    hot = task_experts[:, :, None] == lax.broadcasted_iota(jnp.int32, (1, 1, experts), 2)
    pair_sum = jnp.sum(jnp.where(hot, sums[:, None, :], 0.0), axis=2)
    lean = gates[:, 0] * gates[:, 1] * (pair_sum[:, 0] - pair_sum[:, 1])
    grad_logits = jnp.where(hot[:, 0], lean[:, None], 0.0) - jnp.where(hot[:, 1], lean[:, None], 0.0)
    return (
        hidden_out, grad_in, grad_logits, gn, grad_qkv, grad_attn, grad_up, grad_down,
        expert_up_sum[None], expert_down_sum[None],
    )


def solution(mesh):
    n_dp, n_ex = mesh.shape["dp"], mesh.shape["expert"]
    mesh = jax.sharding.Mesh(mesh.devices.reshape(n_dp, n_ex // 2, 2), BOTH)
    token = P(BOTH, None)
    expert = P(EXPERT, "dp", None)
    in_specs = (
        token, token, token, P(), P(), P(), P("dp", None), P("dp", None, None), P("dp", None, None),
        P("dp", None), P("dp", None), expert, expert, token,
    )
    out_specs = (
        token, token, P(), P("dp", None), P("dp", None, None), P("dp", None, None), P("dp", None), P("dp", None),
        expert, expert,
    )
    step = functools.partial(local, n_dp, n_ex)
    return jax.shard_map(step, mesh=mesh, in_specs=in_specs, out_specs=out_specs, check_vma=False)
```

```python
import functools

import jax
import jax.numpy as jnp
from jax import lax
from jax.experimental import pallas as pl
from jax.experimental.pallas import tpu as pltpu
from jax.sharding import PartitionSpec as P

D = 512
FF = 2048
HEADS = 8
HEAD = D // HEADS
PACK = 1024
MOST_LEN = 64
ROWS = 256
QB = 128
KB = QB + 2 * MOST_LEN
EPS = 1e-05
BLOCKED = -1e30
BF = jnp.bfloat16
F32 = jnp.float32
GELU_C = 0.7978845608028654
GELU_A = 0.044715


COST = 4


def mm(left, right):
    return lax.dot_general(left, right, (((1,), (0,)), ((), ())), preferred_element_type=F32)


def mm_t(left, right):
    return lax.dot_general(left, right, (((1,), (1,)), ((), ())), preferred_element_type=F32)


def t_mm(left, right):
    return lax.dot_general(left, right, (((0,), (0,)), ((), ())), preferred_element_type=F32)


def unit_rows(hidden):
    centered = hidden - jnp.mean(hidden, axis=-1, keepdims=True)
    spread = jnp.mean(centered * centered, axis=-1, keepdims=True)
    scale = lax.rsqrt(spread + EPS)
    return centered * scale, scale


def unit_back(unit, scale, gain, grad):
    inner = grad * gain
    first = jnp.mean(inner, axis=-1, keepdims=True)
    second = jnp.mean(inner * unit, axis=-1, keepdims=True)
    return scale * (inner - first - unit * second)


def gelu_both(z):
    square = z * z
    half = 0.5 + 0.5 * jnp.tanh(z * (GELU_C + GELU_C * GELU_A * square))
    act = z * half
    return act, half + (act - act * half) * (2.0 * GELU_C + 6.0 * GELU_C * GELU_A * square)


def call(kernel, out_shape, *args, grid=None, in_specs=None, out_specs=None, scratch=(), mib=62, flops=0, moved=0,
         alias=None, pos=False):
    extra = {}
    if grid is not None and pos:
        extra["grid_spec"] = pltpu.PrefetchScalarGridSpec(
            num_scalar_prefetch=1, grid=grid, in_specs=in_specs, out_specs=out_specs, scratch_shapes=scratch
        )
    else:
        extra["scratch_shapes"] = scratch
        if grid is not None:
            extra.update(grid=grid, in_specs=in_specs, out_specs=out_specs)
        elif pos:
            held = pl.BlockSpec(memory_space=pltpu.VMEM)
            extra["in_specs"] = [pl.BlockSpec(memory_space=pltpu.SMEM)] + [held] * (len(args) - 1)
    if alias:
        extra["input_output_aliases"] = alias
    return pl.pallas_call(
        kernel,
        out_shape=out_shape,
        compiler_params=pltpu.CompilerParams(vmem_limit_bytes=mib << 20),
        cost_estimate=pl.CostEstimate(flops=flops // COST, bytes_accessed=moved // COST, transcendentals=0),
        **extra,
    )(*args)


def sds(shape, dtype):
    return jax.ShapeDtypeStruct(shape, dtype)


WIRE = 512


def piece_rows(split):
    dp, ex = split
    return D // (dp * ex)


def wired(split):
    dp, ex = split
    return piece_rows(split) % 16 == 0 and ex == 8


def near(split, pos_ref, j, k):
    return k * split[1] + jnp.bitwise_xor(pos_ref[0], j)


def send_rows(split, pos_ref, scr_ref, own_ref, core_ref, at, rows):
    dp, ex = split
    for j in range(ex):
        out = core_ref if j % 2 else own_ref
        for k in range(dp):
            start = pl.multiple_of(near(split, pos_ref, j, k) * rows, rows)
            out[j // 2, k, at : at + rows, :] = scr_ref[pl.ds(start, rows), :]


def wire_shapes(split, blocks):
    dp, ex = split
    shape = (ex // 2, dp, blocks * piece_rows(split), WIRE)
    return [sds(shape, BF), sds(shape, BF)]


WINDOW = 12 << 20


class Stage:
    def __init__(self, ins, outs, split_in, split_out, hold_in, hold_out, sem_in, sem_out, order, axes):
        self.ins, self.outs = hold_in, hold_out
        self.split_in, self.split_out, self.axes = split_in, split_out, axes
        self.out_hbm, self.out_sem, self.sent = outs, sem_out, []
        self.got, self.begun, self.copies, self.bytes = set(), 0, {}, {}
        order = order or [(i, r) for i, parts in enumerate(split_in) for r in range(parts)]
        for n, (i, r) in enumerate(order):
            rows = self.rows(hold_in[i], split_in[i], r)
            self.copies[i, r] = pltpu.make_async_copy(ins[i].at[rows], hold_in[i].at[rows], sem_in.at[n])
            self.bytes[i, r] = hold_in[i].size * hold_in[i].dtype.itemsize // split_in[i]
        self.order = order
        self.ahead(0)

    def rows(self, ref, parts, r, axis=0):
        size = ref.shape[axis] // parts
        return (slice(None),) * axis + (pl.ds(r * size, size),)

    def ahead(self, least):
        while self.begun < len(self.order):
            flying = sum(self.bytes[key] for key in self.order[: self.begun] if key not in self.got)
            if self.begun >= least and flying >= WINDOW:
                break
            self.copies[self.order[self.begun]].start()
            self.begun += 1

    def need(self, *which):
        for i in which:
            i, r = i if isinstance(i, tuple) else (i, None)
            for k in range(self.split_in[i]) if r is None else [r]:
                if (i, k) not in self.got:
                    self.ahead(self.order.index((i, k)) + 1)
                    self.copies[i, k].wait()
                    self.got.add((i, k))
                    self.ahead(0)

    def done(self, i, r=None):
        parts = self.split_out[i]
        for k in range(parts) if r is None else [r]:
            rows = self.rows(self.outs[i], parts, k, self.axes[i])
            sem = self.out_sem.at[sum(self.split_out[:i]) + k]
            copy = pltpu.make_async_copy(self.outs[i].at[rows], self.out_hbm[i].at[rows], sem)
            copy.start()
            self.sent.append(copy)

    def finish(self):
        self.need(*self.order)
        for copy in self.sent:
            copy.wait()


def staged(body, outs, ins, small=(), small_outs=(), scratch=(), flops=0, moved=0, order=None, mib=62):
    arrays, split_in = [x for x, _ in ins], [n for _, n in ins]
    shapes, split_out = [x[0] for x in outs], [x[1] for x in outs]
    axes = [x[2] if len(x) > 2 else 0 for x in outs]

    def kernel(*refs):
        at = 0
        groups = []
        for n in (len(small), len(arrays), len(small_outs), len(shapes), len(arrays), len(shapes), len(scratch), 2):
            groups.append(refs[at : at + n])
            at += n
        few, hbm_in, few_out, hbm_out, hold_in, hold_out, own, (sem_in, sem_out) = groups
        stage = Stage(hbm_in, hbm_out, split_in, split_out, hold_in, hold_out, sem_in, sem_out, order, axes)
        body(stage, few, few_out, own)
        stage.finish()

    space = [pl.BlockSpec(memory_space=pltpu.SMEM if x.dtype == jnp.int32 else pltpu.VMEM) for x in small]
    got = pl.pallas_call(
        kernel,
        out_shape=list(small_outs) + shapes,
        in_specs=space + [pl.BlockSpec(memory_space=pl.ANY)] * len(arrays),
        out_specs=[pl.BlockSpec(memory_space=pltpu.VMEM)] * len(small_outs)
        + [pl.BlockSpec(memory_space=pl.ANY)] * len(shapes),
        scratch_shapes=[pltpu.VMEM(x.shape, x.dtype) for x in arrays + shapes]
        + list(scratch)
        + [pltpu.SemaphoreType.DMA((sum(split_in),)), pltpu.SemaphoreType.DMA((max(sum(split_out), 1),))],
        compiler_params=pltpu.CompilerParams(vmem_limit_bytes=mib << 20),
        cost_estimate=pl.CostEstimate(flops=flops // COST, bytes_accessed=moved // COST, transcendentals=0),
    )(*small, *arrays)
    return list(got)


def route_kernel(slots, sent_ref, pair_ref, tok_ref, slot_ref):
    t = lax.broadcasted_iota(jnp.int32, (PACK, 128), 0).astype(F32)
    start, end = sent_ref[0:1, :], sent_ref[1:2, :]
    member = (t >= start) & (t < end)

    def pick(value):
        return jnp.sum(jnp.where(member, value, 0.0), axis=1, keepdims=True)

    lane = lax.broadcasted_iota(jnp.int32, (PACK, 8), 1)
    out = jnp.where(lane == 0, pick(start), 0.0)
    out = jnp.where(lane == 1, pick(end), out)
    for k in range(2):
        base = sent_ref[2 + k : 3 + k, :]
        slot = pick(jnp.where(base >= 0, base - start + t + 1.0, 0.0)) - 1.0
        out = jnp.where(lane == 2 + k, slot, out)
    tok_ref[...] = out
    chunk = 512
    base, length, first = pair_ref[0:1, :], pair_ref[1:2, :], pair_ref[2:3, :]
    gate, task = pair_ref[3:4, :], pair_ref[4:5, :]
    for i in range(slots // chunk):
        s = lax.broadcasted_iota(jnp.int32, (chunk, 128), 0).astype(F32) + float(i * chunk)
        held = (base >= 0) & (s >= base) & (s < base + length)

        def take(value, held=held):
            return jnp.sum(jnp.where(held, value, 0.0), axis=1, keepdims=True)

        lane = lax.broadcasted_iota(jnp.int32, (chunk, 8), 1)
        out = jnp.where(lane == 0, take(first - base + s + 1.0) - 1.0, 0.0)
        out = jnp.where(lane == 1, take(gate), out)
        out = jnp.where(lane == 2, take(task + 1.0) - 1.0, out)
        slot_ref[i * chunk : (i + 1) * chunk, :] = out


def head_halves(block):
    low = lax.broadcasted_iota(jnp.int32, (1, 128), 1) < HEAD
    zero = jnp.zeros_like(block)
    return jnp.concatenate([jnp.where(low, block, zero), jnp.where(low, zero, block)], axis=0)


def merge_halves(stacked):
    low = lax.broadcasted_iota(jnp.int32, (1, 128), 1) < HEAD
    return jnp.where(low, stacked[:QB], stacked[QB:])


def key_start(i):
    return jnp.clip(i * QB - MOST_LEN, 0, PACK - KB)


def attention_kernel(norm_at, last, x_ref, np_ref, tok_ref, w_ref, *refs):
    if last:
        h_ref, a_ref, qkv_ref, ctx_ref, c_ref = refs
    else:
        h_ref, a_ref, qkv_ref, ctx_ref = refs
    gain, shift = np_ref[norm_at : norm_at + 1, :], np_ref[norm_at + 1 : norm_at + 2, :]
    for r in range(PACK // ROWS):
        rows = slice(r * ROWS, (r + 1) * ROWS)
        unit, _ = unit_rows(x_ref[rows, :].astype(F32))
        a = (unit * gain + shift).astype(BF)
        a_ref[rows, :] = a
        qkv_ref[rows, :] = mm(a, w_ref[:, 0 : 3 * D]).astype(BF)

    def block(i, carry):
        q0 = pl.multiple_of(i * QB, QB)
        k0 = pl.multiple_of(key_start(i), MOST_LEN)
        start, end = tok_ref[pl.ds(q0, QB), 0:1], tok_ref[pl.ds(q0, QB), 1:2]
        key = (lax.broadcasted_iota(jnp.int32, (QB, KB), 1) + k0).astype(F32)
        mask = (key >= start) & (key < end)
        mask = jnp.concatenate([mask, mask], axis=0)
        at = [pair * 128 for pair in range(HEADS // 2)]
        q = [head_halves(qkv_ref[pl.ds(q0, QB), a : a + 128] * BF(HEAD**-0.5)) for a in at]
        k = [qkv_ref[pl.ds(k0, KB), D + a : D + a + 128] for a in at]
        v = [qkv_ref[pl.ds(k0, KB), 2 * D + a : 2 * D + a + 128] for a in at]
        scores = [jnp.where(mask, mm_t(x, y), BLOCKED) for x, y in zip(q, k)]
        raised = [jnp.exp(x - jnp.max(x, axis=1, keepdims=True)) for x in scores]
        probs = [(x * (1.0 / jnp.sum(x, axis=1, keepdims=True))).astype(BF) for x in raised]
        ctx = [merge_halves(mm(x, y)).astype(BF) for x, y in zip(probs, v)]
        ctx_ref[pl.ds(q0, QB), :] = jnp.concatenate(ctx, axis=1)
        return carry

    lax.fori_loop(0, PACK // QB, block, 0, unroll=4)
    for r in range(PACK // ROWS):
        rows = slice(r * ROWS, (r + 1) * ROWS)
        h = x_ref[rows, :].astype(F32) + mm(ctx_ref[rows, :], w_ref[:, 3 * D : 4 * D])
        h_ref[rows, :] = h
        if last:
            unit, _ = unit_rows(h)
            c_ref[rows, :] = (unit * np_ref[6:7, :] + np_ref[7:8, :]).astype(BF)


def attention_forward(hidden, params, tok, weights, norm_at, last):
    outs = [sds((PACK, D), F32), sds((PACK, D), BF), sds((PACK, 3 * D), BF), sds((PACK, D), BF)]
    if last:
        outs.append(sds((PACK, D), BF))
    return call(
        functools.partial(attention_kernel, norm_at, last),
        outs, hidden, params, tok, weights,
        flops=6_000_000_000, moved=12 << 20, mib=40,
    )


def combine_grads(io, tok_ref, h_ref, cot_ref, blocks, np_ref, dx_ref, gn_ref, needs):
    for e, ref in enumerate(blocks):
        size = ref.shape[0] // 2
        io.need((needs[2 + e], e % 2))
        part = mm(slots_hot(tok_ref, size, e), ref[e % 2 * size : (e % 2 + 1) * size, :])
        dx_ref[...] = part if e == 0 else dx_ref[...] + part
    io.need(*needs[:2])
    dgain, dshift = jnp.zeros((1, D), F32), jnp.zeros((1, D), F32)
    for r in range(PACK // ROWS):
        rows = slice(r * ROWS, (r + 1) * ROWS)
        dnorm = dx_ref[rows, :]
        unit, scale = unit_rows(h_ref[rows, :])
        dgain += jnp.sum(dnorm * unit, axis=0, keepdims=True)
        dshift += jnp.sum(dnorm, axis=0, keepdims=True)
        dx_ref[rows, :] = cot_ref[rows, :].astype(F32) + unit_back(unit, scale, np_ref[6:7, :], dnorm)
    gn_ref[0:1, :] = dgain
    gn_ref[1:2, :] = dshift


def attention_core_back(io, dx_ref, dx_at, w_ref, w_at, tok_ref, qkv_ref, at_need, dctx_ref, dqkv_ref, acc_ref):
    io.need(w_at)
    for r in range(PACK // ROWS):
        rows = slice(r * ROWS, (r + 1) * ROWS)
        if dx_at is not None:
            io.need((dx_at, r))
        dctx_ref[rows, :] = mm_t(dx_ref[rows, :].astype(BF), w_ref[:, 3 * D : 4 * D]).astype(BF)
    acc_ref[...] = jnp.zeros_like(acc_ref)
    io.need(*at_need)

    def block(i, carry):
        q0 = pl.multiple_of(i * QB, QB)
        k0 = pl.multiple_of(key_start(i), MOST_LEN)
        start, end = tok_ref[pl.ds(k0, KB), 0:1], tok_ref[pl.ds(k0, KB), 1:2]
        query = (lax.broadcasted_iota(jnp.int32, (KB, QB), 1) + q0).astype(F32)
        mask = (query >= start) & (query < end)
        mask = jnp.concatenate([mask, mask], axis=1)
        at = [pair * 128 for pair in range(HEADS // 2)]
        q = [head_halves(qkv_ref[pl.ds(q0, QB), a : a + 128] * BF(HEAD**-0.5)) for a in at]
        k = [qkv_ref[pl.ds(k0, KB), D + a : D + a + 128] for a in at]
        v = [qkv_ref[pl.ds(k0, KB), 2 * D + a : 2 * D + a + 128] for a in at]
        g = [head_halves(dctx_ref[pl.ds(q0, QB), a : a + 128]) for a in at]
        scores = [jnp.where(mask, mm_t(x, y), BLOCKED) for x, y in zip(k, q)]
        dprobs = [mm_t(x, y) for x, y in zip(v, g)]
        raised = [jnp.exp(x - jnp.max(x, axis=0, keepdims=True)) for x in scores]
        probs = [x * (1.0 / jnp.sum(x, axis=0, keepdims=True)) for x in raised]
        delta = [jnp.sum(x * y, axis=0, keepdims=True) for x, y in zip(probs, dprobs)]
        dscores = [(x * (y - z)).astype(BF) for x, y, z in zip(probs, dprobs, delta)]
        dq = [(merge_halves(t_mm(x, y)) * (HEAD**-0.5)).astype(BF) for x, y in zip(dscores, k)]
        dk = [mm(x, y) for x, y in zip(dscores, q)]
        dv = [mm(x.astype(BF), y) for x, y in zip(probs, g)]
        dqkv_ref[pl.ds(q0, QB), 0:D] = jnp.concatenate(dq, axis=1)
        acc_ref[pl.ds(k0, KB), :] += jnp.concatenate(dk + dv, axis=1)
        return carry

    lax.fori_loop(0, PACK // QB, block, 0, unroll=2)
    dqkv_ref[:, D:] = acc_ref[...].astype(BF)


def wire_outs(split, blocks):
    return [(x, blocks, 2) for x in wire_shapes(split, blocks)]


def attention_weight_back(io, split, pos_ref, a_ref, ctx_ref, dx_ref, dqkv_ref, grads, scr_ref):
    rows = piece_rows(split)
    for c in range(4):
        cols = slice(c * D, (c + 1) * D)
        if c < 3:
            grad = t_mm(a_ref[...], dqkv_ref[:, cols]).astype(BF)
        else:
            grad = t_mm(ctx_ref[...], dx_ref[...].astype(BF)).astype(BF)
        if wired(split):
            scr_ref[...] = grad
            send_rows(split, pos_ref, scr_ref, grads[0], grads[1], c * rows, rows)
            io.done(1, c)
            io.done(2, c)
        else:
            grads[0][:, cols] = grad


def first_back_kernel(split, norm_at, io, few, few_out, own):
    pos_ref, np_ref = few
    tok_ref, h_ref, cot_ref, w_ref, qkv_ref, a_ref, ctx_ref, x_ref = io.ins[:8]
    dx_ref, dctx_ref, dqkv_ref, acc_ref, scr_ref = own
    blocks = io.ins[8:]
    io.need(0)
    combine_grads(io, tok_ref, h_ref, cot_ref, blocks, np_ref, dx_ref, few_out[1], [1, 2] + list(range(8, 8 + len(blocks))))
    attention_core_back(io, dx_ref, None, w_ref, 3, tok_ref, qkv_ref, [4], dctx_ref, dqkv_ref, acc_ref)
    io.need(5, 6, 7)
    attention_weight_back(io, split, pos_ref, a_ref, ctx_ref, dx_ref, dqkv_ref, io.outs[1:], scr_ref)
    if not wired(split):
        io.done(1)
    norm_back_rows(norm_at, dx_ref, x_ref, dqkv_ref, np_ref, w_ref, io.outs[0], few_out[0], io)


def first_backward(pos, blocks, h, cotangent, hidden, saved, params, tok, weights, norm_at, split):
    a, qkv, ctx = saved
    grads = wire_outs(split, 4) if wired(split) else [(sds((D, 4 * D), BF), 1)]
    ins = [(x, 1) for x in (tok, h, cotangent, weights, qkv, a, ctx, hidden)] + [(x, 2) for x in blocks]
    order = [(0, 0)] + [(8 + n, n % 2) for n in range(len(blocks))] + [(n, 0) for n in range(1, 8)]
    norm, norm_moe, out, *grads = staged(
        functools.partial(first_back_kernel, split, norm_at),
        [(sds((PACK, D), F32), 4)] + grads, ins, [pos, params], [sds((2, D), F32)] * 2,
        [pltpu.VMEM((PACK, D), F32), pltpu.VMEM((PACK, D), BF), pltpu.VMEM((PACK, 3 * D), BF),
         pltpu.VMEM((PACK, 2 * D), F32), pltpu.VMEM((D, D), BF)],
        flops=16_000_000_000, moved=20 << 20, order=order,
    )
    return norm, norm_moe, out, grads


def last_back_kernel(split, norm_at, io, few, few_out, own):
    pos_ref, np_ref, more = few[0], few[1], few[2:]
    dx_ref, w_ref, tok_ref, qkv_ref, a_ref, ctx_ref, x_ref = io.ins
    gn_ref, grads = few_out[0], io.outs[1:]
    dctx_ref, dqkv_ref, acc_ref, scr_ref, row_ref = own
    attention_core_back(io, dx_ref, 0, w_ref, 1, tok_ref, qkv_ref, [2, 3], dctx_ref, dqkv_ref, acc_ref)
    io.need(4, 5, 6)
    attention_weight_back(io, split, pos_ref, a_ref, ctx_ref, dx_ref, dqkv_ref, grads, scr_ref)
    norm_back_rows(norm_at, dx_ref, x_ref, dqkv_ref, np_ref, w_ref, io.outs[0], gn_ref, io)
    if wired(split):
        dp, ex = split
        rows, wide = piece_rows(split), D // dp
        for n, ref in enumerate((gn_ref,) + tuple(more[:-1])):
            for i in range(2):
                for d in range(dp):
                    row_ref[(2 * n + i) * dp + d : (2 * n + i) * dp + d + 1, :] = ref[i : i + 1, d * wide : (d + 1) * wide]
        first = lax.broadcasted_iota(jnp.int32, (16, WIRE), 0) == 0
        for j in range(ex):
            for k in range(dp):
                at = jnp.bitwise_xor(pos_ref[0], j) * dp + k
                table = jnp.zeros((1, 128), F32) if j else more[-1][0:1, :]
                row = jnp.concatenate(
                    [row_ref[pl.ds(at, 1), :], table, jnp.zeros((1, WIRE - wide - 128), F32)], axis=1
                )
                grads[j % 2][j // 2, k, 4 * rows : 4 * rows + 16, :] = jnp.where(first, row, 0.0).astype(BF)
    if wired(split):
        io.done(1, 4)
        io.done(2, 4)
    else:
        io.done(1)


def last_backward(pos, dx, hidden, saved, params, tok, weights, norm_at, split, more):
    a, qkv, ctx = saved
    grads = wire_outs(split, 5) if wired(split) else [(sds((D, 4 * D), BF), 1)]
    norm, out, *grads = staged(
        functools.partial(last_back_kernel, split, norm_at),
        [(sds((PACK, D), F32), 4)] + grads,
        [(dx, 4), (weights, 1), (tok, 1), (qkv, 1), (a, 1), (ctx, 1), (hidden, 1)], [pos, params, *more],
        [sds((2, D), F32)],
        [pltpu.VMEM((PACK, D), BF), pltpu.VMEM((PACK, 3 * D), BF), pltpu.VMEM((PACK, 2 * D), F32),
         pltpu.VMEM((D, D), BF), pltpu.VMEM((8 * split[0], D // split[0]), F32)],
        flops=14_000_000_000, moved=16 << 20,
        order=[(0, 0), (1, 0), (0, 1), (0, 2), (0, 3), (2, 0), (3, 0), (4, 0), (5, 0), (6, 0)],
    )
    return norm, out, grads


def feed_kernel(io, few, few_out, own):
    (np_ref,) = few
    x_ref, up_ref, down_ref = io.ins
    h_ref, n_ref, act_ref, slope_ref = io.outs
    gain, shift = np_ref[2:3, :], np_ref[3:4, :]
    for r in range(PACK // ROWS):
        rows = slice(r * ROWS, (r + 1) * ROWS)
        io.need((0, r))
        x = x_ref[rows, :]
        unit, _ = unit_rows(x)
        n = (unit * gain + shift).astype(BF)
        n_ref[rows, :] = n
        io.need(1)
        act, slope = gelu_both(mm(n, up_ref[...]))
        act = act.astype(BF)
        act_ref[rows, :] = act
        slope_ref[rows, :] = slope.astype(BF)
        io.need(2)
        h_ref[rows, :] = x + mm(act, down_ref[...])
        for i in range(4):
            io.done(i, r)


def feed_forward(hidden, params, up, down):
    return staged(
        feed_kernel,
        [(sds((PACK, D), F32), 4), (sds((PACK, D), BF), 4), (sds((PACK, FF), BF), 4), (sds((PACK, FF), BF), 4)],
        [(hidden, 4), (up, 1), (down, 1)], [params], flops=4_300_000_000, moved=17 << 20, mib=36,
        order=[(0, 0), (1, 0), (2, 0), (0, 1), (0, 2), (0, 3)],
    )


def feed_back_kernel(split, io, few, few_out, own):
    wire = wired(split)
    pos_ref, np_ref = few
    dx_ref, down_ref, slope_ref, n_ref, act_ref, up_ref, x_ref = io.ins
    out_ref, grads = io.outs[0], io.outs[1:]
    dz_ref, dy_ref, scr_ref, tall_ref = own
    for r in range(PACK // ROWS):
        rows = slice(r * ROWS, (r + 1) * ROWS)
        io.need((0, r), 1, (2, r))
        dy = dx_ref[rows, :].astype(BF)
        dy_ref[rows, :] = dy
        dz_ref[rows, :] = (mm_t(dy, down_ref[...]) * slope_ref[rows, :].astype(F32)).astype(BF)
    io.need(3, 4)
    if wire:
        rows = piece_rows(split)
        for c in range(FF // D):
            scr_ref[...] = t_mm(n_ref[...], dz_ref[:, c * D : (c + 1) * D]).astype(BF)
            send_rows(split, pos_ref, scr_ref, *grads, c * rows, rows)
            io.done(1, c)
            io.done(2, c)
        for c in range(FF // D):
            tall_ref[c * D : (c + 1) * D, :] = t_mm(act_ref[:, c * D : (c + 1) * D], dy_ref[...]).astype(BF)
        send_rows(split, pos_ref, tall_ref, *grads, FF // D * rows, FF // D * rows)
        for c in range(FF // D):
            io.done(1, FF // D + c)
            io.done(2, FF // D + c)
    else:
        grads[0][...] = t_mm(n_ref[...], dz_ref[...]).astype(BF)
        grads[1][...] = t_mm(act_ref[...], dy_ref[...]).astype(BF)
        io.done(1)
        io.done(2)
    io.need(5, 6)
    norm_back_rows(2, dx_ref, x_ref, dz_ref, np_ref, up_ref, out_ref, few_out[0], io)


def feed_backward(pos, dx, hidden, saved, params, up, down, split):
    n, act, slope = saved
    grads = wire_outs(split, 8) if wired(split) else [(sds((D, FF), BF), 1), (sds((FF, D), BF), 1)]
    norm, out, *grads = staged(
        functools.partial(feed_back_kernel, split),
        [(sds((PACK, D), F32), 4)] + grads,
        [(dx, 4), (down, 1), (slope, 4), (n, 1), (act, 1), (up, 1), (hidden, 1)], [pos, params], [sds((2, D), F32)],
        scratch=[pltpu.VMEM((PACK, FF), BF), pltpu.VMEM((PACK, D), BF), pltpu.VMEM((D, D), BF), pltpu.VMEM((FF, D), BF)],
        order=[(0, 0), (1, 0), (2, 0)] + [(i, r) for r in range(1, 4) for i in (0, 2)] + [(n, 0) for n in range(3, 7)],
        flops=8_600_000_000, moved=24 << 20,
    )
    return norm, out, grads


def norm_back_rows(norm_at, dx_ref, x_ref, grad_ref, np_ref, w_ref, out_ref, gn_ref, io, needs=()):
    gain = np_ref[norm_at : norm_at + 1, :]
    dgain, dshift = jnp.zeros((1, D), F32), jnp.zeros((1, D), F32)
    for r in range(PACK // ROWS):
        rows = slice(r * ROWS, (r + 1) * ROWS)
        for i in needs:
            io.need((i, r))
        dnorm = mm_t(grad_ref[rows, :], w_ref[:, : grad_ref.shape[1]])
        unit, scale = unit_rows(x_ref[rows, :].astype(F32))
        dgain += jnp.sum(dnorm * unit, axis=0, keepdims=True)
        dshift += jnp.sum(dnorm, axis=0, keepdims=True)
        out_ref[rows, :] = dx_ref[rows, :] + unit_back(unit, scale, gain, dnorm)
        io.done(0, r)
    gn_ref[0:1, :] = dgain
    gn_ref[1:2, :] = dshift


def assemble_kernel(split, blocks, tall, *refs):
    dp, ex = split
    rows = piece_rows(split)
    pos_ref, pieces, outs = refs[0], refs[1 : 1 + ex], refs[1 + ex :]
    for j in range(ex):
        for k in range(dp):
            at = lax.rem(pos_ref[1] + dp - k, dp) * ex + jnp.bitwise_xor(pos_ref[0], j)
            start = pl.multiple_of(at * rows, rows)
            for c in range(blocks):
                outs[0][pl.ds(start, rows), c * WIRE : (c + 1) * WIRE] = pieces[j][k, c * rows : (c + 1) * rows, :]
            if tall:
                high = blocks * rows
                start = pl.multiple_of(at * high, high)
                outs[1][pl.ds(start, high), :] = pieces[j][k, high : 2 * high, :]


def assemble(split, pos, pieces, tall):
    outs = [sds((D, 4 * D), BF)] + ([sds((FF, D), BF)] if tall else [])
    return call(
        functools.partial(assemble_kernel, split, 4, tall), outs, pos, *pieces,
        pos=True, flops=1_000_000, moved=4 << 20, mib=24,
    )


def assemble_norm_kernel(split, *refs):
    dp, ex = split
    rows = piece_rows(split)
    pos_ref, pieces, (w_ref, np_ref, scr_ref) = refs[0], refs[1 : 1 + ex], refs[1 + ex :]
    for j in range(ex):
        for k in range(dp):
            at = lax.rem(pos_ref[1] + dp - k, dp) * ex + jnp.bitwise_xor(pos_ref[0], j)
            start = pl.multiple_of(at * rows, rows)
            for c in range(4):
                w_ref[pl.ds(start, rows), c * WIRE : (c + 1) * WIRE] = pieces[j][k, c * rows : (c + 1) * rows, :]
            scr_ref[pl.ds(start, rows), :] = pieces[j][k, 4 * rows : 5 * rows, 0:128].astype(F32)
    np_ref[...] = jnp.transpose(scr_ref[...])[:8]


def add_core_kernel(near, io, few, few_out, own):
    mine_ref, got_ref = io.ins
    for j in range(mine_ref.shape[0]):
        io.need((0, j), (1, j))
        total = (mine_ref[j].astype(F32) + got_ref[j].astype(F32)).astype(BF)
        if near:
            io.outs[j][...] = total
            io.done(j)
        else:
            io.outs[0][jnp.bitwise_xor(few[0][0] // 2, j)] = total
    if not near:
        io.done(0)


def add_near_kernel(lists, pos_ref, *refs):
    ins, outs = refs[: sum(lists)], refs[sum(lists) :]
    dp = len(outs)
    for k, out in enumerate(outs):
        at = lax.rem(pos_ref[1] + k, dp)
        first, top = 0, 0
        for n in lists:
            parts = ins[first : first + n]
            first += n
            parts = [parts[0].at[i] for i in range(parts[0].shape[0])] if n == 1 else parts
            total = parts[0][at].astype(F32)
            for part in parts[1:]:
                total = total + part[at].astype(F32)
            out[top : top + total.shape[0], :] = total.astype(BF)
            top += total.shape[0]


def add_turn_kernel(*refs):
    total = refs[0][...].astype(F32)
    for ref in refs[1:-1]:
        total = total + ref[...].astype(F32)
    refs[-1][...] = total.astype(BF)


def spread_kernel(split, *refs):
    dp, ex = split
    rows = piece_rows(split)
    pos_ref, last_ref, early_ref, qkv_ref, attn_ref, up_ref, down_ref, gn_ref, table_ref = refs

    def put(n, start, piece):
        for c in range(3):
            qkv_ref[n, pl.ds(start, rows), c * D : (c + 1) * D] = piece[c * rows : (c + 1) * rows]
        attn_ref[n, pl.ds(start, rows), :] = piece[3 * rows : 4 * rows]

    for j in range(ex):
        start, high = j * rows, j * 4 * rows
        piece = early_ref[j].astype(F32)
        for c in range(4):
            up_ref[pl.ds(start, rows), c * D : (c + 1) * D] = piece[c * rows : (c + 1) * rows]
        down_ref[pl.ds(high, 4 * rows), :] = piece[4 * rows : 8 * rows]
        put(1, start, piece[8 * rows :])
        piece = last_ref[j].astype(F32)
        put(0, j * rows, piece)
        gn_ref[j : j + 1, :] = piece[4 * rows : 4 * rows + 1, 0 : D // dp]
        table_ref[j : j + 1, :] = piece[4 * rows : 4 * rows + 1, D // dp : D // dp + 128]


def gather_kernel(io, few, few_out, own):
    src_ref, slot_ref = io.ins
    pairs = len(io.outs)
    size = io.outs[0].shape[0] // 2
    tokens = lax.broadcasted_iota(jnp.int32, (size, PACK), 1).astype(F32)
    io.need(0)
    for n in range(2 * pairs):
        io.need((1, n))
        hot = jnp.where(slot_ref[n * size : (n + 1) * size, 0:1] == tokens, 1.0, 0.0).astype(BF)
        io.outs[n // 2][n % 2 * size : (n % 2 + 1) * size, :] = mm(hot, src_ref[...]).astype(BF)
        io.done(n // 2, n % 2)


def gather_rows(slot, source, experts):
    size = slot.shape[0] // experts
    return staged(
        gather_kernel, [(sds((2 * size, D), BF), 2)] * (experts // 2), [(source, 1), (slot, experts)],
        flops=2 * slot.shape[0] * PACK * D, moved=6 << 20, mib=24,
    )


def gather_near_kernel(at, io, few, few_out, own):
    (pair_ref,) = few
    size = io.outs[0].shape[0] // len(io.ins)
    tokens = lax.broadcasted_iota(jnp.int32, (size, PACK), 1).astype(F32)
    lane = lax.broadcasted_iota(jnp.int32, (size, 8), 1)
    for n, source in enumerate(io.ins):
        one = 8 * (at + n)
        base, length, first, gate, task = [pair_ref[one + i : one + i + 1, :] for i in range(5)]
        s = lax.broadcasted_iota(jnp.int32, (size, 128), 0).astype(F32) + float((at + n) * size)
        held = (base >= 0) & (s >= base) & (s < base + length)

        def take(value, held=held):
            return jnp.sum(jnp.where(held, value, 0.0), axis=1, keepdims=True)

        gate, task = take(gate), take(task + 1.0) - 1.0
        hot = jnp.where(take(first - base + s + 1.0) - 1.0 == tokens, 1.0, 0.0).astype(BF)
        io.need(n)
        rows = slice(n * size, (n + 1) * size)
        io.outs[0][rows, :] = (mm(hot, source[...]) * gate).astype(BF)
        io.outs[1][rows, :] = jnp.where(lane == 0, gate, jnp.where(lane == 1, task, 0.0))
        io.done(0, n)
        io.done(1, n)


def gather_near(pairs, sources, size, at):
    count = len(sources)
    return staged(
        functools.partial(gather_near_kernel, at),
        [(sds((count * size, D), BF), count), (sds((count * size, 8), F32), count)], [(x, 1) for x in sources], [pairs],
        flops=2 * count * size * PACK * D, moved=4 << 20, mib=20,
    )


def slots_hot(tok_ref, size, n):
    at = lax.broadcasted_iota(jnp.int32, (PACK, size), 1).astype(F32) + float(n * size)
    return jnp.where((tok_ref[:, 2:3] == at) | (tok_ref[:, 3:4] == at), 1.0, 0.0).astype(BF)


def whole(shape):
    return pl.BlockSpec(shape, lambda e: (0,) * len(shape))


def combine_out_kernel(experts, io, few, few_out, own):
    pos_ref = few[0]
    tok_ref, slot_ref, rows_ref, h_ref = io.ins
    acc_ref, size = own[0], rows_ref.shape[0] // experts
    io.need(0, 1, 2)
    for e in range(experts):
        start = pl.multiple_of(jnp.bitwise_xor(pos_ref[0], e) * size, size)
        rows = rows_ref[pl.ds(start, size), :].astype(F32)
        part = mm(slots_hot(tok_ref, size, e), (rows * slot_ref[e * size : (e + 1) * size, 1:2]).astype(BF))
        acc_ref[...] = part if e == 0 else acc_ref[...] + part
    for r in range(PACK // ROWS):
        rows = slice(r * ROWS, (r + 1) * ROWS)
        io.need((3, r))
        io.outs[0][rows, :] = (h_ref[rows, :] + acc_ref[rows, :]).astype(BF)
        io.done(0, r)


def combine_out(pos, tok, slot, rows, hidden, experts):
    return staged(
        functools.partial(combine_out_kernel, experts), [(sds((PACK, D), BF), 4)],
        [(tok, 1), (slot, 1), (rows, 1), (hidden, 4)], [pos], scratch=[pltpu.VMEM((PACK, D), F32)],
        flops=2 * 4096 * PACK * D, moved=14 << 20,
    )[0]


def expert_kernel(count, steps, *refs):
    bufs = refs[1 : 1 + count]
    dout_in, slot_ref, up_ref, down_ref = refs[1 + count : 5 + count]
    dbufs = refs[-count // 2 - 6 : -6]
    table_ref, out_ref, act_ref, du_ref, buf_ref, dout_ref = refs[-6:]
    i = pl.program_id(0)

    @pl.when(i == 0)
    def _():
        table_ref[...] = jnp.zeros_like(table_ref)

    def work(n):
        buf, dout = bufs[n][...], dout_in[...]
        buf_ref[...] = buf
        dout_ref[...] = dout
        z, dact = mm(buf, up_ref[...]), mm_t(dout, down_ref[...])
        act, slope = gelu_both(z)
        act = act.astype(BF)
        act_ref[...] = act
        out = mm(act, down_ref[...]).astype(BF)
        du = (dact * slope).astype(BF)
        du_ref[...] = du
        dbufs[n // 2][...] = mm_t(du, up_ref[...]).astype(BF)
        out_ref[...] = out
        gate, task = slot_ref[:, 0:1], slot_ref[:, 1:2]
        dgate = jnp.sum(out.astype(F32) * dout.astype(F32), axis=1, keepdims=True)
        dgate = jnp.where(task >= 0, dgate / jnp.where(task >= 0, gate, 1.0), 0.0)
        tasks = lax.broadcasted_iota(jnp.int32, (buf.shape[0], 128), 1).astype(F32)
        table_ref[0:1, :] += jnp.sum(jnp.where(tasks == task, dgate, 0.0), axis=0, keepdims=True)

    for n in range(count):
        pl.when(i // steps == n)(functools.partial(work, n))


def expert_rows(pos, bufs, dout, slot, up, down, total, at, held):
    rows = bufs[0].shape[0] // 2
    count = len(bufs)
    size = min(256, rows)
    steps = rows // size
    blocks = [
        pl.BlockSpec((size, D), lambda i, p, n=n: (jnp.clip(i - n * steps, 0, steps - 1) + n % 2 * steps, 0))
        for n in range(count)
    ]
    pairs = [
        pl.BlockSpec((size, D), lambda i, p, n=n: (jnp.clip(i - 2 * n * steps, 0, 2 * steps - 1), 0))
        for n in range(count // 2)
    ]

    def there(i, p):
        return (jnp.bitwise_xor(p[0], at + i // steps) * steps + lax.rem(i, steps), 0)

    def fixed(shape):
        return pl.BlockSpec(shape, lambda i, p: (0, 0), pipeline_mode=pl.Buffered(1))

    first = at * steps

    def tile(cols, first=first):
        return pl.BlockSpec((size, cols), lambda i, p: (i + first, 0))

    alias = {count + 5 + n: count // 2 + 1 + n for n in range(5)} if held else None
    outs = call(
        functools.partial(expert_kernel, count, steps),
        [sds((2 * rows, D), BF)] * (count // 2) + [sds((8, 128), F32)]
        + [sds((total, cols), BF) for cols in (D, FF, FF, D, D)],
        pos, *bufs, dout, slot, up, down, *held,
        grid=(count * steps,), pos=True,
        in_specs=blocks + [tile(D, 0), tile(8, 0), fixed((D, FF)), fixed((FF, D))]
        + [pl.BlockSpec(memory_space=pl.ANY)] * len(held),
        out_specs=pairs + [pl.BlockSpec((8, 128), lambda i, p: (0, 0)), pl.BlockSpec((size, D), there)]
        + [tile(FF), tile(FF), tile(D), tile(D)],
        alias=alias,
        flops=8 * rows * count * D * FF, moved=count * rows * 13 << 10,
    )
    return outs[: count // 2], outs[count // 2], outs[count // 2 + 1 :]


def expert_grad_kernel(steps, act_ref, du_ref, buf_ref, dout_ref, gup_ref, gdown_ref, up_acc, down_acc):
    i = pl.program_id(0)

    @pl.when(i == 0)
    def _():
        up_acc[...] = jnp.zeros_like(up_acc)
        down_acc[...] = jnp.zeros_like(down_acc)

    up_acc[...] += t_mm(buf_ref[...], du_ref[...])
    down_acc[...] += t_mm(act_ref[...], dout_ref[...])

    @pl.when(i == steps - 1)
    def _():
        gup_ref[...] = up_acc[...].astype(BF)
        gdown_ref[...] = down_acc[...].astype(BF)


def expert_grads(act, du, buf, dout):
    rows = buf.shape[0]
    size = 1024
    tile = lambda cols: pl.BlockSpec((size, cols), lambda i: (i, 0))
    return call(
        functools.partial(expert_grad_kernel, rows // size),
        [sds((D, FF), BF), sds((FF, D), BF)], act, du, buf, dout,
        grid=(rows // size,),
        in_specs=[tile(FF), tile(FF), tile(D), tile(D)],
        out_specs=[whole((D, FF)), whole((FF, D))],
        scratch=[pltpu.VMEM((D, FF), F32), pltpu.VMEM((FF, D), F32)],
        flops=4 * rows * D * FF, moved=44 << 20, mib=62,
    )


def route(lengths, task_ids, task_experts, capacity, task_logits, cap_slots, rel):
    sentences = lengths.shape[1]
    experts = capacity.shape[0]
    tasks = task_experts.shape[0]
    lens, ids = lengths.reshape(-1), task_ids.reshape(-1)
    ends = jnp.cumsum(lens)
    starts = ends - lens
    table = jnp.take_along_axis(task_logits, task_experts, axis=1)
    gates = jax.nn.softmax(table, axis=-1)
    hot = ids[:, None] == lax.broadcasted_iota(jnp.int32, (1, tasks), 1)
    expert = jnp.sum(jnp.where(hot[:, :, None], task_experts[None], 0), axis=1)
    gate = jnp.sum(jnp.where(hot[:, :, None], gates[None], 0.0), axis=1)
    pair_expert = expert.reshape(-1)
    pair_len = jnp.repeat(lens, 2)
    expert_hot = (pair_expert[:, None] == lax.broadcasted_iota(jnp.int32, (1, experts), 1)).astype(jnp.int32)
    running = jnp.cumsum(expert_hot * pair_len[:, None], axis=0)
    filled = jnp.sum(running * expert_hot, axis=1)
    limits = jnp.sum(expert_hot * capacity[None, :], axis=1)
    base = jnp.where(filled <= limits, jnp.bitwise_xor(pair_expert, rel) * cap_slots + filled - pair_len, -1)
    base_two = base.reshape(sentences, 2)

    def lanes(rows):
        rows = jnp.stack([row.astype(F32) for row in rows])
        return jnp.pad(rows, ((0, 8 - rows.shape[0]), (0, 128 - rows.shape[1])))

    sent = lanes([starts, ends, base_two[:, 0], base_two[:, 1]])
    pair = lanes([base, pair_len, jnp.repeat(starts, 2), gate.reshape(-1), jnp.repeat(ids, 2)])
    slots = experts * cap_slots
    tok, slot = call(
        functools.partial(route_kernel, slots),
        [sds((PACK, 8), F32), sds((slots, 8), F32)], sent, pair,
        flops=1_000_000, moved=3 << 20, mib=24,
    )
    return tok, slot, pair, gates


EXPERT = ("xy", "core")
BOTH = ("dp", "xy", "core")


def flip(rows, j, ex):
    return lax.ppermute(rows, EXPERT, [(i, i ^ j) for i in range(ex)])


def turn(rows, k, dp):
    return lax.ppermute(rows, "dp", [(i, (i + k) % dp) for i in range(dp)])


def tie(value, *after):
    return lax.optimization_barrier((value,) + after)[0]


def send_even(here, ex):
    return [here] + [flip(here, j, ex) for j in range(2, ex, 2)]


def send_core(even, ex):
    got = []
    for one in even:
        got += [one, flip(one, 1, ex)]
    return got


def add_core(pos, own, got, near=False):
    parts = own.shape[0]
    outs = [(sds(own.shape[1:], BF), 1)] * parts if near else [(sds(own.shape, BF), parts)]
    got = staged(
        functools.partial(add_core_kernel, near), outs, [(own, parts), (got, parts)], [pos],
        order=[(i, j) for j in range(parts) for i in range(2)], flops=1_000_000, moved=own.size * 6,
    )
    return got if near else got[0]


def add_near(pos, *lists):
    lists = [one if isinstance(one, list) else [one] for one in lists]
    rows = sum(one[0].shape[-2] for one in lists)
    dp = lists[0][0].shape[-3]
    return call(
        functools.partial(add_near_kernel, [len(one) for one in lists]), [sds((rows, WIRE), BF)] * dp,
        pos, *sum(lists, []), pos=True, flops=1_000_000, moved=rows << 14,
    )


def send_near(sums, ex):
    return [sums[0]] + [flip(sums[j], 2 * j, ex) for j in range(1, ex // 2)]


def send_turn(sums, dp):
    return [sums[0]] + [turn(sums[k], k, dp) for k in range(1, dp)]


def add_turn(got):
    return call(add_turn_kernel, sds(got[0].shape, BF), *got, flops=1_000_000, moved=got[0].size * 10, mib=62)


def swap(parts, axis):
    return lax.all_to_all(parts, axis, split_axis=0, concat_axis=0, tiled=True)


def local(n_dp, n_ex, hidden_in, lengths, task_ids, task_experts, capacity, task_logits, norm_params,
          w_qkv, w_attn, w_up, w_down, expert_up, expert_down, cotangent):
    experts = capacity.shape[0]
    cap_slots = max(4 * hidden_in.shape[0] // experts, 2 * MOST_LEN)
    slots = experts * cap_slots
    me, here = lax.axis_index(EXPERT), lax.axis_index("dp")
    pos = jnp.stack([me, here]).astype(jnp.int32)
    split = (n_dp, n_ex)
    wire = wired(split)

    def mine(shard):
        rows = shard.shape[0] // n_ex
        return lax.dynamic_slice_in_dim(shard, me * rows, rows, 0)

    def exchange(pair, j):
        return flip(pair, j, n_ex) if j else pair

    tok, slot, pair, gates = route(lengths, task_ids, task_experts, capacity, task_logits, cap_slots, me)
    if wire:
        rows = piece_rows(split)

        def blocks(wide):
            return [wide[:, c * WIRE : (c + 1) * WIRE] for c in range(wide.shape[1] // WIRE)]

        norms = jnp.pad(mine(norm_params), ((0, 0), (0, WIRE - 8)))
        qkv, attn = mine(w_qkv), mine(w_attn)
        piece = blocks(qkv[:, 0]) + [attn[:, 0], norms] + blocks(mine(w_up)) + [mine(w_down)]
        piece = jnp.concatenate(piece + blocks(qkv[:, 1]) + [attn[:, 1]])
        parts = [piece] + [turn(piece, k, n_dp) for k in range(1, n_dp)]
        expert_up, expert_down = tie(expert_up, *parts[1:]), tie(expert_down, *parts[1:])
        zero, feed, one = [
            jnp.stack([part[lo * rows : hi * rows] for part in parts]) for lo, hi in ((0, 5), (5, 13), (13, 17))
        ]
        cots = [cotangent, flip(cotangent, 2, n_ex), flip(cotangent, 4, n_ex)]
        zero = send_even(tie(zero, *cots[1:]), n_ex)
        pairs = pair
        j = 1
        while j < n_ex:
            pairs = jnp.concatenate([pairs, flip(pairs, j, n_ex)])
            j *= 2
        zero = send_core([tie(part, tok, pairs) for part in zero], n_ex)
        feed = send_even(tie(feed, *zero[1:]), n_ex)
        groups = [(0, 2), (2, 6), (6, 8)]

        def gather_group(lo, hi, pairs):
            sources = sum([[cots[j], flip(cots[j], 1, n_ex)] for j in range(lo // 2, hi // 2)], [])
            return gather_near(pairs, sources, cap_slots, lo)

        near = [gather_group(*group, pairs) for group in groups[:2]]
        attn_zero, params = call(
            functools.partial(assemble_norm_kernel, split), [sds((D, 4 * D), BF), sds((8, D), F32)], pos, *zero,
            scratch=[pltpu.VMEM((D, 128), F32)], pos=True, flops=1_000_000, moved=4 << 20, mib=24,
        )
        fwd = tie(hidden_in, *sum(near, []))
        h1, *saved_zero = attention_forward(fwd, params, tok, attn_zero, 0, False)
        one = send_even(tie(one, h1, *feed[1:]), n_ex)
        feed = send_core([tie(part, h1) for part in feed], n_ex)
        up, down = assemble(split, pos, feed, True)
        h2, *saved_feed = feed_forward(h1, params, up, down)
        one = [tie(part, h2) for part in one]
        cots.append(flip(tie(cotangent, *one[1:]), 6, n_ex))
        one = send_core(one, n_ex)
        attn_one = assemble(split, pos, one, False)[0]
    else:

        def gather_all(shard):
            return lax.all_gather(mine(shard), BOTH, axis=0, tiled=True)

        params = lax.all_gather(norm_params, "dp", axis=0, tiled=True).astype(F32).T
        attn_zero = gather_all(jnp.concatenate([w_qkv[:, 0], w_attn[:, 0]], axis=1))
        up, down = gather_all(w_up), gather_all(w_down)
        attn_one = gather_all(jnp.concatenate([w_qkv[:, 1], w_attn[:, 1]], axis=1))
        h1, *saved_zero = attention_forward(hidden_in, params, tok, attn_zero, 0, False)
        h2, *saved_feed = feed_forward(h1, params, up, down)
        pairs = pair
        j = 1
        while j < n_ex:
            pairs = jnp.concatenate([pairs, flip(pairs, j, n_ex)])
            j *= 2
        groups = [(j, j + 4) for j in range(0, n_ex, 4)]
        cots = [cotangent] + [flip(cotangent, j, n_ex) for j in range(1, n_ex)]
        near = [gather_near(pairs, cots[lo:hi], cap_slots, lo) for lo, hi in groups]
    up_expert = lax.all_gather(expert_up[0], "dp", axis=0, tiled=True)
    down_expert = lax.all_gather(expert_down[0], "dp", axis=0, tiled=True)
    h3, *saved_one, c = attention_forward(h2, params, tok, attn_one, 4, True)
    sent = gather_rows(slot, c, experts)
    sums, held, table = [], (), 0.0
    if wire:
        sent = [tie(pair, cots[-1]) for pair in sent]
    bufs = {j: exchange(sent[j // 2], j) for j in range(0, groups[-1][0], 2)}
    for n, (lo, hi) in enumerate(groups):
        if wire and n == 1:
            near.append(gather_group(*groups[2], tie(pairs, sums[0])))
        dout, slot_near = near[n]
        if n == 1:
            for j in range(groups[-1][0], n_ex, 2):
                bufs[j] = exchange(tie(sent[j // 2], *[bufs[i] for i in range(lo, hi, 2)], *sums[:1]), j)
        for j in range(lo, hi, 2):
            bufs[j + 1] = flip(tie(bufs[j], *sums[-1:], *near[-1]), 1, n_ex)
        back, part, held = expert_rows(
            pos, [bufs[j] for j in range(lo, hi)], dout, slot_near, up_expert, down_expert, slots, lo, held
        )
        sums += back
        table = table + part
    out, *held = held
    back = [exchange(pair, 2 * j) for j, pair in enumerate(sums)]
    gup_expert, gdown_expert = expert_grads(*held)
    far = [flip(tie(pair, gup_expert), 1, n_ex) for pair in back]
    dbuf_home = sum([list(both) for both in zip(back, far)], [])
    out_home = swap(tie(out, *back, gup_expert).reshape(experts, cap_slots, D), EXPERT).reshape(-1, D)
    gn_one, gn_moe, dx, g_one = first_backward(
        pos, dbuf_home, h3, cotangent, h2, saved_one, params, tok, attn_one, 4, split
    )
    expert_up_sum = lax.psum_scatter(tie(gup_expert, gn_moe), "dp", scatter_dimension=0, tiled=True).astype(F32)
    expert_down_sum = lax.psum_scatter(tie(gdown_expert, gn_moe), "dp", scatter_dimension=0, tiled=True).astype(F32)
    if wire:
        got_one = add_core(pos, g_one[0], flip(g_one[1], 1, n_ex), True)
        dx = tie(dx, got_one[0])
        got_one = send_near(got_one, n_ex)
    gn_feed, dx, g_feed = feed_backward(pos, dx, h1, saved_feed, params, up, down, split)
    if wire:
        got_feed = flip(tie(g_feed[1], out_home, *got_one[1:]), 1, n_ex)
        sum_feed = add_core(pos, g_feed[0], got_feed)
        dx = tie(dx, sum_feed)
        got_feed = swap(sum_feed, "xy")
    gn_zero, grad_in, g_zero = last_backward(
        pos, dx, hidden_in, saved_zero, params, tok, attn_zero, 0, split, (gn_feed, gn_one, gn_moe, table)
    )
    if wire:
        early = add_near(pos, tie(got_feed, gn_zero), got_one)
        got_zero = tie(flip(g_zero[1], 1, n_ex), early[0])
        early = send_turn(early, n_dp)
        sum_zero = add_core(pos, g_zero[0], got_zero)
        h3 = tie(h3, sum_zero)
        sum_zero = swap(sum_zero, "xy")
    hidden_out = combine_out(pos, tok, slot, out_home, h3, experts)
    if wire:
        sum_zero = tie(sum_zero, hidden_out)
        early = lax.all_gather(add_turn([tie(one, sum_zero) for one in early]), EXPERT, axis=0)
        sum_zero = send_turn(add_near(pos, tie(sum_zero, hidden_out)), n_dp)
        sum_zero = add_turn([tie(part, expert_up_sum, expert_down_sum) for part in sum_zero])
        last = lax.all_gather(sum_zero, EXPERT, axis=0)
        rows = D // n_dp
        grad_qkv, grad_attn, grad_up, grad_down, gn, sums = call(
            functools.partial(spread_kernel, split),
            [sds((2, rows, 3 * D), F32), sds((2, rows, D), F32), sds((rows, FF), F32), sds((FF // n_dp, D), F32),
             sds((8, rows), F32), sds((experts, 128), F32)],
            pos, last, early,
            pos=True, flops=1_000_000, moved=7 << 20, mib=32,
        )
        grad_qkv, grad_attn, gn = grad_qkv.transpose(1, 0, 2), grad_attn.transpose(1, 0, 2), gn.T
    else:
        small = jnp.concatenate([gn_zero, gn_feed, gn_one, gn_moe], axis=0)
        table = lax.dynamic_update_slice_in_dim(jnp.zeros((experts, 128), F32), table[:1], me, 0)
        small = jnp.concatenate([small, jnp.pad(table, ((0, 0), (0, D - 128)))], axis=0)
        small = lax.psum(small, BOTH)
        gn = lax.dynamic_slice_in_dim(small[:8], here * (D // n_dp), D // n_dp, 1).T
        sums = small[8:]

        def reduce_all(grad):
            rows = grad.shape[0] // (n_dp * n_ex)
            grad = grad.reshape(n_dp, n_ex, rows, -1).transpose(1, 0, 2, 3).reshape(grad.shape)
            part = lax.psum_scatter(grad, EXPERT, scatter_dimension=0, tiled=True)
            part = lax.psum_scatter(part, "dp", scatter_dimension=0, tiled=True)
            return lax.all_gather(part, EXPERT, axis=0, tiled=True).astype(F32)

        g_one, grad_up, grad_down, g_zero = [reduce_all(g) for g in (*g_one, *g_feed, *g_zero)]
        grad_qkv = jnp.stack([g_zero[:, : 3 * D], g_one[:, : 3 * D]], axis=1)
        grad_attn = jnp.stack([g_zero[:, 3 * D :], g_one[:, 3 * D :]], axis=1)
    sums = sums[:, : task_logits.shape[0]].T
    hot = task_experts[:, :, None] == lax.broadcasted_iota(jnp.int32, (1, 1, experts), 2)
    pair_sum = jnp.sum(jnp.where(hot, sums[:, None, :], 0.0), axis=2)
    lean = gates[:, 0] * gates[:, 1] * (pair_sum[:, 0] - pair_sum[:, 1])
    grad_logits = jnp.where(hot[:, 0], lean[:, None], 0.0) - jnp.where(hot[:, 1], lean[:, None], 0.0)
    return (
        hidden_out, grad_in, grad_logits, gn, grad_qkv, grad_attn, grad_up, grad_down,
        expert_up_sum[None], expert_down_sum[None],
    )


def solution(mesh):
    n_dp, n_ex = mesh.shape["dp"], mesh.shape["expert"]
    mesh = jax.sharding.Mesh(mesh.devices.reshape(n_dp, n_ex // 2, 2), BOTH)
    token = P(BOTH, None)
    expert = P(EXPERT, "dp", None)
    in_specs = (
        token, token, token, P(), P(), P(), P("dp", None), P("dp", None, None), P("dp", None, None),
        P("dp", None), P("dp", None), expert, expert, token,
    )
    out_specs = (
        token, token, P(), P("dp", None), P("dp", None, None), P("dp", None, None), P("dp", None), P("dp", None),
        expert, expert,
    )
    step = functools.partial(local, n_dp, n_ex)
    return jax.shard_map(step, mesh=mesh, in_specs=in_specs, out_specs=out_specs, check_vma=False)
```

```python
import functools

import jax
import jax.numpy as jnp
from jax import lax
from jax.experimental import pallas as pl
from jax.experimental.pallas import tpu as pltpu
from jax.sharding import PartitionSpec as P

D = 512
FF = 2048
HEADS = 8
HEAD = D // HEADS
PACK = 1024
MOST_LEN = 64
ROWS = 256
QB = 128
KB = QB + 2 * MOST_LEN
EPS = 1e-05
BLOCKED = -1e30
BF = jnp.bfloat16
F32 = jnp.float32
GELU_C = 0.7978845608028654
GELU_A = 0.044715


COST = 2


def mm(left, right):
    return lax.dot_general(left, right, (((1,), (0,)), ((), ())), preferred_element_type=F32)


def mm_t(left, right):
    return lax.dot_general(left, right, (((1,), (1,)), ((), ())), preferred_element_type=F32)


def t_mm(left, right):
    return lax.dot_general(left, right, (((0,), (0,)), ((), ())), preferred_element_type=F32)


def unit_rows(hidden):
    centered = hidden - jnp.mean(hidden, axis=-1, keepdims=True)
    spread = jnp.mean(centered * centered, axis=-1, keepdims=True)
    scale = lax.rsqrt(spread + EPS)
    return centered * scale, scale


def unit_back(unit, scale, gain, grad):
    inner = grad * gain
    first = jnp.mean(inner, axis=-1, keepdims=True)
    second = jnp.mean(inner * unit, axis=-1, keepdims=True)
    return scale * (inner - first - unit * second)


def gelu_both(z):
    square = z * z
    half = 0.5 + 0.5 * jnp.tanh(z * (GELU_C + GELU_C * GELU_A * square))
    act = z * half
    return act, half + (act - act * half) * (2.0 * GELU_C + 6.0 * GELU_C * GELU_A * square)


def call(kernel, out_shape, *args, grid=None, in_specs=None, out_specs=None, scratch=(), mib=62, flops=0, moved=0,
         alias=None, pos=False):
    extra = {}
    if grid is not None and pos:
        extra["grid_spec"] = pltpu.PrefetchScalarGridSpec(
            num_scalar_prefetch=1, grid=grid, in_specs=in_specs, out_specs=out_specs, scratch_shapes=scratch
        )
    else:
        extra["scratch_shapes"] = scratch
        if grid is not None:
            extra.update(grid=grid, in_specs=in_specs, out_specs=out_specs)
        elif pos:
            held = pl.BlockSpec(memory_space=pltpu.VMEM)
            extra["in_specs"] = [pl.BlockSpec(memory_space=pltpu.SMEM)] + [held] * (len(args) - 1)
    if alias:
        extra["input_output_aliases"] = alias
    return pl.pallas_call(
        kernel,
        out_shape=out_shape,
        compiler_params=pltpu.CompilerParams(vmem_limit_bytes=mib << 20),
        cost_estimate=pl.CostEstimate(flops=flops // COST, bytes_accessed=moved // COST, transcendentals=0),
        **extra,
    )(*args)


def sds(shape, dtype):
    return jax.ShapeDtypeStruct(shape, dtype)


WIRE = 512


def piece_rows(split):
    dp, ex = split
    return D // (dp * ex)


def wired(split):
    dp, ex = split
    return piece_rows(split) % 16 == 0 and ex == 8


def near(split, pos_ref, j, k):
    return k * split[1] + jnp.bitwise_xor(pos_ref[0], j)


def send_rows(split, pos_ref, scr_ref, own_ref, core_ref, at, rows):
    dp, ex = split
    for j in range(ex):
        out = core_ref if j % 2 else own_ref
        for k in range(dp):
            start = pl.multiple_of(near(split, pos_ref, j, k) * rows, rows)
            out[j // 2, k, at : at + rows, :] = scr_ref[pl.ds(start, rows), :]


def wire_shapes(split, blocks):
    dp, ex = split
    shape = (ex // 2, dp, blocks * piece_rows(split), WIRE)
    return [sds(shape, BF), sds(shape, BF)]


WINDOW = 12 << 20


class Stage:
    def __init__(self, ins, outs, split_in, split_out, hold_in, hold_out, sem_in, sem_out, order, axes):
        self.ins, self.outs = hold_in, hold_out
        self.split_in, self.split_out, self.axes = split_in, split_out, axes
        self.out_hbm, self.out_sem, self.sent = outs, sem_out, []
        self.got, self.begun, self.copies, self.bytes = set(), 0, {}, {}
        order = order or [(i, r) for i, parts in enumerate(split_in) for r in range(parts)]
        for n, (i, r) in enumerate(order):
            rows = self.rows(hold_in[i], split_in[i], r)
            self.copies[i, r] = pltpu.make_async_copy(ins[i].at[rows], hold_in[i].at[rows], sem_in.at[n])
            self.bytes[i, r] = hold_in[i].size * hold_in[i].dtype.itemsize // split_in[i]
        self.order = order
        self.ahead(0)

    def rows(self, ref, parts, r, axis=0):
        size = ref.shape[axis] // parts
        return (slice(None),) * axis + (pl.ds(r * size, size),)

    def ahead(self, least):
        while self.begun < len(self.order):
            flying = sum(self.bytes[key] for key in self.order[: self.begun] if key not in self.got)
            if self.begun >= least and flying >= WINDOW:
                break
            self.copies[self.order[self.begun]].start()
            self.begun += 1

    def need(self, *which):
        for i in which:
            i, r = i if isinstance(i, tuple) else (i, None)
            for k in range(self.split_in[i]) if r is None else [r]:
                if (i, k) not in self.got:
                    self.ahead(self.order.index((i, k)) + 1)
                    self.copies[i, k].wait()
                    self.got.add((i, k))
                    self.ahead(0)

    def done(self, i, r=None):
        parts = self.split_out[i]
        for k in range(parts) if r is None else [r]:
            rows = self.rows(self.outs[i], parts, k, self.axes[i])
            sem = self.out_sem.at[sum(self.split_out[:i]) + k]
            copy = pltpu.make_async_copy(self.outs[i].at[rows], self.out_hbm[i].at[rows], sem)
            copy.start()
            self.sent.append(copy)

    def finish(self):
        self.need(*self.order)
        for copy in self.sent:
            copy.wait()


def staged(body, outs, ins, small=(), small_outs=(), scratch=(), flops=0, moved=0, order=None, mib=62):
    arrays, split_in = [x for x, _ in ins], [n for _, n in ins]
    shapes, split_out = [x[0] for x in outs], [x[1] for x in outs]
    axes = [x[2] if len(x) > 2 else 0 for x in outs]

    def kernel(*refs):
        at = 0
        groups = []
        for n in (len(small), len(arrays), len(small_outs), len(shapes), len(arrays), len(shapes), len(scratch), 2):
            groups.append(refs[at : at + n])
            at += n
        few, hbm_in, few_out, hbm_out, hold_in, hold_out, own, (sem_in, sem_out) = groups
        stage = Stage(hbm_in, hbm_out, split_in, split_out, hold_in, hold_out, sem_in, sem_out, order, axes)
        body(stage, few, few_out, own)
        stage.finish()

    space = [pl.BlockSpec(memory_space=pltpu.SMEM if x.dtype == jnp.int32 else pltpu.VMEM) for x in small]
    got = pl.pallas_call(
        kernel,
        out_shape=list(small_outs) + shapes,
        in_specs=space + [pl.BlockSpec(memory_space=pl.ANY)] * len(arrays),
        out_specs=[pl.BlockSpec(memory_space=pltpu.VMEM)] * len(small_outs)
        + [pl.BlockSpec(memory_space=pl.ANY)] * len(shapes),
        scratch_shapes=[pltpu.VMEM(x.shape, x.dtype) for x in arrays + shapes]
        + list(scratch)
        + [pltpu.SemaphoreType.DMA((sum(split_in),)), pltpu.SemaphoreType.DMA((max(sum(split_out), 1),))],
        compiler_params=pltpu.CompilerParams(vmem_limit_bytes=mib << 20),
        cost_estimate=pl.CostEstimate(flops=flops // COST, bytes_accessed=moved // COST, transcendentals=0),
    )(*small, *arrays)
    return list(got)


def route_kernel(slots, sent_ref, pair_ref, tok_ref, slot_ref):
    t = lax.broadcasted_iota(jnp.int32, (PACK, 128), 0).astype(F32)
    start, end = sent_ref[0:1, :], sent_ref[1:2, :]
    member = (t >= start) & (t < end)

    def pick(value):
        return jnp.sum(jnp.where(member, value, 0.0), axis=1, keepdims=True)

    lane = lax.broadcasted_iota(jnp.int32, (PACK, 8), 1)
    out = jnp.where(lane == 0, pick(start), 0.0)
    out = jnp.where(lane == 1, pick(end), out)
    for k in range(2):
        base = sent_ref[2 + k : 3 + k, :]
        slot = pick(jnp.where(base >= 0, base - start + t + 1.0, 0.0)) - 1.0
        out = jnp.where(lane == 2 + k, slot, out)
    tok_ref[...] = out
    chunk = 512
    base, length, first = pair_ref[0:1, :], pair_ref[1:2, :], pair_ref[2:3, :]
    gate, task = pair_ref[3:4, :], pair_ref[4:5, :]
    for i in range(slots // chunk):
        s = lax.broadcasted_iota(jnp.int32, (chunk, 128), 0).astype(F32) + float(i * chunk)
        held = (base >= 0) & (s >= base) & (s < base + length)

        def take(value, held=held):
            return jnp.sum(jnp.where(held, value, 0.0), axis=1, keepdims=True)

        lane = lax.broadcasted_iota(jnp.int32, (chunk, 8), 1)
        out = jnp.where(lane == 0, take(first - base + s + 1.0) - 1.0, 0.0)
        out = jnp.where(lane == 1, take(gate), out)
        out = jnp.where(lane == 2, take(task + 1.0) - 1.0, out)
        slot_ref[i * chunk : (i + 1) * chunk, :] = out


def head_halves(block):
    low = lax.broadcasted_iota(jnp.int32, (1, 128), 1) < HEAD
    zero = jnp.zeros_like(block)
    return jnp.concatenate([jnp.where(low, block, zero), jnp.where(low, zero, block)], axis=0)


def merge_halves(stacked):
    low = lax.broadcasted_iota(jnp.int32, (1, 128), 1) < HEAD
    return jnp.where(low, stacked[:QB], stacked[QB:])


def key_start(i):
    return jnp.clip(i * QB - MOST_LEN, 0, PACK - KB)


def attention_kernel(norm_at, last, x_ref, np_ref, tok_ref, w_ref, *refs):
    if last:
        slot_ref, h_ref, a_ref, qkv_ref, ctx_ref = refs[:5]
        pair_refs, c_ref = refs[5:-1], refs[-1]
    else:
        h_ref, a_ref, qkv_ref, ctx_ref = refs
    gain, shift = np_ref[norm_at : norm_at + 1, :], np_ref[norm_at + 1 : norm_at + 2, :]
    for r in range(PACK // ROWS):
        rows = slice(r * ROWS, (r + 1) * ROWS)
        unit, _ = unit_rows(x_ref[rows, :].astype(F32))
        a = (unit * gain + shift).astype(BF)
        a_ref[rows, :] = a
        qkv_ref[rows, :] = mm(a, w_ref[:, 0 : 3 * D]).astype(BF)

    def block(i, carry):
        q0 = pl.multiple_of(i * QB, QB)
        k0 = pl.multiple_of(key_start(i), MOST_LEN)
        start, end = tok_ref[pl.ds(q0, QB), 0:1], tok_ref[pl.ds(q0, QB), 1:2]
        key = (lax.broadcasted_iota(jnp.int32, (QB, KB), 1) + k0).astype(F32)
        mask = (key >= start) & (key < end)
        mask = jnp.concatenate([mask, mask], axis=0)
        at = [pair * 128 for pair in range(HEADS // 2)]
        q = [head_halves(qkv_ref[pl.ds(q0, QB), a : a + 128] * BF(HEAD**-0.5)) for a in at]
        k = [qkv_ref[pl.ds(k0, KB), D + a : D + a + 128] for a in at]
        v = [qkv_ref[pl.ds(k0, KB), 2 * D + a : 2 * D + a + 128] for a in at]
        scores = [jnp.where(mask, mm_t(x, y), BLOCKED) for x, y in zip(q, k)]
        raised = [jnp.exp(x - jnp.max(x, axis=1, keepdims=True)) for x in scores]
        probs = [(x * (1.0 / jnp.sum(x, axis=1, keepdims=True))).astype(BF) for x in raised]
        ctx = [merge_halves(mm(x, y)).astype(BF) for x, y in zip(probs, v)]
        ctx_ref[pl.ds(q0, QB), :] = jnp.concatenate(ctx, axis=1)
        return carry

    lax.fori_loop(0, PACK // QB, block, 0, unroll=4)
    for r in range(PACK // ROWS):
        rows = slice(r * ROWS, (r + 1) * ROWS)
        h = x_ref[rows, :].astype(F32) + mm(ctx_ref[rows, :], w_ref[:, 3 * D : 4 * D])
        h_ref[rows, :] = h
        if last:
            unit, _ = unit_rows(h)
            c_ref[rows, :] = (unit * np_ref[6:7, :] + np_ref[7:8, :]).astype(BF)
    if last:
        size = pair_refs[0].shape[0] // 2
        tokens = lax.broadcasted_iota(jnp.int32, (size, PACK), 1).astype(F32)
        for n in range(2 * len(pair_refs)):
            hot = jnp.where(slot_ref[n * size : (n + 1) * size, 0:1] == tokens, 1.0, 0.0).astype(BF)
            pair_refs[n // 2][n % 2 * size : (n % 2 + 1) * size, :] = mm(hot, c_ref[...]).astype(BF)


def attention_forward(hidden, params, tok, weights, norm_at, slot=None, experts=0):
    last = slot is not None
    outs = [sds((PACK, D), F32), sds((PACK, D), BF), sds((PACK, 3 * D), BF), sds((PACK, D), BF)]
    more, scratch = (), ()
    if last:
        outs += [sds((2 * slot.shape[0] // experts, D), BF)] * (experts // 2)
        more, scratch = (slot,), [pltpu.VMEM((PACK, D), BF)]
    return call(
        functools.partial(attention_kernel, norm_at, last),
        outs, hidden, params, tok, weights, *more, scratch=scratch,
        flops=6_000_000_000, moved=12 << 20, mib=40,
    )


def combine_grads(io, tok_ref, h_ref, cot_ref, blocks, np_ref, dx_ref, gn_ref, needs):
    for e, ref in enumerate(blocks):
        size = ref.shape[0] // 2
        io.need((needs[2 + e], e % 2))
        part = mm(slots_hot(tok_ref, size, e), ref[e % 2 * size : (e % 2 + 1) * size, :])
        dx_ref[...] = part if e == 0 else dx_ref[...] + part
    io.need(*needs[:2])
    dgain, dshift = jnp.zeros((1, D), F32), jnp.zeros((1, D), F32)
    for r in range(PACK // ROWS):
        rows = slice(r * ROWS, (r + 1) * ROWS)
        dnorm = dx_ref[rows, :]
        unit, scale = unit_rows(h_ref[rows, :])
        dgain += jnp.sum(dnorm * unit, axis=0, keepdims=True)
        dshift += jnp.sum(dnorm, axis=0, keepdims=True)
        dx_ref[rows, :] = cot_ref[rows, :].astype(F32) + unit_back(unit, scale, np_ref[6:7, :], dnorm)
    gn_ref[0:1, :] = dgain
    gn_ref[1:2, :] = dshift


def attention_core_back(io, dx_ref, dx_at, w_ref, w_at, tok_ref, qkv_ref, at_need, dctx_ref, dqkv_ref, acc_ref):
    io.need(w_at)
    for r in range(PACK // ROWS):
        rows = slice(r * ROWS, (r + 1) * ROWS)
        if dx_at is not None:
            io.need((dx_at, r))
        dctx_ref[rows, :] = mm_t(dx_ref[rows, :].astype(BF), w_ref[:, 3 * D : 4 * D]).astype(BF)
    acc_ref[...] = jnp.zeros_like(acc_ref)
    io.need(*at_need)

    def block(i, carry):
        q0 = pl.multiple_of(i * QB, QB)
        k0 = pl.multiple_of(key_start(i), MOST_LEN)
        start, end = tok_ref[pl.ds(k0, KB), 0:1], tok_ref[pl.ds(k0, KB), 1:2]
        query = (lax.broadcasted_iota(jnp.int32, (KB, QB), 1) + q0).astype(F32)
        mask = (query >= start) & (query < end)
        mask = jnp.concatenate([mask, mask], axis=1)
        at = [pair * 128 for pair in range(HEADS // 2)]
        q = [head_halves(qkv_ref[pl.ds(q0, QB), a : a + 128] * BF(HEAD**-0.5)) for a in at]
        k = [qkv_ref[pl.ds(k0, KB), D + a : D + a + 128] for a in at]
        v = [qkv_ref[pl.ds(k0, KB), 2 * D + a : 2 * D + a + 128] for a in at]
        g = [head_halves(dctx_ref[pl.ds(q0, QB), a : a + 128]) for a in at]
        scores = [jnp.where(mask, mm_t(x, y), BLOCKED) for x, y in zip(k, q)]
        dprobs = [mm_t(x, y) for x, y in zip(v, g)]
        raised = [jnp.exp(x - jnp.max(x, axis=0, keepdims=True)) for x in scores]
        probs = [x * (1.0 / jnp.sum(x, axis=0, keepdims=True)) for x in raised]
        delta = [jnp.sum(x * y, axis=0, keepdims=True) for x, y in zip(probs, dprobs)]
        dscores = [(x * (y - z)).astype(BF) for x, y, z in zip(probs, dprobs, delta)]
        dq = [(merge_halves(t_mm(x, y)) * (HEAD**-0.5)).astype(BF) for x, y in zip(dscores, k)]
        dk = [mm(x, y) for x, y in zip(dscores, q)]
        dv = [mm(x.astype(BF), y) for x, y in zip(probs, g)]
        dqkv_ref[pl.ds(q0, QB), 0:D] = jnp.concatenate(dq, axis=1)
        acc_ref[pl.ds(k0, KB), :] += jnp.concatenate(dk + dv, axis=1)
        return carry

    lax.fori_loop(0, PACK // QB, block, 0, unroll=2)
    dqkv_ref[:, D:] = acc_ref[...].astype(BF)


def wire_outs(split, blocks):
    return [(x, blocks, 2) for x in wire_shapes(split, blocks)]


def attention_weight_back(io, split, pos_ref, a_ref, ctx_ref, dx_ref, dqkv_ref, grads, scr_ref):
    rows = piece_rows(split)
    for c in range(4):
        cols = slice(c * D, (c + 1) * D)
        if c < 3:
            grad = t_mm(a_ref[...], dqkv_ref[:, cols]).astype(BF)
        else:
            grad = t_mm(ctx_ref[...], dx_ref[...].astype(BF)).astype(BF)
        if wired(split):
            scr_ref[...] = grad
            send_rows(split, pos_ref, scr_ref, grads[0], grads[1], c * rows, rows)
            io.done(1, c)
            io.done(2, c)
        else:
            grads[0][:, cols] = grad


def first_back_kernel(split, norm_at, io, few, few_out, own):
    pos_ref, np_ref = few
    tok_ref, h_ref, cot_ref, w_ref, qkv_ref, a_ref, ctx_ref, x_ref = io.ins[:8]
    dx_ref, dctx_ref, dqkv_ref, acc_ref, scr_ref = own
    blocks = io.ins[8:]
    io.need(0)
    combine_grads(io, tok_ref, h_ref, cot_ref, blocks, np_ref, dx_ref, few_out[1], [1, 2] + list(range(8, 8 + len(blocks))))
    attention_core_back(io, dx_ref, None, w_ref, 3, tok_ref, qkv_ref, [4], dctx_ref, dqkv_ref, acc_ref)
    io.need(5, 6, 7)
    attention_weight_back(io, split, pos_ref, a_ref, ctx_ref, dx_ref, dqkv_ref, io.outs[1:], scr_ref)
    if not wired(split):
        io.done(1)
    norm_back_rows(norm_at, dx_ref, x_ref, dqkv_ref, np_ref, w_ref, io.outs[0], few_out[0], io)


def first_backward(pos, blocks, h, cotangent, hidden, saved, params, tok, weights, norm_at, split):
    a, qkv, ctx = saved
    grads = wire_outs(split, 4) if wired(split) else [(sds((D, 4 * D), BF), 1)]
    ins = [(x, 1) for x in (tok, h, cotangent, weights, qkv, a, ctx, hidden)] + [(x, 2) for x in blocks]
    order = [(0, 0)] + [(8 + n, n % 2) for n in range(len(blocks))] + [(n, 0) for n in range(1, 8)]
    norm, norm_moe, out, *grads = staged(
        functools.partial(first_back_kernel, split, norm_at),
        [(sds((PACK, D), F32), 4)] + grads, ins, [pos, params], [sds((2, D), F32)] * 2,
        [pltpu.VMEM((PACK, D), F32), pltpu.VMEM((PACK, D), BF), pltpu.VMEM((PACK, 3 * D), BF),
         pltpu.VMEM((PACK, 2 * D), F32), pltpu.VMEM((D, D), BF)],
        flops=16_000_000_000, moved=20 << 20, order=order,
    )
    return norm, norm_moe, out, grads


def last_back_kernel(split, norm_at, io, few, few_out, own):
    pos_ref, np_ref, more = few[0], few[1], few[2:]
    dx_ref, w_ref, tok_ref, qkv_ref, a_ref, ctx_ref, x_ref = io.ins
    gn_ref, grads = few_out[0], io.outs[1:]
    dctx_ref, dqkv_ref, acc_ref, scr_ref, row_ref = own
    attention_core_back(io, dx_ref, 0, w_ref, 1, tok_ref, qkv_ref, [2, 3], dctx_ref, dqkv_ref, acc_ref)
    io.need(4, 5, 6)
    attention_weight_back(io, split, pos_ref, a_ref, ctx_ref, dx_ref, dqkv_ref, grads, scr_ref)
    norm_back_rows(norm_at, dx_ref, x_ref, dqkv_ref, np_ref, w_ref, io.outs[0], gn_ref, io)
    if wired(split):
        dp, ex = split
        rows, wide = piece_rows(split), D // dp
        for n, ref in enumerate((gn_ref,) + tuple(more[:-1])):
            for i in range(2):
                for d in range(dp):
                    row_ref[(2 * n + i) * dp + d : (2 * n + i) * dp + d + 1, :] = ref[i : i + 1, d * wide : (d + 1) * wide]
        first = lax.broadcasted_iota(jnp.int32, (16, WIRE), 0) == 0
        for j in range(ex):
            for k in range(dp):
                at = jnp.bitwise_xor(pos_ref[0], j) * dp + k
                table = jnp.zeros((1, 128), F32) if j else more[-1][0:1, :]
                row = jnp.concatenate(
                    [row_ref[pl.ds(at, 1), :], table, jnp.zeros((1, WIRE - wide - 128), F32)], axis=1
                )
                grads[j % 2][j // 2, k, 4 * rows : 4 * rows + 16, :] = jnp.where(first, row, 0.0).astype(BF)
    if wired(split):
        io.done(1, 4)
        io.done(2, 4)
    else:
        io.done(1)


def last_backward(pos, dx, hidden, saved, params, tok, weights, norm_at, split, more):
    a, qkv, ctx = saved
    grads = wire_outs(split, 5) if wired(split) else [(sds((D, 4 * D), BF), 1)]
    norm, out, *grads = staged(
        functools.partial(last_back_kernel, split, norm_at),
        [(sds((PACK, D), F32), 4)] + grads,
        [(dx, 4), (weights, 1), (tok, 1), (qkv, 1), (a, 1), (ctx, 1), (hidden, 1)], [pos, params, *more],
        [sds((2, D), F32)],
        [pltpu.VMEM((PACK, D), BF), pltpu.VMEM((PACK, 3 * D), BF), pltpu.VMEM((PACK, 2 * D), F32),
         pltpu.VMEM((D, D), BF), pltpu.VMEM((8 * split[0], D // split[0]), F32)],
        flops=14_000_000_000, moved=16 << 20,
        order=[(0, 0), (1, 0), (0, 1), (0, 2), (0, 3), (2, 0), (3, 0), (4, 0), (5, 0), (6, 0)],
    )
    return norm, out, grads


def feed_kernel(io, few, few_out, own):
    (np_ref,) = few
    x_ref, up_ref, down_ref = io.ins
    h_ref, n_ref, act_ref, slope_ref = io.outs
    gain, shift = np_ref[2:3, :], np_ref[3:4, :]
    for r in range(PACK // ROWS):
        rows = slice(r * ROWS, (r + 1) * ROWS)
        io.need((0, r))
        x = x_ref[rows, :]
        unit, _ = unit_rows(x)
        n = (unit * gain + shift).astype(BF)
        n_ref[rows, :] = n
        io.need(1)
        act, slope = gelu_both(mm(n, up_ref[...]))
        act = act.astype(BF)
        act_ref[rows, :] = act
        slope_ref[rows, :] = slope.astype(BF)
        io.need(2)
        h_ref[rows, :] = x + mm(act, down_ref[...])
        for i in range(4):
            io.done(i, r)


def feed_forward(hidden, params, up, down):
    return staged(
        feed_kernel,
        [(sds((PACK, D), F32), 4), (sds((PACK, D), BF), 4), (sds((PACK, FF), BF), 4), (sds((PACK, FF), BF), 4)],
        [(hidden, 4), (up, 1), (down, 1)], [params], flops=4_300_000_000, moved=17 << 20, mib=36,
        order=[(0, 0), (1, 0), (2, 0), (0, 1), (0, 2), (0, 3)],
    )


def feed_back_kernel(split, io, few, few_out, own):
    wire = wired(split)
    pos_ref, np_ref = few
    dx_ref, down_ref, slope_ref, n_ref, act_ref, up_ref, x_ref = io.ins
    out_ref, grads = io.outs[0], io.outs[1:]
    dz_ref, dy_ref, scr_ref, tall_ref = own
    for r in range(PACK // ROWS):
        rows = slice(r * ROWS, (r + 1) * ROWS)
        io.need((0, r), 1, (2, r))
        dy = dx_ref[rows, :].astype(BF)
        dy_ref[rows, :] = dy
        dz_ref[rows, :] = (mm_t(dy, down_ref[...]) * slope_ref[rows, :].astype(F32)).astype(BF)
    io.need(3, 4)
    if wire:
        rows = piece_rows(split)
        for c in range(FF // D):
            scr_ref[...] = t_mm(n_ref[...], dz_ref[:, c * D : (c + 1) * D]).astype(BF)
            send_rows(split, pos_ref, scr_ref, *grads, c * rows, rows)
            io.done(1, c)
            io.done(2, c)
        for c in range(FF // D):
            tall_ref[c * D : (c + 1) * D, :] = t_mm(act_ref[:, c * D : (c + 1) * D], dy_ref[...]).astype(BF)
        send_rows(split, pos_ref, tall_ref, *grads, FF // D * rows, FF // D * rows)
        for c in range(FF // D):
            io.done(1, FF // D + c)
            io.done(2, FF // D + c)
    else:
        grads[0][...] = t_mm(n_ref[...], dz_ref[...]).astype(BF)
        grads[1][...] = t_mm(act_ref[...], dy_ref[...]).astype(BF)
        io.done(1)
        io.done(2)
    io.need(5, 6)
    norm_back_rows(2, dx_ref, x_ref, dz_ref, np_ref, up_ref, out_ref, few_out[0], io)


def feed_backward(pos, dx, hidden, saved, params, up, down, split):
    n, act, slope = saved
    grads = wire_outs(split, 8) if wired(split) else [(sds((D, FF), BF), 1), (sds((FF, D), BF), 1)]
    norm, out, *grads = staged(
        functools.partial(feed_back_kernel, split),
        [(sds((PACK, D), F32), 4)] + grads,
        [(dx, 4), (down, 1), (slope, 4), (n, 1), (act, 1), (up, 1), (hidden, 1)], [pos, params], [sds((2, D), F32)],
        scratch=[pltpu.VMEM((PACK, FF), BF), pltpu.VMEM((PACK, D), BF), pltpu.VMEM((D, D), BF), pltpu.VMEM((FF, D), BF)],
        order=[(0, 0), (1, 0), (2, 0)] + [(i, r) for r in range(1, 4) for i in (0, 2)] + [(n, 0) for n in range(3, 7)],
        flops=8_600_000_000, moved=24 << 20,
    )
    return norm, out, grads


def norm_back_rows(norm_at, dx_ref, x_ref, grad_ref, np_ref, w_ref, out_ref, gn_ref, io, needs=()):
    gain = np_ref[norm_at : norm_at + 1, :]
    dgain, dshift = jnp.zeros((1, D), F32), jnp.zeros((1, D), F32)
    for r in range(PACK // ROWS):
        rows = slice(r * ROWS, (r + 1) * ROWS)
        for i in needs:
            io.need((i, r))
        dnorm = mm_t(grad_ref[rows, :], w_ref[:, : grad_ref.shape[1]])
        unit, scale = unit_rows(x_ref[rows, :].astype(F32))
        dgain += jnp.sum(dnorm * unit, axis=0, keepdims=True)
        dshift += jnp.sum(dnorm, axis=0, keepdims=True)
        out_ref[rows, :] = dx_ref[rows, :] + unit_back(unit, scale, gain, dnorm)
        io.done(0, r)
    gn_ref[0:1, :] = dgain
    gn_ref[1:2, :] = dshift


def assemble_kernel(split, blocks, tall, *refs):
    dp, ex = split
    rows = piece_rows(split)
    pos_ref, pieces, outs = refs[0], refs[1 : 1 + ex], refs[1 + ex :]
    for j in range(ex):
        for k in range(dp):
            at = lax.rem(pos_ref[1] + dp - k, dp) * ex + jnp.bitwise_xor(pos_ref[0], j)
            start = pl.multiple_of(at * rows, rows)
            for c in range(blocks):
                outs[0][pl.ds(start, rows), c * WIRE : (c + 1) * WIRE] = pieces[j][k, c * rows : (c + 1) * rows, :]
            if tall:
                high = blocks * rows
                start = pl.multiple_of(at * high, high)
                outs[1][pl.ds(start, high), :] = pieces[j][k, high : 2 * high, :]


def assemble(split, pos, pieces, tall):
    outs = [sds((D, 4 * D), BF)] + ([sds((FF, D), BF)] if tall else [])
    return call(
        functools.partial(assemble_kernel, split, 4, tall), outs, pos, *pieces,
        pos=True, flops=1_000_000, moved=4 << 20, mib=24,
    )


def assemble_norm_kernel(split, *refs):
    dp, ex = split
    rows = piece_rows(split)
    pos_ref, pieces, (w_ref, np_ref, scr_ref) = refs[0], refs[1 : 1 + ex], refs[1 + ex :]
    for j in range(ex):
        for k in range(dp):
            at = lax.rem(pos_ref[1] + dp - k, dp) * ex + jnp.bitwise_xor(pos_ref[0], j)
            start = pl.multiple_of(at * rows, rows)
            for c in range(4):
                w_ref[pl.ds(start, rows), c * WIRE : (c + 1) * WIRE] = pieces[j][k, c * rows : (c + 1) * rows, :]
            scr_ref[pl.ds(start, rows), :] = pieces[j][k, 4 * rows : 5 * rows, 0:128].astype(F32)
    np_ref[...] = jnp.transpose(scr_ref[...])[:8]


def add_core_kernel(near, io, few, few_out, own):
    mine_ref, got_ref = io.ins
    for j in range(mine_ref.shape[0]):
        io.need((0, j), (1, j))
        total = (mine_ref[j].astype(F32) + got_ref[j].astype(F32)).astype(BF)
        if near:
            io.outs[j][...] = total
            io.done(j)
        else:
            io.outs[0][jnp.bitwise_xor(few[0][0] // 2, j)] = total
    if not near:
        io.done(0)


def add_near_kernel(lists, pos_ref, *refs):
    ins, outs = refs[: sum(lists)], refs[sum(lists) :]
    dp = len(outs)
    for k, out in enumerate(outs):
        at = lax.rem(pos_ref[1] + k, dp)
        first, top = 0, 0
        for n in lists:
            parts = ins[first : first + n]
            first += n
            parts = [parts[0].at[i] for i in range(parts[0].shape[0])] if n == 1 else parts
            total = parts[0][at].astype(F32)
            for part in parts[1:]:
                total = total + part[at].astype(F32)
            out[top : top + total.shape[0], :] = total.astype(BF)
            top += total.shape[0]


def add_turn_kernel(*refs):
    total = refs[0][...].astype(F32)
    for ref in refs[1:-1]:
        total = total + ref[...].astype(F32)
    refs[-1][...] = total.astype(BF)


def spread_kernel(split, *refs):
    dp, ex = split
    rows = piece_rows(split)
    pos_ref, last_ref, early_ref, qkv_ref, attn_ref, up_ref, down_ref, gn_ref, table_ref = refs

    def put(n, start, piece):
        for c in range(3):
            qkv_ref[pl.ds(start, rows), n, c * D : (c + 1) * D] = piece[c * rows : (c + 1) * rows]
        attn_ref[pl.ds(start, rows), n, :] = piece[3 * rows : 4 * rows]

    for j in range(ex):
        start, high = j * rows, j * 4 * rows
        piece = early_ref[j].astype(F32)
        for c in range(4):
            up_ref[pl.ds(start, rows), c * D : (c + 1) * D] = piece[c * rows : (c + 1) * rows]
        down_ref[pl.ds(high, 4 * rows), :] = piece[4 * rows : 8 * rows]
        put(1, start, piece[8 * rows :])
        piece = last_ref[j].astype(F32)
        put(0, j * rows, piece)
        gn_ref[j : j + 1, :] = piece[4 * rows : 4 * rows + 1, 0 : D // dp]
        table_ref[j : j + 1, :] = piece[4 * rows : 4 * rows + 1, D // dp : D // dp + 128]


def gather_near_kernel(at, io, few, few_out, own):
    (pair_ref,) = few
    size = io.outs[0].shape[0] // len(io.ins)
    tokens = lax.broadcasted_iota(jnp.int32, (size, PACK), 1).astype(F32)
    lane = lax.broadcasted_iota(jnp.int32, (size, 8), 1)
    for n, source in enumerate(io.ins):
        one = 8 * (at + n)
        base, length, first, gate, task = [pair_ref[one + i : one + i + 1, :] for i in range(5)]
        s = lax.broadcasted_iota(jnp.int32, (size, 128), 0).astype(F32) + float((at + n) * size)
        held = (base >= 0) & (s >= base) & (s < base + length)

        def take(value, held=held):
            return jnp.sum(jnp.where(held, value, 0.0), axis=1, keepdims=True)

        gate, task = take(gate), take(task + 1.0) - 1.0
        hot = jnp.where(take(first - base + s + 1.0) - 1.0 == tokens, 1.0, 0.0).astype(BF)
        io.need(n)
        rows = slice(n * size, (n + 1) * size)
        io.outs[0][rows, :] = (mm(hot, source[...]) * gate).astype(BF)
        io.outs[1][rows, :] = jnp.where(lane == 0, gate, jnp.where(lane == 1, task, 0.0))
        io.done(0, n)
        io.done(1, n)


def gather_near(pairs, sources, size, at):
    count = len(sources)
    return staged(
        functools.partial(gather_near_kernel, at),
        [(sds((count * size, D), BF), count), (sds((count * size, 8), F32), count)], [(x, 1) for x in sources], [pairs],
        flops=2 * count * size * PACK * D, moved=4 << 20, mib=20,
    )


def slots_hot(tok_ref, size, n):
    at = lax.broadcasted_iota(jnp.int32, (PACK, size), 1).astype(F32) + float(n * size)
    return jnp.where((tok_ref[:, 2:3] == at) | (tok_ref[:, 3:4] == at), 1.0, 0.0).astype(BF)


def whole(shape):
    return pl.BlockSpec(shape, lambda e: (0,) * len(shape))


def combine_out_kernel(experts, io, few, few_out, own):
    pos_ref = few[0]
    tok_ref, slot_ref, rows_ref, h_ref = io.ins
    acc_ref, size = own[0], rows_ref.shape[0] // experts
    io.need(0, 1, 2)
    for e in range(experts):
        start = pl.multiple_of(jnp.bitwise_xor(pos_ref[0], e) * size, size)
        rows = rows_ref[pl.ds(start, size), :].astype(F32)
        part = mm(slots_hot(tok_ref, size, e), (rows * slot_ref[e * size : (e + 1) * size, 1:2]).astype(BF))
        acc_ref[...] = part if e == 0 else acc_ref[...] + part
    for r in range(PACK // ROWS):
        rows = slice(r * ROWS, (r + 1) * ROWS)
        io.need((3, r))
        io.outs[0][rows, :] = (h_ref[rows, :] + acc_ref[rows, :]).astype(BF)
        io.done(0, r)


def combine_out(pos, tok, slot, rows, hidden, experts):
    return staged(
        functools.partial(combine_out_kernel, experts), [(sds((PACK, D), BF), 4)],
        [(tok, 1), (slot, 1), (rows, 1), (hidden, 4)], [pos], scratch=[pltpu.VMEM((PACK, D), F32)],
        flops=2 * 4096 * PACK * D, moved=14 << 20,
    )[0]


def expert_kernel(count, steps, *refs):
    bufs = refs[1 : 1 + count]
    dout_in, slot_ref, up_ref, down_ref = refs[1 + count : 5 + count]
    dbufs = refs[-count // 2 - 6 : -6]
    table_ref, out_ref, act_ref, du_ref, buf_ref, dout_ref = refs[-6:]
    i = pl.program_id(0)

    @pl.when(i == 0)
    def _():
        table_ref[...] = jnp.zeros_like(table_ref)

    def work(n):
        buf, dout = bufs[n][...], dout_in[...]
        buf_ref[...] = buf
        dout_ref[...] = dout
        z, dact = mm(buf, up_ref[...]), mm_t(dout, down_ref[...])
        act, slope = gelu_both(z)
        act = act.astype(BF)
        act_ref[...] = act
        out = mm(act, down_ref[...]).astype(BF)
        du = (dact * slope).astype(BF)
        du_ref[...] = du
        dbufs[n // 2][...] = mm_t(du, up_ref[...]).astype(BF)
        out_ref[...] = out
        gate, task = slot_ref[:, 0:1], slot_ref[:, 1:2]
        dgate = jnp.sum(out.astype(F32) * dout.astype(F32), axis=1, keepdims=True)
        dgate = jnp.where(task >= 0, dgate / jnp.where(task >= 0, gate, 1.0), 0.0)
        tasks = lax.broadcasted_iota(jnp.int32, (buf.shape[0], 128), 1).astype(F32)
        table_ref[0:1, :] += jnp.sum(jnp.where(tasks == task, dgate, 0.0), axis=0, keepdims=True)

    for n in range(count):
        pl.when(i // steps == n)(functools.partial(work, n))


def expert_rows(pos, bufs, dout, slot, up, down, total, at, held):
    rows = bufs[0].shape[0] // 2
    count = len(bufs)
    size = min(256, rows)
    steps = rows // size
    blocks = [
        pl.BlockSpec((size, D), lambda i, p, n=n: (jnp.clip(i - n * steps, 0, steps - 1) + n % 2 * steps, 0))
        for n in range(count)
    ]
    pairs = [
        pl.BlockSpec((size, D), lambda i, p, n=n: (jnp.clip(i - 2 * n * steps, 0, 2 * steps - 1), 0))
        for n in range(count // 2)
    ]

    def there(i, p):
        return (jnp.bitwise_xor(p[0], at + i // steps) * steps + lax.rem(i, steps), 0)

    def fixed(shape):
        return pl.BlockSpec(shape, lambda i, p: (0, 0), pipeline_mode=pl.Buffered(1))

    first = at * steps

    def tile(cols, first=first):
        return pl.BlockSpec((size, cols), lambda i, p: (i + first, 0))

    alias = {count + 5 + n: count // 2 + 1 + n for n in range(5)} if held else None
    outs = call(
        functools.partial(expert_kernel, count, steps),
        [sds((2 * rows, D), BF)] * (count // 2) + [sds((8, 128), F32)]
        + [sds((total, cols), BF) for cols in (D, FF, FF, D, D)],
        pos, *bufs, dout, slot, up, down, *held,
        grid=(count * steps,), pos=True,
        in_specs=blocks + [tile(D, 0), tile(8, 0), fixed((D, FF)), fixed((FF, D))]
        + [pl.BlockSpec(memory_space=pl.ANY)] * len(held),
        out_specs=pairs + [pl.BlockSpec((8, 128), lambda i, p: (0, 0)), pl.BlockSpec((size, D), there)]
        + [tile(FF), tile(FF), tile(D), tile(D)],
        alias=alias,
        flops=8 * rows * count * D * FF, moved=count * rows * 13 << 10,
    )
    return outs[: count // 2], outs[count // 2], outs[count // 2 + 1 :]


def expert_grad_kernel(steps, act_ref, du_ref, buf_ref, dout_ref, gup_ref, gdown_ref, up_acc, down_acc):
    i = pl.program_id(0)

    @pl.when(i == 0)
    def _():
        up_acc[...] = jnp.zeros_like(up_acc)
        down_acc[...] = jnp.zeros_like(down_acc)

    up_acc[...] += t_mm(buf_ref[...], du_ref[...])
    down_acc[...] += t_mm(act_ref[...], dout_ref[...])

    @pl.when(i == steps - 1)
    def _():
        gup_ref[...] = up_acc[...].astype(BF)
        gdown_ref[...] = down_acc[...].astype(BF)


def expert_grads(act, du, buf, dout):
    rows = buf.shape[0]
    size = 1024
    tile = lambda cols: pl.BlockSpec((size, cols), lambda i: (i, 0))
    return call(
        functools.partial(expert_grad_kernel, rows // size),
        [sds((D, FF), BF), sds((FF, D), BF)], act, du, buf, dout,
        grid=(rows // size,),
        in_specs=[tile(FF), tile(FF), tile(D), tile(D)],
        out_specs=[whole((D, FF)), whole((FF, D))],
        scratch=[pltpu.VMEM((D, FF), F32), pltpu.VMEM((FF, D), F32)],
        flops=4 * rows * D * FF, moved=44 << 20, mib=62,
    )


def route(lengths, task_ids, task_experts, capacity, task_logits, cap_slots, rel):
    sentences = lengths.shape[1]
    experts = capacity.shape[0]
    tasks = task_experts.shape[0]
    lens, ids = lengths.reshape(-1), task_ids.reshape(-1)
    ends = jnp.cumsum(lens)
    starts = ends - lens
    table = jnp.take_along_axis(task_logits, task_experts, axis=1)
    gates = jax.nn.softmax(table, axis=-1)
    hot = ids[:, None] == lax.broadcasted_iota(jnp.int32, (1, tasks), 1)
    expert = jnp.sum(jnp.where(hot[:, :, None], task_experts[None], 0), axis=1)
    gate = jnp.sum(jnp.where(hot[:, :, None], gates[None], 0.0), axis=1)
    pair_expert = expert.reshape(-1)
    pair_len = jnp.repeat(lens, 2)
    expert_hot = (pair_expert[:, None] == lax.broadcasted_iota(jnp.int32, (1, experts), 1)).astype(jnp.int32)
    running = jnp.cumsum(expert_hot * pair_len[:, None], axis=0)
    filled = jnp.sum(running * expert_hot, axis=1)
    limits = jnp.sum(expert_hot * capacity[None, :], axis=1)
    base = jnp.where(filled <= limits, jnp.bitwise_xor(pair_expert, rel) * cap_slots + filled - pair_len, -1)
    base_two = base.reshape(sentences, 2)

    def lanes(rows):
        rows = jnp.stack([row.astype(F32) for row in rows])
        return jnp.pad(rows, ((0, 8 - rows.shape[0]), (0, 128 - rows.shape[1])))

    sent = lanes([starts, ends, base_two[:, 0], base_two[:, 1]])
    pair = lanes([base, pair_len, jnp.repeat(starts, 2), gate.reshape(-1), jnp.repeat(ids, 2)])
    slots = experts * cap_slots
    tok, slot = call(
        functools.partial(route_kernel, slots),
        [sds((PACK, 8), F32), sds((slots, 8), F32)], sent, pair,
        flops=1_000_000, moved=3 << 20, mib=24,
    )
    return tok, slot, pair, gates


EXPERT = ("xy", "core")
BOTH = ("dp", "xy", "core")


def flip(rows, j, ex):
    return lax.ppermute(rows, EXPERT, [(i, i ^ j) for i in range(ex)])


def turn(rows, k, dp):
    return lax.ppermute(rows, "dp", [(i, (i + k) % dp) for i in range(dp)])


def tie(value, *after):
    return lax.optimization_barrier((value,) + after)[0]


def send_even(here, ex):
    return [here] + [flip(here, j, ex) for j in range(2, ex, 2)]


def send_core(even, ex):
    got = []
    for one in even:
        got += [one, flip(one, 1, ex)]
    return got


def add_core(pos, own, got, near=False):
    parts = own.shape[0]
    outs = [(sds(own.shape[1:], BF), 1)] * parts if near else [(sds(own.shape, BF), parts)]
    got = staged(
        functools.partial(add_core_kernel, near), outs, [(own, parts), (got, parts)], [pos],
        order=[(i, j) for j in range(parts) for i in range(2)], flops=1_000_000, moved=own.size * 6,
    )
    return got if near else got[0]


def add_near(pos, *lists):
    lists = [one if isinstance(one, list) else [one] for one in lists]
    rows = sum(one[0].shape[-2] for one in lists)
    dp = lists[0][0].shape[-3]
    return call(
        functools.partial(add_near_kernel, [len(one) for one in lists]), [sds((rows, WIRE), BF)] * dp,
        pos, *sum(lists, []), pos=True, flops=1_000_000, moved=rows << 14,
    )


def send_near(sums, ex):
    return [sums[0]] + [flip(sums[j], 2 * j, ex) for j in range(1, ex // 2)]


def send_turn(sums, dp):
    return [sums[0]] + [turn(sums[k], k, dp) for k in range(1, dp)]


def add_turn(got):
    return call(add_turn_kernel, sds(got[0].shape, BF), *got, flops=1_000_000, moved=got[0].size * 10, mib=62)


def swap(parts, axis):
    return lax.all_to_all(parts, axis, split_axis=0, concat_axis=0, tiled=True)


def local(n_dp, n_ex, hidden_in, lengths, task_ids, task_experts, capacity, task_logits, norm_params,
          w_qkv, w_attn, w_up, w_down, expert_up, expert_down, cotangent):
    experts = capacity.shape[0]
    cap_slots = max(4 * hidden_in.shape[0] // experts, 2 * MOST_LEN)
    slots = experts * cap_slots
    me, here = lax.axis_index(EXPERT), lax.axis_index("dp")
    pos = jnp.stack([me, here]).astype(jnp.int32)
    split = (n_dp, n_ex)
    wire = wired(split)

    def mine(shard):
        rows = shard.shape[0] // n_ex
        return lax.dynamic_slice_in_dim(shard, me * rows, rows, 0)

    def exchange(pair, j):
        return flip(pair, j, n_ex) if j else pair

    tok, slot, pair, gates = route(lengths, task_ids, task_experts, capacity, task_logits, cap_slots, me)
    if wire:
        rows = piece_rows(split)

        def blocks(wide):
            return [wide[:, c * WIRE : (c + 1) * WIRE] for c in range(wide.shape[1] // WIRE)]

        norms = jnp.pad(mine(norm_params), ((0, 0), (0, WIRE - 8)))
        qkv, attn = mine(w_qkv), mine(w_attn)
        piece = blocks(qkv[:, 0]) + [attn[:, 0], norms] + blocks(mine(w_up)) + [mine(w_down)]
        piece = jnp.concatenate(piece + blocks(qkv[:, 1]) + [attn[:, 1]])
        parts = [piece] + [turn(piece, k, n_dp) for k in range(1, n_dp)]
        expert_up, expert_down = tie(expert_up, *parts[1:]), tie(expert_down, *parts[1:])
        zero, feed, one = [
            jnp.stack([part[lo * rows : hi * rows] for part in parts]) for lo, hi in ((0, 5), (5, 13), (13, 17))
        ]
        cots = [cotangent, flip(cotangent, 2, n_ex), flip(cotangent, 4, n_ex)]
        zero = send_even(tie(zero, *cots[1:]), n_ex)
        pairs = pair
        j = 1
        while j < n_ex:
            pairs = jnp.concatenate([pairs, flip(pairs, j, n_ex)])
            j *= 2
        feed = send_even(tie(feed, *zero[1:]), n_ex)
        zero = send_core([tie(part, tok, pairs) for part in zero], n_ex)
        groups = [(0, 2), (2, 6), (6, 8)]

        def gather_group(lo, hi, pairs):
            sources = sum([[cots[j], flip(cots[j], 1, n_ex)] for j in range(lo // 2, hi // 2)], [])
            return gather_near(pairs, sources, cap_slots, lo)

        near = [gather_group(*group, pairs) for group in groups[:2]]
        attn_zero, params = call(
            functools.partial(assemble_norm_kernel, split), [sds((D, 4 * D), BF), sds((8, D), F32)], pos, *zero,
            scratch=[pltpu.VMEM((D, 128), F32)], pos=True, flops=1_000_000, moved=4 << 20, mib=24,
        )
        fwd = tie(hidden_in, *sum(near, []))
        h1, *saved_zero = attention_forward(fwd, params, tok, attn_zero, 0)
        one = send_even(tie(one, h1, *feed[1:]), n_ex)
        feed = send_core([tie(part, h1) for part in feed], n_ex)
        up, down = assemble(split, pos, feed, True)
        h2, *saved_feed = feed_forward(h1, params, up, down)
        one = [tie(part, h2) for part in one]
        cots.append(flip(tie(cotangent, *one[1:]), 6, n_ex))
        one = send_core(one, n_ex)
        attn_one = assemble(split, pos, one, False)[0]
    else:

        def gather_all(shard):
            return lax.all_gather(mine(shard), BOTH, axis=0, tiled=True)

        params = lax.all_gather(norm_params, "dp", axis=0, tiled=True).astype(F32).T
        attn_zero = gather_all(jnp.concatenate([w_qkv[:, 0], w_attn[:, 0]], axis=1))
        up, down = gather_all(w_up), gather_all(w_down)
        attn_one = gather_all(jnp.concatenate([w_qkv[:, 1], w_attn[:, 1]], axis=1))
        h1, *saved_zero = attention_forward(hidden_in, params, tok, attn_zero, 0)
        h2, *saved_feed = feed_forward(h1, params, up, down)
        pairs = pair
        j = 1
        while j < n_ex:
            pairs = jnp.concatenate([pairs, flip(pairs, j, n_ex)])
            j *= 2
        groups = [(j, j + 4) for j in range(0, n_ex, 4)]
        cots = [cotangent] + [flip(cotangent, j, n_ex) for j in range(1, n_ex)]
        near = [gather_near(pairs, cots[lo:hi], cap_slots, lo) for lo, hi in groups]
    up_expert = lax.all_gather(expert_up[0], "dp", axis=0, tiled=True)
    down_expert = lax.all_gather(expert_down[0], "dp", axis=0, tiled=True)
    h3, *saved_one = attention_forward(h2, params, tok, attn_one, 4, slot, experts)
    saved_one, sent = saved_one[:3], saved_one[3:]
    sums, held, table = [], (), 0.0
    if wire:
        sent = [tie(pair, cots[-1]) for pair in sent]
    bufs = {j: exchange(sent[j // 2], j) for j in range(0, groups[-1][0], 2)}
    for n, (lo, hi) in enumerate(groups):
        if wire and n == 1:
            near.append(gather_group(*groups[2], tie(pairs, sums[0])))
        dout, slot_near = near[n]
        if n == 1:
            for j in range(groups[-1][0], n_ex, 2):
                bufs[j] = exchange(tie(sent[j // 2], *[bufs[i] for i in range(lo, hi, 2)], *sums[:1]), j)
        for j in range(lo, hi, 2):
            bufs[j + 1] = flip(tie(bufs[j], *sums[-1:], *near[-1]), 1, n_ex)
        back, part, held = expert_rows(
            pos, [bufs[j] for j in range(lo, hi)], dout, slot_near, up_expert, down_expert, slots, lo, held
        )
        sums += back
        table = table + part
    out, *held = held
    back = [exchange(pair, 2 * j) for j, pair in enumerate(sums)]
    gup_expert, gdown_expert = expert_grads(*held)
    far = [flip(tie(pair, gup_expert), 1, n_ex) for pair in back]
    dbuf_home = sum([list(both) for both in zip(back, far)], [])
    out_home = swap(tie(out, *back, gup_expert).reshape(experts, cap_slots, D), EXPERT).reshape(-1, D)
    gn_one, gn_moe, dx, g_one = first_backward(
        pos, dbuf_home, h3, cotangent, h2, saved_one, params, tok, attn_one, 4, split
    )
    expert_up_sum = lax.psum_scatter(tie(gup_expert, gn_moe), "dp", scatter_dimension=0, tiled=True)
    expert_down_sum = lax.psum_scatter(tie(gdown_expert, gn_moe), "dp", scatter_dimension=0, tiled=True)
    if wire:
        got_one = add_core(pos, g_one[0], flip(g_one[1], 1, n_ex), True)
        dx = tie(dx, got_one[0])
        got_one = send_near(got_one, n_ex)
    gn_feed, dx, g_feed = feed_backward(pos, dx, h1, saved_feed, params, up, down, split)
    if wire:
        got_feed = flip(tie(g_feed[1], out_home, *got_one[1:]), 1, n_ex)
        sum_feed = add_core(pos, g_feed[0], got_feed)
        dx = tie(dx, sum_feed)
        got_feed = swap(sum_feed, "xy")
    gn_zero, grad_in, g_zero = last_backward(
        pos, dx, hidden_in, saved_zero, params, tok, attn_zero, 0, split, (gn_feed, gn_one, gn_moe, table)
    )
    if wire:
        sum_zero = add_core(pos, g_zero[0], flip(g_zero[1], 1, n_ex))
        early = add_near(pos, tie(got_feed, sum_zero), got_one)
        h3 = tie(h3, sum_zero)
        sum_zero = swap(sum_zero, "xy")
        early = send_turn(early, n_dp)
    hidden_out = combine_out(pos, tok, slot, out_home, h3, experts)
    if wire:
        sum_zero = add_near(pos, tie(sum_zero, hidden_out))
        early = lax.all_gather(add_turn([tie(one, sum_zero[0]) for one in early]), EXPERT, axis=0)
        expert_up_sum, expert_down_sum = tie(expert_up_sum, sum_zero[0]), tie(expert_down_sum, sum_zero[0])
        expert_up_sum, expert_down_sum = expert_up_sum.astype(F32), expert_down_sum.astype(F32)
        sum_zero = send_turn(sum_zero, n_dp)
        sum_zero = add_turn([tie(part, expert_up_sum, expert_down_sum) for part in sum_zero])
        last = lax.all_gather(sum_zero, EXPERT, axis=0)
        rows = D // n_dp
        grad_qkv, grad_attn, grad_up, grad_down, gn, sums = call(
            functools.partial(spread_kernel, split),
            [sds((rows, 2, 3 * D), F32), sds((rows, 2, D), F32), sds((rows, FF), F32), sds((FF // n_dp, D), F32),
             sds((8, rows), F32), sds((experts, 128), F32)],
            pos, last, early,
            pos=True, flops=1_000_000, moved=7 << 20, mib=32,
        )
        gn = gn.T
    else:
        small = jnp.concatenate([gn_zero, gn_feed, gn_one, gn_moe], axis=0)
        table = lax.dynamic_update_slice_in_dim(jnp.zeros((experts, 128), F32), table[:1], me, 0)
        small = jnp.concatenate([small, jnp.pad(table, ((0, 0), (0, D - 128)))], axis=0)
        small = lax.psum(small, BOTH)
        gn = lax.dynamic_slice_in_dim(small[:8], here * (D // n_dp), D // n_dp, 1).T
        sums = small[8:]

        def reduce_all(grad):
            rows = grad.shape[0] // (n_dp * n_ex)
            grad = grad.reshape(n_dp, n_ex, rows, -1).transpose(1, 0, 2, 3).reshape(grad.shape)
            part = lax.psum_scatter(grad, EXPERT, scatter_dimension=0, tiled=True)
            part = lax.psum_scatter(part, "dp", scatter_dimension=0, tiled=True)
            return lax.all_gather(part, EXPERT, axis=0, tiled=True).astype(F32)

        g_one, grad_up, grad_down, g_zero = [reduce_all(g) for g in (*g_one, *g_feed, *g_zero)]
        grad_qkv = jnp.stack([g_zero[:, : 3 * D], g_one[:, : 3 * D]], axis=1)
        grad_attn = jnp.stack([g_zero[:, 3 * D :], g_one[:, 3 * D :]], axis=1)
    sums = sums[:, : task_logits.shape[0]].T
    hot = task_experts[:, :, None] == lax.broadcasted_iota(jnp.int32, (1, 1, experts), 2)
    pair_sum = jnp.sum(jnp.where(hot, sums[:, None, :], 0.0), axis=2)
    lean = gates[:, 0] * gates[:, 1] * (pair_sum[:, 0] - pair_sum[:, 1])
    grad_logits = jnp.where(hot[:, 0], lean[:, None], 0.0) - jnp.where(hot[:, 1], lean[:, None], 0.0)
    return (
        hidden_out, grad_in, grad_logits, gn, grad_qkv, grad_attn, grad_up, grad_down,
        expert_up_sum.astype(F32)[None], expert_down_sum.astype(F32)[None],
    )


def solution(mesh):
    n_dp, n_ex = mesh.shape["dp"], mesh.shape["expert"]
    mesh = jax.sharding.Mesh(mesh.devices.reshape(n_dp, n_ex // 2, 2), BOTH)
    token = P(BOTH, None)
    expert = P(EXPERT, "dp", None)
    in_specs = (
        token, token, token, P(), P(), P(), P("dp", None), P("dp", None, None), P("dp", None, None),
        P("dp", None), P("dp", None), expert, expert, token,
    )
    out_specs = (
        token, token, P(), P("dp", None), P("dp", None, None), P("dp", None, None), P("dp", None), P("dp", None),
        expert, expert,
    )
    step = functools.partial(local, n_dp, n_ex)
    return jax.shard_map(step, mesh=mesh, in_specs=in_specs, out_specs=out_specs, check_vma=False)
```

```python
import functools

import jax
import jax.numpy as jnp
from jax import lax
from jax.experimental import pallas as pl
from jax.experimental.pallas import tpu as pltpu
from jax.sharding import PartitionSpec as P

D = 512
FF = 2048
HEADS = 8
HEAD = D // HEADS
PACK = 1024
MOST_LEN = 64
ROWS = 256
QB = 128
KB = QB + 2 * MOST_LEN
EPS = 1e-05
BLOCKED = -1e30
BF = jnp.bfloat16
F32 = jnp.float32
GELU_C = 0.7978845608028654
GELU_A = 0.044715


COST = 2


def mm(left, right):
    return lax.dot_general(left, right, (((1,), (0,)), ((), ())), preferred_element_type=F32)


def mm_t(left, right):
    return lax.dot_general(left, right, (((1,), (1,)), ((), ())), preferred_element_type=F32)


def t_mm(left, right):
    return lax.dot_general(left, right, (((0,), (0,)), ((), ())), preferred_element_type=F32)


def unit_rows(hidden):
    centered = hidden - jnp.mean(hidden, axis=-1, keepdims=True)
    spread = jnp.mean(centered * centered, axis=-1, keepdims=True)
    scale = lax.rsqrt(spread + EPS)
    return centered * scale, scale


def unit_back(unit, scale, gain, grad):
    inner = grad * gain
    first = jnp.mean(inner, axis=-1, keepdims=True)
    second = jnp.mean(inner * unit, axis=-1, keepdims=True)
    return scale * (inner - first - unit * second)


def gelu_both(z):
    square = z * z
    half = 0.5 + 0.5 * jnp.tanh(z * (GELU_C + GELU_C * GELU_A * square))
    act = z * half
    return act, half + (act - act * half) * (2.0 * GELU_C + 6.0 * GELU_C * GELU_A * square)


def call(kernel, out_shape, *args, grid=None, in_specs=None, out_specs=None, scratch=(), mib=62, flops=0, moved=0,
         alias=None, pos=False):
    extra = {}
    if grid is not None and pos:
        extra["grid_spec"] = pltpu.PrefetchScalarGridSpec(
            num_scalar_prefetch=1, grid=grid, in_specs=in_specs, out_specs=out_specs, scratch_shapes=scratch
        )
    else:
        extra["scratch_shapes"] = scratch
        if grid is not None:
            extra.update(grid=grid, in_specs=in_specs, out_specs=out_specs)
        elif pos:
            held = pl.BlockSpec(memory_space=pltpu.VMEM)
            extra["in_specs"] = [pl.BlockSpec(memory_space=pltpu.SMEM)] + [held] * (len(args) - 1)
    if alias:
        extra["input_output_aliases"] = alias
    return pl.pallas_call(
        kernel,
        out_shape=out_shape,
        compiler_params=pltpu.CompilerParams(vmem_limit_bytes=mib << 20),
        cost_estimate=pl.CostEstimate(flops=flops // COST, bytes_accessed=moved // COST, transcendentals=0),
        **extra,
    )(*args)


def sds(shape, dtype):
    return jax.ShapeDtypeStruct(shape, dtype)


WIRE = 512


def piece_rows(split):
    dp, ex = split
    return D // (dp * ex)


def wired(split):
    dp, ex = split
    return piece_rows(split) % 16 == 0 and ex == 8


def near(split, pos_ref, j, k):
    return k * split[1] + jnp.bitwise_xor(pos_ref[0], j)


def send_rows(split, pos_ref, scr_ref, own_ref, core_ref, at, rows):
    dp, ex = split
    for j in range(ex):
        out = core_ref if j % 2 else own_ref
        for k in range(dp):
            start = pl.multiple_of(near(split, pos_ref, j, k) * rows, rows)
            out[j // 2, k, at : at + rows, :] = scr_ref[pl.ds(start, rows), :]


def wire_shapes(split, blocks):
    dp, ex = split
    shape = (ex // 2, dp, blocks * piece_rows(split), WIRE)
    return [sds(shape, BF), sds(shape, BF)]


WINDOW = 12 << 20


class Stage:
    def __init__(self, ins, outs, split_in, split_out, hold_in, hold_out, sem_in, sem_out, order, axes):
        self.ins, self.outs = hold_in, hold_out
        self.split_in, self.split_out, self.axes = split_in, split_out, axes
        self.out_hbm, self.out_sem, self.sent = outs, sem_out, []
        self.got, self.begun, self.copies, self.bytes = set(), 0, {}, {}
        order = order or [(i, r) for i, parts in enumerate(split_in) for r in range(parts)]
        for n, (i, r) in enumerate(order):
            rows = self.rows(hold_in[i], split_in[i], r)
            self.copies[i, r] = pltpu.make_async_copy(ins[i].at[rows], hold_in[i].at[rows], sem_in.at[n])
            self.bytes[i, r] = hold_in[i].size * hold_in[i].dtype.itemsize // split_in[i]
        self.order = order
        self.ahead(0)

    def rows(self, ref, parts, r, axis=0):
        size = ref.shape[axis] // parts
        return (slice(None),) * axis + (pl.ds(r * size, size),)

    def ahead(self, least):
        while self.begun < len(self.order):
            flying = sum(self.bytes[key] for key in self.order[: self.begun] if key not in self.got)
            if self.begun >= least and flying >= WINDOW:
                break
            self.copies[self.order[self.begun]].start()
            self.begun += 1

    def need(self, *which):
        for i in which:
            i, r = i if isinstance(i, tuple) else (i, None)
            for k in range(self.split_in[i]) if r is None else [r]:
                if (i, k) not in self.got:
                    self.ahead(self.order.index((i, k)) + 1)
                    self.copies[i, k].wait()
                    self.got.add((i, k))
                    self.ahead(0)

    def done(self, i, r=None):
        parts = self.split_out[i]
        for k in range(parts) if r is None else [r]:
            rows = self.rows(self.outs[i], parts, k, self.axes[i])
            sem = self.out_sem.at[sum(self.split_out[:i]) + k]
            copy = pltpu.make_async_copy(self.outs[i].at[rows], self.out_hbm[i].at[rows], sem)
            copy.start()
            self.sent.append(copy)

    def finish(self):
        self.need(*self.order)
        for copy in self.sent:
            copy.wait()


def staged(body, outs, ins, small=(), small_outs=(), scratch=(), flops=0, moved=0, order=None, mib=62):
    arrays, split_in = [x for x, _ in ins], [n for _, n in ins]
    shapes, split_out = [x[0] for x in outs], [x[1] for x in outs]
    axes = [x[2] if len(x) > 2 else 0 for x in outs]

    def kernel(*refs):
        at = 0
        groups = []
        for n in (len(small), len(arrays), len(small_outs), len(shapes), len(arrays), len(shapes), len(scratch), 2):
            groups.append(refs[at : at + n])
            at += n
        few, hbm_in, few_out, hbm_out, hold_in, hold_out, own, (sem_in, sem_out) = groups
        stage = Stage(hbm_in, hbm_out, split_in, split_out, hold_in, hold_out, sem_in, sem_out, order, axes)
        body(stage, few, few_out, own)
        stage.finish()

    space = [pl.BlockSpec(memory_space=pltpu.SMEM if x.dtype == jnp.int32 else pltpu.VMEM) for x in small]
    got = pl.pallas_call(
        kernel,
        out_shape=list(small_outs) + shapes,
        in_specs=space + [pl.BlockSpec(memory_space=pl.ANY)] * len(arrays),
        out_specs=[pl.BlockSpec(memory_space=pltpu.VMEM)] * len(small_outs)
        + [pl.BlockSpec(memory_space=pl.ANY)] * len(shapes),
        scratch_shapes=[pltpu.VMEM(x.shape, x.dtype) for x in arrays + shapes]
        + list(scratch)
        + [pltpu.SemaphoreType.DMA((sum(split_in),)), pltpu.SemaphoreType.DMA((max(sum(split_out), 1),))],
        compiler_params=pltpu.CompilerParams(vmem_limit_bytes=mib << 20),
        cost_estimate=pl.CostEstimate(flops=flops // COST, bytes_accessed=moved // COST, transcendentals=0),
    )(*small, *arrays)
    return list(got)


def route_kernel(slots, sent_ref, pair_ref, tok_ref, slot_ref):
    t = lax.broadcasted_iota(jnp.int32, (PACK, 128), 0).astype(F32)
    start, end = sent_ref[0:1, :], sent_ref[1:2, :]
    member = (t >= start) & (t < end)

    def pick(value):
        return jnp.sum(jnp.where(member, value, 0.0), axis=1, keepdims=True)

    lane = lax.broadcasted_iota(jnp.int32, (PACK, 8), 1)
    out = jnp.where(lane == 0, pick(start), 0.0)
    out = jnp.where(lane == 1, pick(end), out)
    for k in range(2):
        base = sent_ref[2 + k : 3 + k, :]
        slot = pick(jnp.where(base >= 0, base - start + t + 1.0, 0.0)) - 1.0
        out = jnp.where(lane == 2 + k, slot, out)
    tok_ref[...] = out
    chunk = 512
    base, length, first = pair_ref[0:1, :], pair_ref[1:2, :], pair_ref[2:3, :]
    gate, task = pair_ref[3:4, :], pair_ref[4:5, :]
    for i in range(slots // chunk):
        s = lax.broadcasted_iota(jnp.int32, (chunk, 128), 0).astype(F32) + float(i * chunk)
        held = (base >= 0) & (s >= base) & (s < base + length)

        def take(value, held=held):
            return jnp.sum(jnp.where(held, value, 0.0), axis=1, keepdims=True)

        lane = lax.broadcasted_iota(jnp.int32, (chunk, 8), 1)
        out = jnp.where(lane == 0, take(first - base + s + 1.0) - 1.0, 0.0)
        out = jnp.where(lane == 1, take(gate), out)
        out = jnp.where(lane == 2, take(task + 1.0) - 1.0, out)
        slot_ref[i * chunk : (i + 1) * chunk, :] = out


def head_halves(block):
    low = lax.broadcasted_iota(jnp.int32, (1, 128), 1) < HEAD
    zero = jnp.zeros_like(block)
    return jnp.concatenate([jnp.where(low, block, zero), jnp.where(low, zero, block)], axis=0)


def merge_halves(stacked):
    low = lax.broadcasted_iota(jnp.int32, (1, 128), 1) < HEAD
    return jnp.where(low, stacked[:QB], stacked[QB:])


def key_start(i):
    return jnp.clip(i * QB - MOST_LEN, 0, PACK - KB)


def attention_kernel(norm_at, last, x_ref, np_ref, tok_ref, w_ref, *refs):
    if last:
        slot_ref, h_ref, a_ref, qkv_ref, ctx_ref = refs[:5]
        pair_refs, c_ref = refs[5:-1], refs[-1]
    else:
        h_ref, a_ref, qkv_ref, ctx_ref = refs
    gain, shift = np_ref[norm_at : norm_at + 1, :], np_ref[norm_at + 1 : norm_at + 2, :]
    for r in range(PACK // ROWS):
        rows = slice(r * ROWS, (r + 1) * ROWS)
        unit, _ = unit_rows(x_ref[rows, :].astype(F32))
        a = (unit * gain + shift).astype(BF)
        a_ref[rows, :] = a
        qkv_ref[rows, :] = mm(a, w_ref[:, 0 : 3 * D]).astype(BF)

    def block(i, carry):
        q0 = pl.multiple_of(i * QB, QB)
        k0 = pl.multiple_of(key_start(i), MOST_LEN)
        start, end = tok_ref[pl.ds(q0, QB), 0:1], tok_ref[pl.ds(q0, QB), 1:2]
        key = (lax.broadcasted_iota(jnp.int32, (QB, KB), 1) + k0).astype(F32)
        mask = (key >= start) & (key < end)
        mask = jnp.concatenate([mask, mask], axis=0)
        at = [pair * 128 for pair in range(HEADS // 2)]
        q = [head_halves(qkv_ref[pl.ds(q0, QB), a : a + 128] * BF(HEAD**-0.5)) for a in at]
        k = [qkv_ref[pl.ds(k0, KB), D + a : D + a + 128] for a in at]
        v = [qkv_ref[pl.ds(k0, KB), 2 * D + a : 2 * D + a + 128] for a in at]
        scores = [jnp.where(mask, mm_t(x, y), BLOCKED) for x, y in zip(q, k)]
        raised = [jnp.exp(x - jnp.max(x, axis=1, keepdims=True)) for x in scores]
        probs = [(x * (1.0 / jnp.sum(x, axis=1, keepdims=True))).astype(BF) for x in raised]
        ctx = [merge_halves(mm(x, y)).astype(BF) for x, y in zip(probs, v)]
        ctx_ref[pl.ds(q0, QB), :] = jnp.concatenate(ctx, axis=1)
        return carry

    lax.fori_loop(0, PACK // QB, block, 0, unroll=4)
    for r in range(PACK // ROWS):
        rows = slice(r * ROWS, (r + 1) * ROWS)
        h = x_ref[rows, :].astype(F32) + mm(ctx_ref[rows, :], w_ref[:, 3 * D : 4 * D])
        h_ref[rows, :] = h
        if last:
            unit, _ = unit_rows(h)
            c_ref[rows, :] = (unit * np_ref[6:7, :] + np_ref[7:8, :]).astype(BF)
    if last:
        size = pair_refs[0].shape[0] // 2
        tokens = lax.broadcasted_iota(jnp.int32, (size, PACK), 1).astype(F32)
        for n in range(2 * len(pair_refs)):
            hot = jnp.where(slot_ref[n * size : (n + 1) * size, 0:1] == tokens, 1.0, 0.0).astype(BF)
            pair_refs[n // 2][n % 2 * size : (n % 2 + 1) * size, :] = mm(hot, c_ref[...]).astype(BF)


def attention_forward(hidden, params, tok, weights, norm_at, slot=None, experts=0):
    last = slot is not None
    outs = [sds((PACK, D), F32), sds((PACK, D), BF), sds((PACK, 3 * D), BF), sds((PACK, D), BF)]
    more, scratch = (), ()
    if last:
        outs += [sds((2 * slot.shape[0] // experts, D), BF)] * (experts // 2)
        more, scratch = (slot,), [pltpu.VMEM((PACK, D), BF)]
    return call(
        functools.partial(attention_kernel, norm_at, last),
        outs, hidden, params, tok, weights, *more, scratch=scratch,
        flops=6_000_000_000, moved=12 << 20, mib=40,
    )


def combine_grads(io, tok_ref, h_ref, cot_ref, blocks, np_ref, dx_ref, gn_ref, needs):
    for e, ref in enumerate(blocks):
        size = ref.shape[0] // 2
        io.need((needs[2 + e], e % 2))
        part = mm(slots_hot(tok_ref, size, e), ref[e % 2 * size : (e % 2 + 1) * size, :])
        dx_ref[...] = part if e == 0 else dx_ref[...] + part
    io.need(*needs[:2])
    dgain, dshift = jnp.zeros((1, D), F32), jnp.zeros((1, D), F32)
    for r in range(PACK // ROWS):
        rows = slice(r * ROWS, (r + 1) * ROWS)
        dnorm = dx_ref[rows, :]
        unit, scale = unit_rows(h_ref[rows, :])
        dgain += jnp.sum(dnorm * unit, axis=0, keepdims=True)
        dshift += jnp.sum(dnorm, axis=0, keepdims=True)
        dx_ref[rows, :] = cot_ref[rows, :].astype(F32) + unit_back(unit, scale, np_ref[6:7, :], dnorm)
    gn_ref[0:1, :] = dgain
    gn_ref[1:2, :] = dshift


def attention_core_back(io, dx_ref, dx_at, w_ref, w_at, tok_ref, qkv_ref, at_need, dctx_ref, dqkv_ref, acc_ref):
    io.need(w_at)
    for r in range(PACK // ROWS):
        rows = slice(r * ROWS, (r + 1) * ROWS)
        if dx_at is not None:
            io.need((dx_at, r))
        dctx_ref[rows, :] = mm_t(dx_ref[rows, :].astype(BF), w_ref[:, 3 * D : 4 * D]).astype(BF)
    acc_ref[...] = jnp.zeros_like(acc_ref)
    io.need(*at_need)

    def block(i, carry):
        q0 = pl.multiple_of(i * QB, QB)
        k0 = pl.multiple_of(key_start(i), MOST_LEN)
        start, end = tok_ref[pl.ds(k0, KB), 0:1], tok_ref[pl.ds(k0, KB), 1:2]
        query = (lax.broadcasted_iota(jnp.int32, (KB, QB), 1) + q0).astype(F32)
        mask = (query >= start) & (query < end)
        mask = jnp.concatenate([mask, mask], axis=1)
        at = [pair * 128 for pair in range(HEADS // 2)]
        q = [head_halves(qkv_ref[pl.ds(q0, QB), a : a + 128] * BF(HEAD**-0.5)) for a in at]
        k = [qkv_ref[pl.ds(k0, KB), D + a : D + a + 128] for a in at]
        v = [qkv_ref[pl.ds(k0, KB), 2 * D + a : 2 * D + a + 128] for a in at]
        g = [head_halves(dctx_ref[pl.ds(q0, QB), a : a + 128]) for a in at]
        scores = [jnp.where(mask, mm_t(x, y), BLOCKED) for x, y in zip(k, q)]
        dprobs = [mm_t(x, y) for x, y in zip(v, g)]
        raised = [jnp.exp(x - jnp.max(x, axis=0, keepdims=True)) for x in scores]
        probs = [x * (1.0 / jnp.sum(x, axis=0, keepdims=True)) for x in raised]
        delta = [jnp.sum(x * y, axis=0, keepdims=True) for x, y in zip(probs, dprobs)]
        dscores = [(x * (y - z)).astype(BF) for x, y, z in zip(probs, dprobs, delta)]
        dq = [(merge_halves(t_mm(x, y)) * (HEAD**-0.5)).astype(BF) for x, y in zip(dscores, k)]
        dk = [mm(x, y) for x, y in zip(dscores, q)]
        dv = [mm(x.astype(BF), y) for x, y in zip(probs, g)]
        dqkv_ref[pl.ds(q0, QB), 0:D] = jnp.concatenate(dq, axis=1)
        acc_ref[pl.ds(k0, KB), :] += jnp.concatenate(dk + dv, axis=1)
        return carry

    lax.fori_loop(0, PACK // QB, block, 0, unroll=4)
    dqkv_ref[:, D:] = acc_ref[...].astype(BF)


def wire_outs(split, blocks):
    return [(x, blocks, 2) for x in wire_shapes(split, blocks)]


def attention_weight_back(io, split, pos_ref, a_ref, ctx_ref, dx_ref, dqkv_ref, grads, scr_ref):
    rows = piece_rows(split)
    for c in range(4):
        cols = slice(c * D, (c + 1) * D)
        if c < 3:
            grad = t_mm(a_ref[...], dqkv_ref[:, cols]).astype(BF)
        else:
            grad = t_mm(ctx_ref[...], dx_ref[...].astype(BF)).astype(BF)
        if wired(split):
            scr_ref[...] = grad
            send_rows(split, pos_ref, scr_ref, grads[0], grads[1], c * rows, rows)
            io.done(1, c)
            io.done(2, c)
        else:
            grads[0][:, cols] = grad


def first_back_kernel(split, norm_at, io, few, few_out, own):
    pos_ref, np_ref = few
    tok_ref, h_ref, cot_ref, w_ref, qkv_ref, a_ref, ctx_ref, x_ref = io.ins[:8]
    dx_ref, dctx_ref, dqkv_ref, acc_ref, scr_ref = own
    blocks = io.ins[8:]
    io.need(0)
    combine_grads(io, tok_ref, h_ref, cot_ref, blocks, np_ref, dx_ref, few_out[1], [1, 2] + list(range(8, 8 + len(blocks))))
    attention_core_back(io, dx_ref, None, w_ref, 3, tok_ref, qkv_ref, [4], dctx_ref, dqkv_ref, acc_ref)
    io.need(5, 6, 7)
    attention_weight_back(io, split, pos_ref, a_ref, ctx_ref, dx_ref, dqkv_ref, io.outs[1:], scr_ref)
    if not wired(split):
        io.done(1)
    norm_back_rows(norm_at, dx_ref, x_ref, dqkv_ref, np_ref, w_ref, io.outs[0], few_out[0], io)


def first_backward(pos, blocks, h, cotangent, hidden, saved, params, tok, weights, norm_at, split):
    a, qkv, ctx = saved
    grads = wire_outs(split, 4) if wired(split) else [(sds((D, 4 * D), BF), 1)]
    ins = [(x, 1) for x in (tok, h, cotangent, weights, qkv, a, ctx, hidden)] + [(x, 2) for x in blocks]
    order = [(0, 0)] + [(8 + n, n % 2) for n in range(len(blocks))] + [(n, 0) for n in range(1, 8)]
    norm, norm_moe, out, *grads = staged(
        functools.partial(first_back_kernel, split, norm_at),
        [(sds((PACK, D), F32), 4)] + grads, ins, [pos, params], [sds((2, D), F32)] * 2,
        [pltpu.VMEM((PACK, D), F32), pltpu.VMEM((PACK, D), BF), pltpu.VMEM((PACK, 3 * D), BF),
         pltpu.VMEM((PACK, 2 * D), F32), pltpu.VMEM((D, D), BF)],
        flops=16_000_000_000, moved=20 << 20, order=order,
    )
    return norm, norm_moe, out, grads


def last_back_kernel(split, norm_at, io, few, few_out, own):
    pos_ref, np_ref, more = few[0], few[1], few[2:]
    dx_ref, w_ref, tok_ref, qkv_ref, a_ref, ctx_ref, x_ref = io.ins
    gn_ref, grads = few_out[0], io.outs[1:]
    dctx_ref, dqkv_ref, acc_ref, scr_ref, row_ref = own
    attention_core_back(io, dx_ref, 0, w_ref, 1, tok_ref, qkv_ref, [2, 3], dctx_ref, dqkv_ref, acc_ref)
    io.need(4, 5, 6)
    attention_weight_back(io, split, pos_ref, a_ref, ctx_ref, dx_ref, dqkv_ref, grads, scr_ref)
    norm_back_rows(norm_at, dx_ref, x_ref, dqkv_ref, np_ref, w_ref, io.outs[0], gn_ref, io)
    if wired(split):
        dp, ex = split
        rows, wide = piece_rows(split), D // dp
        for n, ref in enumerate((gn_ref,) + tuple(more[:-1])):
            for i in range(2):
                for d in range(dp):
                    row_ref[(2 * n + i) * dp + d : (2 * n + i) * dp + d + 1, :] = ref[i : i + 1, d * wide : (d + 1) * wide]
        first = lax.broadcasted_iota(jnp.int32, (16, WIRE), 0) == 0
        for j in range(ex):
            for k in range(dp):
                at = jnp.bitwise_xor(pos_ref[0], j) * dp + k
                table = jnp.zeros((1, 128), F32) if j else more[-1][0:1, :]
                row = jnp.concatenate(
                    [row_ref[pl.ds(at, 1), :], table, jnp.zeros((1, WIRE - wide - 128), F32)], axis=1
                )
                grads[j % 2][j // 2, k, 4 * rows : 4 * rows + 16, :] = jnp.where(first, row, 0.0).astype(BF)
    if wired(split):
        io.done(1, 4)
        io.done(2, 4)
    else:
        io.done(1)


def last_backward(pos, dx, hidden, saved, params, tok, weights, norm_at, split, more):
    a, qkv, ctx = saved
    grads = wire_outs(split, 5) if wired(split) else [(sds((D, 4 * D), BF), 1)]
    norm, out, *grads = staged(
        functools.partial(last_back_kernel, split, norm_at),
        [(sds((PACK, D), F32), 4)] + grads,
        [(dx, 4), (weights, 1), (tok, 1), (qkv, 1), (a, 1), (ctx, 1), (hidden, 1)], [pos, params, *more],
        [sds((2, D), F32)],
        [pltpu.VMEM((PACK, D), BF), pltpu.VMEM((PACK, 3 * D), BF), pltpu.VMEM((PACK, 2 * D), F32),
         pltpu.VMEM((D, D), BF), pltpu.VMEM((8 * split[0], D // split[0]), F32)],
        flops=14_000_000_000, moved=16 << 20,
        order=[(0, 0), (1, 0), (0, 1), (0, 2), (0, 3), (2, 0), (3, 0), (4, 0), (5, 0), (6, 0)],
    )
    return norm, out, grads


def feed_kernel(io, few, few_out, own):
    (np_ref,) = few
    x_ref, up_ref, down_ref = io.ins
    h_ref, n_ref, act_ref, slope_ref = io.outs
    gain, shift = np_ref[2:3, :], np_ref[3:4, :]
    for r in range(PACK // ROWS):
        rows = slice(r * ROWS, (r + 1) * ROWS)
        io.need((0, r))
        x = x_ref[rows, :]
        unit, _ = unit_rows(x)
        n = (unit * gain + shift).astype(BF)
        n_ref[rows, :] = n
        io.need(1)
        act, slope = gelu_both(mm(n, up_ref[...]))
        act = act.astype(BF)
        act_ref[rows, :] = act
        slope_ref[rows, :] = slope.astype(BF)
        io.need(2)
        h_ref[rows, :] = x + mm(act, down_ref[...])
        for i in range(4):
            io.done(i, r)


def feed_forward(hidden, params, up, down):
    return staged(
        feed_kernel,
        [(sds((PACK, D), F32), 4), (sds((PACK, D), BF), 4), (sds((PACK, FF), BF), 4), (sds((PACK, FF), BF), 4)],
        [(hidden, 4), (up, 1), (down, 1)], [params], flops=4_300_000_000, moved=17 << 20, mib=36,
        order=[(0, 0), (1, 0), (2, 0), (0, 1), (0, 2), (0, 3)],
    )


def feed_back_kernel(split, io, few, few_out, own):
    wire = wired(split)
    pos_ref, np_ref = few
    dx_ref, down_ref, slope_ref, n_ref, act_ref, up_ref, x_ref = io.ins
    out_ref, grads = io.outs[0], io.outs[1:]
    dz_ref, dy_ref, scr_ref, tall_ref = own
    for r in range(PACK // ROWS):
        rows = slice(r * ROWS, (r + 1) * ROWS)
        io.need((0, r), 1, (2, r))
        dy = dx_ref[rows, :].astype(BF)
        dy_ref[rows, :] = dy
        dz_ref[rows, :] = (mm_t(dy, down_ref[...]) * slope_ref[rows, :].astype(F32)).astype(BF)
    io.need(3, 4)
    if wire:
        rows = piece_rows(split)
        for c in range(FF // D):
            scr_ref[...] = t_mm(n_ref[...], dz_ref[:, c * D : (c + 1) * D]).astype(BF)
            send_rows(split, pos_ref, scr_ref, *grads, c * rows, rows)
            io.done(1, c)
            io.done(2, c)
        for c in range(FF // D):
            tall_ref[c * D : (c + 1) * D, :] = t_mm(act_ref[:, c * D : (c + 1) * D], dy_ref[...]).astype(BF)
        send_rows(split, pos_ref, tall_ref, *grads, FF // D * rows, FF // D * rows)
        for c in range(FF // D):
            io.done(1, FF // D + c)
            io.done(2, FF // D + c)
    else:
        grads[0][...] = t_mm(n_ref[...], dz_ref[...]).astype(BF)
        grads[1][...] = t_mm(act_ref[...], dy_ref[...]).astype(BF)
        io.done(1)
        io.done(2)
    io.need(5, 6)
    norm_back_rows(2, dx_ref, x_ref, dz_ref, np_ref, up_ref, out_ref, few_out[0], io)


def feed_backward(pos, dx, hidden, saved, params, up, down, split):
    n, act, slope = saved
    grads = wire_outs(split, 8) if wired(split) else [(sds((D, FF), BF), 1), (sds((FF, D), BF), 1)]
    norm, out, *grads = staged(
        functools.partial(feed_back_kernel, split),
        [(sds((PACK, D), F32), 4)] + grads,
        [(dx, 4), (down, 1), (slope, 4), (n, 1), (act, 1), (up, 1), (hidden, 1)], [pos, params], [sds((2, D), F32)],
        scratch=[pltpu.VMEM((PACK, FF), BF), pltpu.VMEM((PACK, D), BF), pltpu.VMEM((D, D), BF), pltpu.VMEM((FF, D), BF)],
        order=[(0, 0), (1, 0), (2, 0)] + [(i, r) for r in range(1, 4) for i in (0, 2)] + [(n, 0) for n in range(3, 7)],
        flops=8_600_000_000, moved=24 << 20,
    )
    return norm, out, grads


def norm_back_rows(norm_at, dx_ref, x_ref, grad_ref, np_ref, w_ref, out_ref, gn_ref, io, needs=()):
    gain = np_ref[norm_at : norm_at + 1, :]
    dgain, dshift = jnp.zeros((1, D), F32), jnp.zeros((1, D), F32)
    for r in range(PACK // ROWS):
        rows = slice(r * ROWS, (r + 1) * ROWS)
        for i in needs:
            io.need((i, r))
        dnorm = mm_t(grad_ref[rows, :], w_ref[:, : grad_ref.shape[1]])
        unit, scale = unit_rows(x_ref[rows, :].astype(F32))
        dgain += jnp.sum(dnorm * unit, axis=0, keepdims=True)
        dshift += jnp.sum(dnorm, axis=0, keepdims=True)
        out_ref[rows, :] = dx_ref[rows, :] + unit_back(unit, scale, gain, dnorm)
        io.done(0, r)
    gn_ref[0:1, :] = dgain
    gn_ref[1:2, :] = dshift


def assemble_kernel(split, blocks, tall, *refs):
    dp, ex = split
    rows = piece_rows(split)
    pos_ref, pieces, outs = refs[0], refs[1 : 1 + ex], refs[1 + ex :]
    for j in range(ex):
        for k in range(dp):
            at = lax.rem(pos_ref[1] + dp - k, dp) * ex + jnp.bitwise_xor(pos_ref[0], j)
            start = pl.multiple_of(at * rows, rows)
            for c in range(blocks):
                outs[0][pl.ds(start, rows), c * WIRE : (c + 1) * WIRE] = pieces[j][k, c * rows : (c + 1) * rows, :]
            if tall:
                high = blocks * rows
                start = pl.multiple_of(at * high, high)
                outs[1][pl.ds(start, high), :] = pieces[j][k, high : 2 * high, :]


def assemble(split, pos, pieces, tall):
    outs = [sds((D, 4 * D), BF)] + ([sds((FF, D), BF)] if tall else [])
    return call(
        functools.partial(assemble_kernel, split, 4, tall), outs, pos, *pieces,
        pos=True, flops=1_000_000, moved=4 << 20, mib=24,
    )


def assemble_norm_kernel(split, *refs):
    dp, ex = split
    rows = piece_rows(split)
    pos_ref, pieces, (w_ref, np_ref, scr_ref) = refs[0], refs[1 : 1 + ex], refs[1 + ex :]
    for j in range(ex):
        for k in range(dp):
            at = lax.rem(pos_ref[1] + dp - k, dp) * ex + jnp.bitwise_xor(pos_ref[0], j)
            start = pl.multiple_of(at * rows, rows)
            for c in range(4):
                w_ref[pl.ds(start, rows), c * WIRE : (c + 1) * WIRE] = pieces[j][k, c * rows : (c + 1) * rows, :]
            scr_ref[pl.ds(start, rows), :] = pieces[j][k, 4 * rows : 5 * rows, 0:128].astype(F32)
    np_ref[...] = jnp.transpose(scr_ref[...])[:8]


def add_core_kernel(near, io, few, few_out, own):
    mine_ref, got_ref = io.ins
    for j in range(mine_ref.shape[0]):
        io.need((0, j), (1, j))
        total = (mine_ref[j].astype(F32) + got_ref[j].astype(F32)).astype(BF)
        if near:
            io.outs[j][...] = total
            io.done(j)
        else:
            io.outs[0][jnp.bitwise_xor(few[0][0] // 2, j)] = total
    if not near:
        io.done(0)


def add_near_kernel(lists, pos_ref, *refs):
    ins, outs = refs[: sum(lists)], refs[sum(lists) :]
    dp = len(outs)
    for k, out in enumerate(outs):
        at = lax.rem(pos_ref[1] + k, dp)
        first, top = 0, 0
        for n in lists:
            parts = ins[first : first + n]
            first += n
            parts = [parts[0].at[i] for i in range(parts[0].shape[0])] if n == 1 else parts
            total = parts[0][at].astype(F32)
            for part in parts[1:]:
                total = total + part[at].astype(F32)
            out[top : top + total.shape[0], :] = total.astype(BF)
            top += total.shape[0]


def add_turn_kernel(*refs):
    total = refs[0][...].astype(F32)
    for ref in refs[1:-1]:
        total = total + ref[...].astype(F32)
    refs[-1][...] = total.astype(BF)


def spread_kernel(split, *refs):
    dp, ex = split
    rows = piece_rows(split)
    pos_ref, last_ref, early_ref, qkv_ref, attn_ref, up_ref, down_ref, gn_ref, table_ref = refs

    def put(n, start, piece):
        for c in range(3):
            qkv_ref[pl.ds(start, rows), n, c * D : (c + 1) * D] = piece[c * rows : (c + 1) * rows]
        attn_ref[pl.ds(start, rows), n, :] = piece[3 * rows : 4 * rows]

    for j in range(ex):
        start, high = j * rows, j * 4 * rows
        piece = early_ref[j].astype(F32)
        for c in range(4):
            up_ref[pl.ds(start, rows), c * D : (c + 1) * D] = piece[c * rows : (c + 1) * rows]
        down_ref[pl.ds(high, 4 * rows), :] = piece[4 * rows : 8 * rows]
        put(1, start, piece[8 * rows :])
        piece = last_ref[j].astype(F32)
        put(0, j * rows, piece)
        gn_ref[j : j + 1, :] = piece[4 * rows : 4 * rows + 1, 0 : D // dp]
        table_ref[j : j + 1, :] = piece[4 * rows : 4 * rows + 1, D // dp : D // dp + 128]


def gather_near_kernel(at, io, few, few_out, own):
    (pair_ref,) = few
    size = io.outs[0].shape[0] // len(io.ins)
    tokens = lax.broadcasted_iota(jnp.int32, (size, PACK), 1).astype(F32)
    lane = lax.broadcasted_iota(jnp.int32, (size, 8), 1)
    for n, source in enumerate(io.ins):
        one = 8 * (at + n)
        base, length, first, gate, task = [pair_ref[one + i : one + i + 1, :] for i in range(5)]
        s = lax.broadcasted_iota(jnp.int32, (size, 128), 0).astype(F32) + float((at + n) * size)
        held = (base >= 0) & (s >= base) & (s < base + length)

        def take(value, held=held):
            return jnp.sum(jnp.where(held, value, 0.0), axis=1, keepdims=True)

        gate, task = take(gate), take(task + 1.0) - 1.0
        hot = jnp.where(take(first - base + s + 1.0) - 1.0 == tokens, 1.0, 0.0).astype(BF)
        io.need(n)
        rows = slice(n * size, (n + 1) * size)
        io.outs[0][rows, :] = (mm(hot, source[...]) * gate).astype(BF)
        io.outs[1][rows, :] = jnp.where(lane == 0, gate, jnp.where(lane == 1, task, 0.0))
        io.done(0, n)
        io.done(1, n)


def gather_near(pairs, sources, size, at):
    count = len(sources)
    return staged(
        functools.partial(gather_near_kernel, at),
        [(sds((count * size, D), BF), count), (sds((count * size, 8), F32), count)], [(x, 1) for x in sources], [pairs],
        flops=2 * count * size * PACK * D, moved=4 << 20, mib=20,
    )


def slots_hot(tok_ref, size, n):
    at = lax.broadcasted_iota(jnp.int32, (PACK, size), 1).astype(F32) + float(n * size)
    return jnp.where((tok_ref[:, 2:3] == at) | (tok_ref[:, 3:4] == at), 1.0, 0.0).astype(BF)


def whole(shape):
    return pl.BlockSpec(shape, lambda e: (0,) * len(shape))


def combine_out_kernel(experts, io, few, few_out, own):
    pos_ref = few[0]
    tok_ref, slot_ref, rows_ref, h_ref = io.ins
    acc_ref, size = own[0], rows_ref.shape[0] // experts
    io.need(0, 1, 2)
    for e in range(experts):
        start = pl.multiple_of(jnp.bitwise_xor(pos_ref[0], e) * size, size)
        rows = rows_ref[pl.ds(start, size), :].astype(F32)
        part = mm(slots_hot(tok_ref, size, e), (rows * slot_ref[e * size : (e + 1) * size, 1:2]).astype(BF))
        acc_ref[...] = part if e == 0 else acc_ref[...] + part
    for r in range(PACK // ROWS):
        rows = slice(r * ROWS, (r + 1) * ROWS)
        io.need((3, r))
        io.outs[0][rows, :] = (h_ref[rows, :] + acc_ref[rows, :]).astype(BF)
        io.done(0, r)


def combine_out(pos, tok, slot, rows, hidden, experts):
    return staged(
        functools.partial(combine_out_kernel, experts), [(sds((PACK, D), BF), 4)],
        [(tok, 1), (slot, 1), (rows, 1), (hidden, 4)], [pos], scratch=[pltpu.VMEM((PACK, D), F32)],
        flops=2 * 4096 * PACK * D, moved=14 << 20,
    )[0]


def expert_kernel(count, steps, *refs):
    bufs = refs[1 : 1 + count]
    dout_in, slot_ref, up_ref, down_ref = refs[1 + count : 5 + count]
    dbufs = refs[-count // 2 - 6 : -6]
    table_ref, out_ref, act_ref, du_ref, buf_ref, dout_ref = refs[-6:]
    i = pl.program_id(0)

    @pl.when(i == 0)
    def _():
        table_ref[...] = jnp.zeros_like(table_ref)

    def work(n):
        buf, dout = bufs[n][...], dout_in[...]
        buf_ref[...] = buf
        dout_ref[...] = dout
        z, dact = mm(buf, up_ref[...]), mm_t(dout, down_ref[...])
        act, slope = gelu_both(z)
        act = act.astype(BF)
        act_ref[...] = act
        out = mm(act, down_ref[...]).astype(BF)
        du = (dact * slope).astype(BF)
        du_ref[...] = du
        dbufs[n // 2][...] = mm_t(du, up_ref[...]).astype(BF)
        out_ref[...] = out
        gate, task = slot_ref[:, 0:1], slot_ref[:, 1:2]
        dgate = jnp.sum(out.astype(F32) * dout.astype(F32), axis=1, keepdims=True)
        dgate = jnp.where(task >= 0, dgate / jnp.where(task >= 0, gate, 1.0), 0.0)
        tasks = lax.broadcasted_iota(jnp.int32, (buf.shape[0], 128), 1).astype(F32)
        table_ref[0:1, :] += jnp.sum(jnp.where(tasks == task, dgate, 0.0), axis=0, keepdims=True)

    for n in range(count):
        pl.when(i // steps == n)(functools.partial(work, n))


def expert_rows(pos, bufs, dout, slot, up, down, total, at, held):
    rows = bufs[0].shape[0] // 2
    count = len(bufs)
    size = min(256, rows)
    steps = rows // size
    blocks = [
        pl.BlockSpec((size, D), lambda i, p, n=n: (jnp.clip(i - n * steps, 0, steps - 1) + n % 2 * steps, 0))
        for n in range(count)
    ]
    pairs = [
        pl.BlockSpec((size, D), lambda i, p, n=n: (jnp.clip(i - 2 * n * steps, 0, 2 * steps - 1), 0))
        for n in range(count // 2)
    ]

    def there(i, p):
        return (jnp.bitwise_xor(p[0], at + i // steps) * steps + lax.rem(i, steps), 0)

    def fixed(shape):
        return pl.BlockSpec(shape, lambda i, p: (0, 0), pipeline_mode=pl.Buffered(1))

    first = at * steps

    def tile(cols, first=first):
        return pl.BlockSpec((size, cols), lambda i, p: (i + first, 0))

    alias = {count + 5 + n: count // 2 + 1 + n for n in range(5)} if held else None
    outs = call(
        functools.partial(expert_kernel, count, steps),
        [sds((2 * rows, D), BF)] * (count // 2) + [sds((8, 128), F32)]
        + [sds((total, cols), BF) for cols in (D, FF, FF, D, D)],
        pos, *bufs, dout, slot, up, down, *held,
        grid=(count * steps,), pos=True,
        in_specs=blocks + [tile(D, 0), tile(8, 0), fixed((D, FF)), fixed((FF, D))]
        + [pl.BlockSpec(memory_space=pl.ANY)] * len(held),
        out_specs=pairs + [pl.BlockSpec((8, 128), lambda i, p: (0, 0)), pl.BlockSpec((size, D), there)]
        + [tile(FF), tile(FF), tile(D), tile(D)],
        alias=alias,
        flops=8 * rows * count * D * FF, moved=count * rows * 13 << 10,
    )
    return outs[: count // 2], outs[count // 2], outs[count // 2 + 1 :]


def expert_grad_kernel(steps, act_ref, du_ref, buf_ref, dout_ref, gup_ref, gdown_ref, up_acc, down_acc):
    i = pl.program_id(0)

    @pl.when(i == 0)
    def _():
        up_acc[...] = jnp.zeros_like(up_acc)
        down_acc[...] = jnp.zeros_like(down_acc)

    up_acc[...] += t_mm(buf_ref[...], du_ref[...])
    down_acc[...] += t_mm(act_ref[...], dout_ref[...])

    @pl.when(i == steps - 1)
    def _():
        gup_ref[...] = up_acc[...].astype(BF)
        gdown_ref[...] = down_acc[...].astype(BF)


def expert_grads(act, du, buf, dout):
    rows = buf.shape[0]
    size = 1024
    tile = lambda cols: pl.BlockSpec((size, cols), lambda i: (i, 0))
    return call(
        functools.partial(expert_grad_kernel, rows // size),
        [sds((D, FF), BF), sds((FF, D), BF)], act, du, buf, dout,
        grid=(rows // size,),
        in_specs=[tile(FF), tile(FF), tile(D), tile(D)],
        out_specs=[whole((D, FF)), whole((FF, D))],
        scratch=[pltpu.VMEM((D, FF), F32), pltpu.VMEM((FF, D), F32)],
        flops=4 * rows * D * FF, moved=44 << 20, mib=62,
    )


def route(lengths, task_ids, task_experts, capacity, task_logits, cap_slots, rel):
    sentences = lengths.shape[1]
    experts = capacity.shape[0]
    tasks = task_experts.shape[0]
    lens, ids = lengths.reshape(-1), task_ids.reshape(-1)
    ends = jnp.cumsum(lens)
    starts = ends - lens
    table = jnp.take_along_axis(task_logits, task_experts, axis=1)
    gates = jax.nn.softmax(table, axis=-1)
    hot = ids[:, None] == lax.broadcasted_iota(jnp.int32, (1, tasks), 1)
    expert = jnp.sum(jnp.where(hot[:, :, None], task_experts[None], 0), axis=1)
    gate = jnp.sum(jnp.where(hot[:, :, None], gates[None], 0.0), axis=1)
    pair_expert = expert.reshape(-1)
    pair_len = jnp.repeat(lens, 2)
    expert_hot = (pair_expert[:, None] == lax.broadcasted_iota(jnp.int32, (1, experts), 1)).astype(jnp.int32)
    running = jnp.cumsum(expert_hot * pair_len[:, None], axis=0)
    filled = jnp.sum(running * expert_hot, axis=1)
    limits = jnp.sum(expert_hot * capacity[None, :], axis=1)
    base = jnp.where(filled <= limits, jnp.bitwise_xor(pair_expert, rel) * cap_slots + filled - pair_len, -1)
    base_two = base.reshape(sentences, 2)

    def lanes(rows):
        rows = jnp.stack([row.astype(F32) for row in rows])
        return jnp.pad(rows, ((0, 8 - rows.shape[0]), (0, 128 - rows.shape[1])))

    sent = lanes([starts, ends, base_two[:, 0], base_two[:, 1]])
    pair = lanes([base, pair_len, jnp.repeat(starts, 2), gate.reshape(-1), jnp.repeat(ids, 2)])
    slots = experts * cap_slots
    tok, slot = call(
        functools.partial(route_kernel, slots),
        [sds((PACK, 8), F32), sds((slots, 8), F32)], sent, pair,
        flops=1_000_000, moved=3 << 20, mib=24,
    )
    return tok, slot, pair, gates


EXPERT = ("xy", "core")
BOTH = ("dp", "xy", "core")


def flip(rows, j, ex):
    return lax.ppermute(rows, EXPERT, [(i, i ^ j) for i in range(ex)])


def turn(rows, k, dp):
    return lax.ppermute(rows, "dp", [(i, (i + k) % dp) for i in range(dp)])


def tie(value, *after):
    return lax.optimization_barrier((value,) + after)[0]


def send_even(here, ex):
    return [here] + [flip(here, j, ex) for j in range(2, ex, 2)]


def send_core(even, ex):
    got = []
    for one in even:
        got += [one, flip(one, 1, ex)]
    return got


def add_core(pos, own, got, near=False):
    parts = own.shape[0]
    outs = [(sds(own.shape[1:], BF), 1)] * parts if near else [(sds(own.shape, BF), parts)]
    got = staged(
        functools.partial(add_core_kernel, near), outs, [(own, parts), (got, parts)], [pos],
        order=[(i, j) for j in range(parts) for i in range(2)], flops=1_000_000, moved=own.size * 6,
    )
    return got if near else got[0]


def add_near(pos, *lists):
    lists = [one if isinstance(one, list) else [one] for one in lists]
    rows = sum(one[0].shape[-2] for one in lists)
    dp = lists[0][0].shape[-3]
    return call(
        functools.partial(add_near_kernel, [len(one) for one in lists]), [sds((rows, WIRE), BF)] * dp,
        pos, *sum(lists, []), pos=True, flops=1_000_000, moved=rows << 14,
    )


def send_near(sums, ex):
    return [sums[0]] + [flip(sums[j], 2 * j, ex) for j in range(1, ex // 2)]


def send_turn(sums, dp):
    return [sums[0]] + [turn(sums[k], k, dp) for k in range(1, dp)]


def add_turn(got):
    return call(add_turn_kernel, sds(got[0].shape, BF), *got, flops=1_000_000, moved=got[0].size * 10, mib=62)


def swap(parts, axis):
    return lax.all_to_all(parts, axis, split_axis=0, concat_axis=0, tiled=True)


def local(n_dp, n_ex, hidden_in, lengths, task_ids, task_experts, capacity, task_logits, norm_params,
          w_qkv, w_attn, w_up, w_down, expert_up, expert_down, cotangent):
    experts = capacity.shape[0]
    cap_slots = max(4 * hidden_in.shape[0] // experts, 2 * MOST_LEN)
    slots = experts * cap_slots
    me, here = lax.axis_index(EXPERT), lax.axis_index("dp")
    pos = jnp.stack([me, here]).astype(jnp.int32)
    split = (n_dp, n_ex)
    wire = wired(split)

    def mine(shard):
        rows = shard.shape[0] // n_ex
        return lax.dynamic_slice_in_dim(shard, me * rows, rows, 0)

    def exchange(pair, j):
        return flip(pair, j, n_ex) if j else pair

    tok, slot, pair, gates = route(lengths, task_ids, task_experts, capacity, task_logits, cap_slots, me)
    if wire:
        rows = piece_rows(split)

        def blocks(wide):
            return [wide[:, c * WIRE : (c + 1) * WIRE] for c in range(wide.shape[1] // WIRE)]

        norms = jnp.pad(mine(norm_params), ((0, 0), (0, WIRE - 8)))
        qkv, attn = mine(w_qkv), mine(w_attn)
        piece = blocks(qkv[:, 0]) + [attn[:, 0], norms] + blocks(mine(w_up)) + [mine(w_down)]
        piece = jnp.concatenate(piece + blocks(qkv[:, 1]) + [attn[:, 1]])
        parts = [piece] + [turn(piece, k, n_dp) for k in range(1, n_dp)]
        expert_up, expert_down = tie(expert_up, *parts[1:]), tie(expert_down, *parts[1:])
        zero, feed, one = [
            jnp.stack([part[lo * rows : hi * rows] for part in parts]) for lo, hi in ((0, 5), (5, 13), (13, 17))
        ]
        cots = [cotangent, flip(cotangent, 2, n_ex), flip(cotangent, 4, n_ex)]
        zero = send_even(tie(zero, *cots[1:]), n_ex)
        pairs = pair
        j = 1
        while j < n_ex:
            pairs = jnp.concatenate([pairs, flip(pairs, j, n_ex)])
            j *= 2
        feed = send_even(tie(feed, *zero[1:]), n_ex)
        zero = send_core([tie(part, tok, pairs) for part in zero], n_ex)
        groups = [(0, 2), (2, 6), (6, 8)]

        def gather_group(lo, hi, pairs):
            sources = sum([[cots[j], flip(cots[j], 1, n_ex)] for j in range(lo // 2, hi // 2)], [])
            return gather_near(pairs, sources, cap_slots, lo)

        near = [gather_group(*group, pairs) for group in groups[:2]]
        attn_zero, params = call(
            functools.partial(assemble_norm_kernel, split), [sds((D, 4 * D), BF), sds((8, D), F32)], pos, *zero,
            scratch=[pltpu.VMEM((D, 128), F32)], pos=True, flops=1_000_000, moved=4 << 20, mib=24,
        )
        fwd = tie(hidden_in, *sum(near, []))
        h1, *saved_zero = attention_forward(fwd, params, tok, attn_zero, 0)
        one = send_even(tie(one, h1, *feed[1:]), n_ex)
        feed = send_core([tie(part, h1) for part in feed], n_ex)
        up, down = assemble(split, pos, feed, True)
        h2, *saved_feed = feed_forward(h1, params, up, down)
        one = [tie(part, h2) for part in one]
        cots.append(flip(tie(cotangent, *one[1:]), 6, n_ex))
        one = send_core(one, n_ex)
        attn_one = assemble(split, pos, one, False)[0]
    else:

        def gather_all(shard):
            return lax.all_gather(mine(shard), BOTH, axis=0, tiled=True)

        params = lax.all_gather(norm_params, "dp", axis=0, tiled=True).astype(F32).T
        attn_zero = gather_all(jnp.concatenate([w_qkv[:, 0], w_attn[:, 0]], axis=1))
        up, down = gather_all(w_up), gather_all(w_down)
        attn_one = gather_all(jnp.concatenate([w_qkv[:, 1], w_attn[:, 1]], axis=1))
        h1, *saved_zero = attention_forward(hidden_in, params, tok, attn_zero, 0)
        h2, *saved_feed = feed_forward(h1, params, up, down)
        pairs = pair
        j = 1
        while j < n_ex:
            pairs = jnp.concatenate([pairs, flip(pairs, j, n_ex)])
            j *= 2
        groups = [(j, j + 4) for j in range(0, n_ex, 4)]
        cots = [cotangent] + [flip(cotangent, j, n_ex) for j in range(1, n_ex)]
        near = [gather_near(pairs, cots[lo:hi], cap_slots, lo) for lo, hi in groups]
    up_expert = lax.all_gather(expert_up[0], "dp", axis=0, tiled=True)
    down_expert = lax.all_gather(expert_down[0], "dp", axis=0, tiled=True)
    h3, *saved_one = attention_forward(h2, params, tok, attn_one, 4, slot, experts)
    saved_one, sent = saved_one[:3], saved_one[3:]
    sums, held, table = [], (), 0.0
    if wire:
        sent = [tie(pair, cots[-1]) for pair in sent]
    bufs = {j: exchange(sent[j // 2], j) for j in range(0, groups[-1][0], 2)}
    for n, (lo, hi) in enumerate(groups):
        if wire and n == 1:
            near.append(gather_group(*groups[2], tie(pairs, sums[0])))
        dout, slot_near = near[n]
        if n == 1:
            for j in range(groups[-1][0], n_ex, 2):
                bufs[j] = exchange(tie(sent[j // 2], *[bufs[i] for i in range(lo, hi, 2)], *sums[:1]), j)
        for j in range(lo, hi, 2):
            bufs[j + 1] = flip(tie(bufs[j], *sums[-1:], *near[-1]), 1, n_ex)
        back, part, held = expert_rows(
            pos, [bufs[j] for j in range(lo, hi)], dout, slot_near, up_expert, down_expert, slots, lo, held
        )
        sums += back
        table = table + part
    out, *held = held
    back = [exchange(pair, 2 * j) for j, pair in enumerate(sums)]
    gup_expert, gdown_expert = expert_grads(*held)
    far = [flip(tie(pair, gup_expert), 1, n_ex) for pair in back]
    dbuf_home = sum([list(both) for both in zip(back, far)], [])
    out_home = swap(tie(out, *back, gup_expert).reshape(experts, cap_slots, D), EXPERT).reshape(-1, D)
    gn_one, gn_moe, dx, g_one = first_backward(
        pos, dbuf_home, h3, cotangent, h2, saved_one, params, tok, attn_one, 4, split
    )
    expert_up_sum = lax.psum_scatter(tie(gup_expert, gn_moe), "dp", scatter_dimension=0, tiled=True)
    expert_down_sum = lax.psum_scatter(tie(gdown_expert, gn_moe), "dp", scatter_dimension=0, tiled=True)
    if wire:
        got_one = add_core(pos, g_one[0], flip(g_one[1], 1, n_ex), True)
        dx = tie(dx, got_one[0])
        got_one = send_near(got_one, n_ex)
    gn_feed, dx, g_feed = feed_backward(pos, dx, h1, saved_feed, params, up, down, split)
    if wire:
        got_feed = flip(tie(g_feed[1], out_home, *got_one[1:]), 1, n_ex)
        sum_feed = add_core(pos, g_feed[0], got_feed)
        dx = tie(dx, sum_feed)
        got_feed = swap(sum_feed, "xy")
    gn_zero, grad_in, g_zero = last_backward(
        pos, dx, hidden_in, saved_zero, params, tok, attn_zero, 0, split, (gn_feed, gn_one, gn_moe, table)
    )
    if wire:
        sum_zero = add_core(pos, g_zero[0], flip(g_zero[1], 1, n_ex))
        early = add_near(pos, tie(got_feed, sum_zero), got_one)
        h3 = tie(h3, sum_zero)
        sum_zero = swap(sum_zero, "xy")
        early = send_turn(early, n_dp)
    hidden_out = combine_out(pos, tok, slot, out_home, h3, experts)
    if wire:
        sum_zero = add_near(pos, tie(sum_zero, hidden_out))
        early = lax.all_gather(add_turn([tie(one, sum_zero[0]) for one in early]), EXPERT, axis=0)
        expert_up_sum, expert_down_sum = tie(expert_up_sum, sum_zero[0]), tie(expert_down_sum, sum_zero[0])
        expert_up_sum, expert_down_sum = expert_up_sum.astype(F32), expert_down_sum.astype(F32)
        sum_zero = send_turn(sum_zero, n_dp)
        sum_zero = add_turn([tie(part, expert_up_sum, expert_down_sum) for part in sum_zero])
        last = lax.all_gather(sum_zero, EXPERT, axis=0)
        rows = D // n_dp
        grad_qkv, grad_attn, grad_up, grad_down, gn, sums = call(
            functools.partial(spread_kernel, split),
            [sds((rows, 2, 3 * D), F32), sds((rows, 2, D), F32), sds((rows, FF), F32), sds((FF // n_dp, D), F32),
             sds((8, rows), F32), sds((experts, 128), F32)],
            pos, last, early,
            pos=True, flops=1_000_000, moved=7 << 20, mib=32,
        )
        gn = gn.T
    else:
        small = jnp.concatenate([gn_zero, gn_feed, gn_one, gn_moe], axis=0)
        table = lax.dynamic_update_slice_in_dim(jnp.zeros((experts, 128), F32), table[:1], me, 0)
        small = jnp.concatenate([small, jnp.pad(table, ((0, 0), (0, D - 128)))], axis=0)
        small = lax.psum(small, BOTH)
        gn = lax.dynamic_slice_in_dim(small[:8], here * (D // n_dp), D // n_dp, 1).T
        sums = small[8:]

        def reduce_all(grad):
            rows = grad.shape[0] // (n_dp * n_ex)
            grad = grad.reshape(n_dp, n_ex, rows, -1).transpose(1, 0, 2, 3).reshape(grad.shape)
            part = lax.psum_scatter(grad, EXPERT, scatter_dimension=0, tiled=True)
            part = lax.psum_scatter(part, "dp", scatter_dimension=0, tiled=True)
            return lax.all_gather(part, EXPERT, axis=0, tiled=True).astype(F32)

        g_one, grad_up, grad_down, g_zero = [reduce_all(g) for g in (*g_one, *g_feed, *g_zero)]
        grad_qkv = jnp.stack([g_zero[:, : 3 * D], g_one[:, : 3 * D]], axis=1)
        grad_attn = jnp.stack([g_zero[:, 3 * D :], g_one[:, 3 * D :]], axis=1)
    sums = sums[:, : task_logits.shape[0]].T
    hot = task_experts[:, :, None] == lax.broadcasted_iota(jnp.int32, (1, 1, experts), 2)
    pair_sum = jnp.sum(jnp.where(hot, sums[:, None, :], 0.0), axis=2)
    lean = gates[:, 0] * gates[:, 1] * (pair_sum[:, 0] - pair_sum[:, 1])
    grad_logits = jnp.where(hot[:, 0], lean[:, None], 0.0) - jnp.where(hot[:, 1], lean[:, None], 0.0)
    return (
        hidden_out, grad_in, grad_logits, gn, grad_qkv, grad_attn, grad_up, grad_down,
        expert_up_sum.astype(F32)[None], expert_down_sum.astype(F32)[None],
    )


def solution(mesh):
    n_dp, n_ex = mesh.shape["dp"], mesh.shape["expert"]
    mesh = jax.sharding.Mesh(mesh.devices.reshape(n_dp, n_ex // 2, 2), BOTH)
    token = P(BOTH, None)
    expert = P(EXPERT, "dp", None)
    in_specs = (
        token, token, token, P(), P(), P(), P("dp", None), P("dp", None, None), P("dp", None, None),
        P("dp", None), P("dp", None), expert, expert, token,
    )
    out_specs = (
        token, token, P(), P("dp", None), P("dp", None, None), P("dp", None, None), P("dp", None), P("dp", None),
        expert, expert,
    )
    step = functools.partial(local, n_dp, n_ex)
    return jax.shard_map(step, mesh=mesh, in_specs=in_specs, out_specs=out_specs, check_vma=False)
```
